32 devices in a mesh: dp: 2 (over y), ctx: 16 (over z, x, core).
Axes of the slice: x: 2, y: 2, z: 4, core: 2. Of those that a mesh axis runs over, the one named last changes fastest.
Arguments:
- hidden_in: bfloat16 [4, 1024, 1024], P('dp', 'ctx'), may hold values from -6 to 6
- out_cotangent: bfloat16 [4, 1024, 1024], P('dp', 'ctx'), may hold values from -6 to 6
- attn_gain: bfloat16 [1024], P(('dp', 'ctx')), may hold values from 0.5 to 1.5
- attn_shift: bfloat16 [1024], P(('dp', 'ctx')), may hold values from -3 to 3
- qkv_weight: bfloat16 [1024, 3072], P(('dp', 'ctx')), may hold values from -1 to 1
- qkv_bias: bfloat16 [3072], P(('dp', 'ctx')), may hold values from -2 to 2
- proj_weight: bfloat16 [1024, 1024], P(('dp', 'ctx')), may hold values from -1.5 to 1.5
- proj_bias: bfloat16 [1024], P(('dp', 'ctx')), may hold values from -2 to 2
- mlp_gain: bfloat16 [1024], P(('dp', 'ctx')), may hold values from 0.5 to 1.5
- mlp_shift: bfloat16 [1024], P(('dp', 'ctx')), may hold values from -3 to 3
- up_weight: bfloat16 [1024, 4096], P(('dp', 'ctx')), may hold values from -0.1875 to 0.1875
- up_bias: bfloat16 [4096], P(('dp', 'ctx')), may hold values from -3 to 3
- down_weight: bfloat16 [4096, 1024], P(('dp', 'ctx')), may hold values from -0.09375 to 0.09375
- down_bias: bfloat16 [1024], P(('dp', 'ctx')), may hold values from -2 to 2
- picture_starts: int32 [4, 4], P('dp'), may hold values from 0 to 768, as said below
- group_order: int32 [16], replicated, may hold values from 0 to 15, each once
Outputs:
- block_out: bfloat16 [4, 1024, 1024], P('dp', 'ctx')
- grad_hidden: bfloat16 [4, 1024, 1024], P('dp', 'ctx')
- grad_attn_gain: float32 [1024], P(('dp', 'ctx'))
- grad_attn_shift: float32 [1024], P(('dp', 'ctx'))
- grad_qkv_weight: float32 [1024, 3072], P(('dp', 'ctx'))
- grad_qkv_bias: float32 [3072], P(('dp', 'ctx'))
- grad_proj_weight: float32 [1024, 1024], P(('dp', 'ctx'))
- grad_proj_bias: float32 [1024], P(('dp', 'ctx'))
- grad_mlp_gain: float32 [1024], P(('dp', 'ctx'))
- grad_mlp_shift: float32 [1024], P(('dp', 'ctx'))
- grad_up_weight: float32 [1024, 4096], P(('dp', 'ctx'))
- grad_up_bias: float32 [4096], P(('dp', 'ctx'))
- grad_down_weight: float32 [4096, 1024], P(('dp', 'ctx'))
- grad_down_bias: float32 [1024], P(('dp', 'ctx'))
- clipped_qkv: float32 [1024, 3072], P(('dp', 'ctx'))
The draws below stay inside these ranges and needn't reach their ends.
Inputs may be any that keep to these rules, and one draw needn't show every extreme that they name: `picture_starts`: piece r of a sequence starts between r * 256 and (r + 1) * 256 - 256, so pieces never intersect.
All inputs are finite; a program needn't handle non-finite values.
Results may differ from the reference program's by a relative error of at most 0.012.
The reference program's roundings to bfloat16 on the way count: a program that leaves them out, or rounds other values in their place, can miss the bound.
Values may be sent and summed in bfloat16 or wider, within the bound.
A program may use at most 256 MiB of HBM per device.

```python
import math
import jax
import jax.numpy as jnp
from jax import lax

D = 1024
H = 16
HD = 64
ROT = 16
FF = 4096
GROUP = 64
PIC = 256
PICS = 4
SEQS = 4
LENGTH = 1024
N_CTX = 16


def draw_qkv_weight(key, part):
    key = jax.random.fold_in(key, 17)
    base_key, head_key = jax.random.split(key)
    base = jnp.clip(jax.random.normal(base_key, (D, 3 * D), jnp.float32), -6.0, 6.0)
    head_scale = jnp.exp(jax.random.uniform(head_key, (3, H), jnp.float32, jnp.log(0.8), jnp.log(1.6)))
    head_scale = jnp.where(jnp.arange(3)[:, None] == 2, 1.0, head_scale)
    columns = jnp.repeat(head_scale.reshape(3 * H), HD)
    return (base * D ** (-0.5) * columns[None, :]).astype(jnp.bfloat16)


def draw_picture_starts(key, part):
    key = jax.random.fold_in(key, 29)
    offset_key, lead_key, tail_key = jax.random.split(key, 3)
    region = LENGTH // PICS
    offsets = jax.random.randint(offset_key, (SEQS, PICS), 0, region - PIC + 1)
    lead_seq = jax.random.randint(lead_key, (), 0, SEQS)
    tail_seq = jax.random.randint(tail_key, (), 0, SEQS)
    seq_rows = jnp.arange(SEQS)[:, None]
    slot_cols = jnp.arange(PICS)[None, :]
    offsets = jnp.where((seq_rows == lead_seq) & (slot_cols == 0), 0, offsets)
    offsets = jnp.where((seq_rows == tail_seq) & (slot_cols == PICS - 1), region - PIC, offsets)
    return (slot_cols * region + offsets).astype(jnp.int32)


def shard_levels(stream_key, dims, cuts, low, top_value):
    def one(dim, parts):
        draws = jax.random.uniform(jax.random.fold_in(jax.random.fold_in(stream_key, 6), dim), (parts,), jnp.float32, low / len(cuts), top_value / len(cuts))
        return jnp.repeat(jnp.exp(draws), dims[dim] // parts).reshape((-1,) + (1,) * (len(dims) - dim - 1))

    factor_of = one(*cuts[0])
    for cut in cuts[1:]:
        factor_of = factor_of * one(*cut)
    return factor_of


def bell_draw(rng, dims, deviation, limit, pieces=(), kind=jnp.bfloat16):
    entries = deviation * jax.random.normal(rng, dims, jnp.float32)
    if pieces:
        entries = entries * shard_levels(rng, dims, pieces, -0.22, 0.18)
    return jnp.clip(entries, -limit, limit).astype(kind)


def setup_inputs(seed: int = 0) -> dict:
    streams_of = jax.random.split(jax.random.key(seed), 17)
    return {
        "hidden_in": bell_draw(streams_of[0], (SEQS, LENGTH, D), 1.0, 6.0, ((0, 2), (1, 16))),
        "out_cotangent": bell_draw(streams_of[1], (SEQS, LENGTH, D), 1.0, 6.0, ((0, 2), (1, 16))),
        "attn_gain": jnp.clip(1.0 + 0.1 * jax.random.normal(streams_of[2], (D,), jnp.float32), 0.5, 1.5).astype(jnp.bfloat16),
        "attn_shift": bell_draw(streams_of[3], (D,), 0.5, 3.0, ((0, 32),)),
        "qkv_weight": draw_qkv_weight(jax.random.fold_in(streams_of[16], 71), 0),
        "qkv_bias": bell_draw(streams_of[5], (3 * D,), 0.3, 2.0, ((0, 32),)),
        "proj_weight": bell_draw(streams_of[6], (D, D), (D // 64) ** -0.5, 1.5, ((0, 32),)),
        "proj_bias": bell_draw(streams_of[7], (D,), 0.3, 2.0, ((0, 32),)),
        "mlp_gain": jnp.clip(1.0 + 0.1 * jax.random.normal(streams_of[8], (D,), jnp.float32), 0.5, 1.5).astype(jnp.bfloat16),
        "mlp_shift": bell_draw(streams_of[9], (D,), 0.5, 3.0, ((0, 32),)),
        "up_weight": bell_draw(streams_of[10], (D, FF), D ** -0.5, 0.1875, ((0, 32),)),
        "up_bias": bell_draw(streams_of[11], (FF,), 0.5, 3.0, ((0, 32),)),
        "down_weight": bell_draw(streams_of[12], (FF, D), FF ** -0.5, 0.09375, ((0, 32),)),
        "down_bias": bell_draw(streams_of[13], (D,), 0.3, 2.0, ((0, 32),)),
        "picture_starts": draw_picture_starts(jax.random.fold_in(streams_of[16], 71), 0),
        "group_order": jax.random.permutation(streams_of[15], N_CTX).astype(jnp.int32),
    }


norm_eps = 1e-05
clip_bound = 8.0
rotary_base = 10000.0
masked_score = -1e+30

@jax.custom_vjp
def low(v):
    return lax.optimization_barrier(v.astype(jnp.bfloat16)).astype(jnp.float32)

@jax.custom_vjp
def low_back(v):
    return v

def low_keep(v):
    return (low(v), None)

def low_pass(kept, grad):
    return (grad,)

def back_keep(v):
    return (v, None)

def back_low(kept, grad):
    return (low(grad),)
low.defvjp(low_keep, low_pass)
low_back.defvjp(back_keep, back_low)

def rotate(values, positions, turn_sign):
    half_rot = ROT // 2
    inv_freq = rotary_base ** (-2.0 * jnp.arange(half_rot, dtype=jnp.float32) / ROT)
    angles = positions.astype(jnp.float32)[:, None] * inv_freq[None, :]
    cosine = jnp.cos(angles)[:, None, :]
    sine_part = turn_sign * jnp.sin(angles)[:, None, :]
    lead_half = values[..., :half_rot]
    tail_half = values[..., half_rot:ROT]
    return jnp.concatenate([lead_half * cosine - tail_half * sine_part, tail_half * cosine + lead_half * sine_part, values[..., ROT:]], axis=-1)

def piece_ids(positions, seq_starts):
    inside = (positions[:, None] >= seq_starts[None, :]) & (positions[:, None] < seq_starts[None, :] + PIC)
    labels = jnp.arange(1, PICS + 1, dtype=jnp.int32)[None, :]
    return lax.optimization_barrier(jnp.sum(jnp.where(inside, labels, 0), axis=1)).astype(jnp.int32)

def block_layer(params, hidden, positions, piece_of_row):
    attn_gain, attn_shift, qkv_weight, qkv_bias, proj_weight, proj_bias, mlp_gain, mlp_shift, up_weight, up_bias, down_weight, down_bias = params
    length = hidden.shape[0]
    score_scale = HD ** (-0.5)
    highest = lax.Precision.HIGHEST
    centered = hidden - lax.optimization_barrier(jnp.mean(hidden, axis=-1, keepdims=True))
    normed = centered * lax.rsqrt(lax.optimization_barrier(jnp.mean(centered * centered, axis=-1, keepdims=True)) + norm_eps)
    norm_attn = low(normed * attn_gain + attn_shift)
    norm_mlp = low(normed * mlp_gain + mlp_shift)
    qkv_full = low_back(jnp.dot(norm_attn, qkv_weight, precision=highest) + qkv_bias).reshape(length, 3, H, HD)
    queries = low(rotate(qkv_full[:, 0], positions, 1.0))
    key_rows = low(rotate(qkv_full[:, 1], positions, 1.0))
    value_rows = low(qkv_full[:, 2])
    block_rows = math.gcd(length, 512)

    def attend(block_index):
        row_begin = block_index * block_rows
        row_block = lax.dynamic_slice_in_dim(queries, row_begin, block_rows, 0)
        row_pos = lax.dynamic_slice_in_dim(positions, row_begin, block_rows, 0)
        row_ids = lax.dynamic_slice_in_dim(piece_of_row, row_begin, block_rows, 0)
        allowed = (positions[None, :] <= row_pos[:, None]) | (row_ids[:, None] == piece_of_row[None, :]) & (row_ids[:, None] > 0)
        scores = low_back(jnp.einsum('qhd,khd->hqk', row_block, key_rows, precision=highest) * score_scale)
        masked = jnp.where(allowed[None], scores, masked_score)
        row_peak = lax.optimization_barrier(jnp.max(masked, axis=-1, keepdims=True))
        weights = jnp.where(allowed[None], jnp.exp(masked - row_peak), 0.0)
        prob_rows = weights / lax.optimization_barrier(jnp.sum(weights, axis=-1, keepdims=True))
        attended = jnp.einsum('hqk,khd->qhd', low(prob_rows), value_rows, precision=highest)
        return (attended, lax.optimization_barrier(jnp.max(row_peak[..., 0], axis=1)))
    per_block, block_peaks = lax.map(jax.checkpoint(attend), jnp.arange(length // block_rows, dtype=jnp.int32))
    attended_low = low_back(low(per_block.reshape(length, H * HD)))
    attn_out = jnp.dot(attended_low, proj_weight, precision=highest) + proj_bias
    up_act = low_back(jnp.dot(norm_mlp, up_weight, precision=highest) + up_bias)
    act_low = low(jax.nn.gelu(up_act, approximate=False))
    down_out = jnp.dot(act_low, down_weight, precision=highest) + down_bias
    return (hidden + attn_out + down_out, lax.optimization_barrier(jnp.max(block_peaks, axis=0)))

def reference(hidden_in, out_cotangent, attn_gain, attn_shift, qkv_weight, qkv_bias, proj_weight, proj_bias, mlp_gain, mlp_shift, up_weight, up_bias, down_weight, down_bias, picture_starts, group_order):
    params = (attn_gain.astype(jnp.float32), attn_shift.astype(jnp.float32), qkv_weight.astype(jnp.float32), qkv_bias.astype(jnp.float32), proj_weight.astype(jnp.float32), proj_bias.astype(jnp.float32), mlp_gain.astype(jnp.float32), mlp_shift.astype(jnp.float32), up_weight.astype(jnp.float32), up_bias.astype(jnp.float32), down_weight.astype(jnp.float32), down_bias.astype(jnp.float32))
    positions = (group_order[:, None] * GROUP + jnp.arange(GROUP, dtype=jnp.int32)[None, :]).reshape(-1).astype(jnp.int32)

    def per_sequence(running, inputs):
        totals, all_peak = running
        hidden, cotangent, seq_starts = inputs
        piece_of_row = piece_ids(positions, seq_starts)

        def apply_layer(layer_params, layer_input):
            return block_layer(layer_params, layer_input, positions, piece_of_row)
        result, pullback, seq_peak = jax.vjp(apply_layer, params, hidden.astype(jnp.float32), has_aux=True)
        param_grads, grad_h = pullback(cotangent.astype(jnp.float32))
        totals = jax.tree.map(lambda acc, extra: acc + extra, totals, param_grads)
        return ((totals, jnp.maximum(all_peak, seq_peak)), (result.astype(jnp.bfloat16), grad_h.astype(jnp.bfloat16)))
    zero_grads = tuple((jnp.zeros_like(item) for item in params))
    start_peak = jnp.full((H,), masked_score, jnp.float32)
    (totals, all_peak), (block_out, grad_hidden) = lax.scan(per_sequence, (zero_grads, start_peak), (hidden_in, out_cotangent, picture_starts))
    clip_ratio = jnp.sqrt(clip_bound / jnp.maximum(all_peak, clip_bound))
    head_cols = jnp.repeat(clip_ratio, HD)
    factor = jnp.concatenate([head_cols, head_cols, jnp.ones((D,), jnp.float32)])
    clipped_qkv = params[2] * factor[None, :]
    return (block_out, grad_hidden, totals[0], totals[1], totals[2], totals[3], totals[4], totals[5], totals[6], totals[7], totals[8], totals[9], totals[10], totals[11], clipped_qkv)
```

```python
import math

import jax
import jax.numpy as jnp
from jax import lax
from jax.experimental import pallas as pl
from jax.experimental.pallas import tpu as pltpu
from jax.sharding import PartitionSpec as P

H = 16
HD = 64
ROT = 16
PIC = 256
PICS = 4


norm_eps = 1e-05
clip_bound = 8.0
rotary_base = 10000.0
masked_score = -1e30


def exact_gelu(values):
    return jax.nn.gelu(values, approximate=False)


def rotate(values, positions, turn_sign):
    half_rot = ROT // 2
    inv_freq = rotary_base ** (-2.0 * jnp.arange(half_rot, dtype=jnp.float32) / ROT)
    angles = positions.astype(jnp.float32)[:, None] * inv_freq[None, :]
    cosine = jnp.cos(angles)[None, :, None, :]
    sine_part = turn_sign * jnp.sin(angles)[None, :, None, :]
    lead_half = values[..., :half_rot]
    tail_half = values[..., half_rot:ROT]
    return jnp.concatenate(
        [
            lead_half * cosine - tail_half * sine_part,
            tail_half * cosine + lead_half * sine_part,
            values[..., ROT:],
        ],
        axis=-1,
    )


def positions_of(row_numbers, group_order, group_len):
    group_ids = row_numbers // group_len
    owners = jnp.arange(group_order.shape[0], dtype=jnp.int32)
    placed = jnp.sum(
        jnp.where(group_ids[:, None] == owners[None, :], group_order[None, :], 0), axis=1
    )
    return placed * group_len + row_numbers % group_len


def piece_ids(positions, picture_starts):
    inside = (positions[None, None, :] >= picture_starts[:, :, None]) & (
        positions[None, None, :] < picture_starts[:, :, None] + PIC
    )
    labels = jnp.arange(1, PICS + 1, dtype=jnp.int32)[None, :, None]
    return jnp.sum(jnp.where(inside, labels, 0), axis=1)


def allowed_for(query_pos, query_ids, key_pos, key_ids):
    causal = key_pos[None, None, :] <= query_pos[None, :, None]
    same_piece = (query_ids[:, :, None] == key_ids[:, None, :]) & (query_ids[:, :, None] > 0)
    return (causal | same_piece)[:, None]


def blocked(running, pieces, group_len, step_fn):
    piece_len = pieces[0].shape[1]
    step_len = math.gcd(piece_len, group_len)

    def one_block(current, block_index):
        row_begin = block_index * step_len
        parts = tuple(
            (lax.dynamic_slice_in_dim(member, row_begin, step_len, 1) for member in pieces)
        )
        return (step_fn(current, parts, row_begin), None)

    running, _ = lax.scan(one_block, running, jnp.arange(piece_len // step_len, dtype=jnp.int32))
    return running


def shards(
    hidden_in,
    out_cotangent,
    attn_gain,
    attn_shift,
    qkv_weight,
    qkv_bias,
    proj_weight,
    proj_bias,
    mlp_gain,
    mlp_shift,
    up_weight,
    up_bias,
    down_weight,
    down_bias,
    picture_starts,
    group_order,
):
    batch_size, group_len, model_dim = hidden_in.shape
    token_rows = batch_size * group_len
    shard_rows = attn_gain.shape[0]
    ff_dim = up_weight.shape[1]
    ff_ratio = ff_dim // model_dim
    score_scale = HD ** (-0.5)
    f32 = jnp.float32
    bf16 = jnp.bfloat16
    hidden = hidden_in.reshape(token_rows, model_dim).astype(f32)
    centered = hidden - jnp.mean(hidden, axis=1, keepdims=True)
    inv_std = lax.rsqrt(jnp.mean(centered * centered, axis=1, keepdims=True) + norm_eps)
    normed = centered * inv_std
    own_rows = lax.axis_index("ctx") * group_len + jnp.arange(group_len, dtype=jnp.int32)
    own_pos = positions_of(own_rows, group_order, group_len)
    own_ids = piece_ids(own_pos, picture_starts)
    small_local = jnp.concatenate(
        [
            jnp.stack([attn_gain, attn_shift, mlp_gain, mlp_shift, proj_bias, down_bias], axis=1),
            qkv_bias.reshape(shard_rows, 3),
            up_bias.reshape(shard_rows, ff_ratio),
        ],
        axis=1,
    )
    down_rows = down_weight.reshape(shard_rows, ff_ratio * model_dim)
    small_piece = lax.all_gather(small_local, ("dp", "ctx"), axis=0, tiled=True)
    qkv_piece = lax.all_gather(qkv_weight, ("dp", "ctx"), axis=0, tiled=True)
    up_piece = lax.all_gather(up_weight, ("dp", "ctx"), axis=0, tiled=True)
    piece_len = qkv_piece.shape[0]
    small_f = small_piece.astype(f32)
    attn_piece = (normed * small_f[:, 0] + small_f[:, 1]).astype(bf16)
    mlp_piece = (normed * small_f[:, 2] + small_f[:, 3]).astype(bf16)
    qkv_sum = jnp.dot(attn_piece, qkv_piece, preferred_element_type=f32)
    up_sum = jnp.dot(mlp_piece, up_piece, preferred_element_type=f32)
    bias_table = small_f
    qkv_sum, up_sum, norm_attn, norm_mlp, bias_table = (
        qkv_sum,
        up_sum,
        attn_piece,
        mlp_piece,
        bias_table,
    )
    qkv_full = qkv_sum + bias_table[:, 6:9].reshape(-1)
    up_pre = up_sum + bias_table[:, 9:].reshape(-1)
    split_heads = qkv_full.reshape(batch_size, group_len, 3, H, HD)
    queries = rotate(split_heads[:, :, 0], own_pos, 1.0).astype(bf16)
    key_rows = rotate(split_heads[:, :, 1], own_pos, 1.0).astype(bf16)
    value_rows = split_heads[:, :, 2].astype(bf16)
    query_flat = queries.reshape(batch_size, group_len, model_dim)
    key_flat = key_rows.reshape(batch_size, group_len, model_dim)
    value_flat = value_rows.reshape(batch_size, group_len, model_dim)

    def forward_step(running, parts, row_begin):
        key_part, value_part = parts
        piece_len = key_part.shape[1]
        key_pos = positions_of(
            row_begin + jnp.arange(piece_len, dtype=jnp.int32), group_order, group_len
        )
        allowed = allowed_for(own_pos, own_ids, key_pos, piece_ids(key_pos, picture_starts))
        row_peak, row_total, summed = running
        key_heads = key_part.reshape(batch_size, piece_len, H, HD)
        value_heads = value_part.reshape(batch_size, piece_len, H, HD)
        scores = (
            jnp.einsum("bqhd,bkhd->bhqk", queries, key_heads, preferred_element_type=f32)
            * score_scale
        )
        masked = jnp.where(allowed, scores, masked_score)
        new_peak = jnp.maximum(row_peak, jnp.max(masked, axis=-1))
        row_fade = jnp.exp(row_peak - new_peak)
        weights = jnp.where(allowed, jnp.exp(masked - new_peak[..., None]), 0.0)
        row_total = row_total * row_fade + jnp.sum(weights, axis=-1)
        summed = summed * row_fade[..., None] + jnp.einsum(
            "bhqk,bkhd->bhqd", weights.astype(bf16), value_heads, preferred_element_type=f32
        )
        return (new_peak, row_total, summed)

    start_attn = (
        jnp.full((batch_size, H, group_len), masked_score, f32),
        jnp.zeros((batch_size, H, group_len), f32),
        jnp.zeros((batch_size, H, group_len, HD), f32),
    )
    row_peak, row_total, summed = blocked(
        start_attn,
        (
            lax.all_gather(key_flat, "ctx", axis=1, tiled=True),
            lax.all_gather(value_flat, "ctx", axis=1, tiled=True),
        ),
        group_len,
        forward_step,
    )
    log_total = row_peak + jnp.log(row_total)
    attended = (summed / row_total[..., None]).transpose(0, 2, 1, 3)
    attended_low = attended.reshape(token_rows, model_dim).astype(bf16)
    head_max = lax.pmax(jnp.max(row_peak, axis=(0, 2)), ("dp", "ctx"))
    act_low = exact_gelu(up_pre).astype(bf16)
    proj_piece = lax.all_gather(proj_weight, ("dp", "ctx"), axis=0, tiled=True)
    down_piece = lax.all_gather(down_rows, ("dp", "ctx"), axis=0, tiled=True)
    piece_len = proj_piece.shape[0]
    mix_sum = jnp.dot(attended_low, proj_piece, preferred_element_type=f32)
    mix_sum = mix_sum + jnp.dot(
        act_low, down_piece.reshape(piece_len * ff_ratio, model_dim), preferred_element_type=f32
    )
    block_out = (
        (hidden + mix_sum + bias_table[:, 4] + bias_table[:, 5])
        .astype(bf16)
        .reshape(batch_size, group_len, model_dim)
    )
    grad_y = out_cotangent.reshape(token_rows, model_dim)
    grad_yf = grad_y.astype(f32)
    proj_piece = lax.all_gather(proj_weight, ("dp", "ctx"), axis=0, tiled=True)
    down_piece = lax.all_gather(down_rows, ("dp", "ctx"), axis=0, tiled=True)
    piece_len = proj_piece.shape[0]
    attn_part = jnp.einsum("rd,nd->rn", grad_y, proj_piece, preferred_element_type=f32)
    act_part = jnp.einsum(
        "rd,md->rm",
        grad_y,
        down_piece.reshape(piece_len * ff_ratio, model_dim),
        preferred_element_type=f32,
    )
    grad_attn = attn_part
    grad_act = act_part
    grad_attn, grad_act = (grad_attn, grad_act)
    _, gelu_back = jax.vjp(exact_gelu, up_pre)
    grad_up = gelu_back(grad_act)[0].astype(bf16)
    grad_attended = grad_attn.astype(bf16)
    out_sum = jnp.sum(grad_yf, axis=0)
    out_width = model_dim + ff_ratio * model_dim + 1
    grad_heads = grad_attended.reshape(batch_size, group_len, H, HD)
    row_dot = jnp.sum(grad_heads.astype(f32) * attended, axis=-1).transpose(0, 2, 1)

    def query_step(running, parts, row_begin):
        key_part, value_part = parts
        piece_len = key_part.shape[1]
        key_pos = positions_of(
            row_begin + jnp.arange(piece_len, dtype=jnp.int32), group_order, group_len
        )
        allowed = allowed_for(own_pos, own_ids, key_pos, piece_ids(key_pos, picture_starts))
        key_heads = key_part.reshape(batch_size, piece_len, H, HD)
        value_heads = value_part.reshape(batch_size, piece_len, H, HD)
        scores = (
            jnp.einsum("bqhd,bkhd->bhqk", queries, key_heads, preferred_element_type=f32)
            * score_scale
        )
        masked = jnp.where(allowed, scores, masked_score)
        prob_rows = jnp.where(allowed, jnp.exp(masked - log_total[..., None]), 0.0)
        grad_prob = jnp.einsum(
            "bqhd,bkhd->bhqk", grad_heads, value_heads, preferred_element_type=f32
        )
        grad_scores = (prob_rows * (grad_prob - row_dot[..., None])).astype(bf16)
        return running + jnp.einsum(
            "bhqk,bkhd->bhqd", grad_scores, key_heads, preferred_element_type=f32
        )

    grad_query = (
        blocked(
            jnp.zeros((batch_size, H, group_len, HD), f32),
            (
                lax.all_gather(key_flat, "ctx", axis=1, tiled=True),
                lax.all_gather(value_flat, "ctx", axis=1, tiled=True),
            ),
            group_len,
            query_step,
        )
        * score_scale
    )
    log_total_all, row_dot_all = (
        lax.all_gather(log_total, "ctx", axis=2, tiled=True),
        lax.all_gather(row_dot, "ctx", axis=2, tiled=True),
    )

    def key_step(running, parts, row_begin):
        query_part, grad_part = parts
        piece_len = query_part.shape[1]
        query_pos = positions_of(
            row_begin + jnp.arange(piece_len, dtype=jnp.int32), group_order, group_len
        )
        allowed = allowed_for(query_pos, piece_ids(query_pos, picture_starts), own_pos, own_ids)
        total_part = lax.dynamic_slice_in_dim(log_total_all, row_begin, piece_len, 2)
        dot_part = lax.dynamic_slice_in_dim(row_dot_all, row_begin, piece_len, 2)
        grad_key, grad_value = running
        query_heads = query_part.reshape(batch_size, piece_len, H, HD)
        grad_piece = grad_part.reshape(batch_size, piece_len, H, HD)
        scores = (
            jnp.einsum("bqhd,bkhd->bhqk", query_heads, key_rows, preferred_element_type=f32)
            * score_scale
        )
        masked = jnp.where(allowed, scores, masked_score)
        prob_rows = jnp.where(allowed, jnp.exp(masked - total_part[..., None]), 0.0)
        grad_value = grad_value + jnp.einsum(
            "bhqk,bqhd->bhkd", prob_rows.astype(bf16), grad_piece, preferred_element_type=f32
        )
        grad_prob = jnp.einsum(
            "bqhd,bkhd->bhqk", grad_piece, value_rows, preferred_element_type=f32
        )
        grad_scores = (prob_rows * (grad_prob - dot_part[..., None])).astype(bf16)
        grad_key = grad_key + jnp.einsum(
            "bhqk,bqhd->bhkd", grad_scores, query_heads, preferred_element_type=f32
        )
        return (grad_key, grad_value)

    start_keys = (
        jnp.zeros((batch_size, H, group_len, HD), f32),
        jnp.zeros((batch_size, H, group_len, HD), f32),
    )
    grad_key, grad_value = blocked(
        start_keys,
        (
            lax.all_gather(query_flat, "ctx", axis=1, tiled=True),
            lax.all_gather(
                grad_attended.reshape(batch_size, group_len, model_dim), "ctx", axis=1, tiled=True
            ),
        ),
        group_len,
        key_step,
    )
    grad_key = grad_key * score_scale
    grad_q_back = rotate(grad_query.transpose(0, 2, 1, 3), own_pos, -1.0)
    grad_k_back = rotate(grad_key.transpose(0, 2, 1, 3), own_pos, -1.0)
    grad_v_back = grad_value.transpose(0, 2, 1, 3)
    grad_qkv = (
        jnp.stack([grad_q_back, grad_k_back, grad_v_back], axis=2)
        .reshape(token_rows, 3 * model_dim)
        .astype(bf16)
    )
    qkv_piece = lax.all_gather(qkv_weight, ("dp", "ctx"), axis=0, tiled=True)
    up_piece = lax.all_gather(up_weight, ("dp", "ctx"), axis=0, tiled=True)
    attn_part = jnp.einsum("re,ne->rn", grad_qkv, qkv_piece, preferred_element_type=f32)
    mlp_part = jnp.einsum("rf,nf->rn", grad_up, up_piece, preferred_element_type=f32)
    grad_norm_attn = attn_part
    grad_norm_mlp = mlp_part
    grad_norm_attn, grad_norm_mlp = (grad_norm_attn, grad_norm_mlp)
    gain_table = bias_table[:, 0:4]
    grad_norm = grad_norm_attn * gain_table[:, 0] + grad_norm_mlp * gain_table[:, 2]
    grad_hidden_f = grad_yf + inv_std * (
        grad_norm
        - jnp.mean(grad_norm, axis=1, keepdims=True)
        - normed * jnp.mean(grad_norm * normed, axis=1, keepdims=True)
    )
    grad_hidden = grad_hidden_f.astype(bf16).reshape(batch_size, group_len, model_dim)
    gain_grads = jnp.stack(
        [
            jnp.sum(grad_norm_attn * normed, axis=0),
            jnp.sum(grad_norm_attn, axis=0),
            jnp.sum(grad_norm_mlp * normed, axis=0),
            jnp.sum(grad_norm_mlp, axis=0),
        ],
        axis=1,
    )
    in_small = jnp.concatenate(
        [
            jnp.sum(grad_qkv.astype(f32), axis=0).reshape(model_dim, 3),
            jnp.sum(grad_up.astype(f32), axis=0).reshape(model_dim, ff_ratio),
            gain_grads,
        ],
        axis=1,
    )
    proj_part = jnp.einsum("rn,rd->nd", attended_low, grad_y, preferred_element_type=f32)
    down_part = jnp.einsum("rm,rd->md", act_low, grad_y, preferred_element_type=f32).reshape(
        model_dim, ff_ratio * model_dim
    )
    qkv_part = jnp.einsum("rn,re->ne", norm_attn, grad_qkv, preferred_element_type=f32)
    up_part = jnp.einsum("rn,rf->nf", norm_mlp, grad_up, preferred_element_type=f32)
    every_rows = lax.psum_scatter(
        jnp.concatenate(
            [
                jnp.concatenate([proj_part, down_part, out_sum[:, None]], axis=1),
                jnp.concatenate([qkv_part, up_part, in_small], axis=1),
            ],
            axis=1,
        ),
        ("dp", "ctx"),
        scatter_dimension=0,
        tiled=True,
    )
    out_rows = every_rows[:, :out_width]
    in_rows = every_rows[:, out_width:]
    grad_proj_weight = out_rows[:, :model_dim]
    grad_down_weight = out_rows[:, model_dim : model_dim + ff_ratio * model_dim].reshape(
        shard_rows * ff_ratio, model_dim
    )
    grad_bias_out = out_rows[:, out_width - 1]
    qkv_width = 3 * model_dim
    grad_qkv_weight = in_rows[:, :qkv_width]
    grad_up_weight = in_rows[:, qkv_width : qkv_width + ff_dim]
    tail_cols = in_rows[:, qkv_width + ff_dim :]
    grad_qkv_bias = tail_cols[:, :3].reshape(-1)
    grad_up_bias = tail_cols[:, 3 : 3 + ff_ratio].reshape(-1)
    gain_rows = tail_cols[:, 3 + ff_ratio :]
    clip_ratio = jnp.sqrt(clip_bound / jnp.maximum(head_max, clip_bound))
    head_cols = jnp.repeat(clip_ratio, HD)
    factor = jnp.concatenate([head_cols, head_cols, jnp.ones((model_dim,), f32)])
    clipped_qkv = qkv_weight.astype(f32) * factor[None, :]
    return (
        block_out,
        grad_hidden,
        gain_rows[:, 0],
        gain_rows[:, 1],
        grad_qkv_weight,
        grad_qkv_bias,
        grad_proj_weight,
        grad_bias_out,
        gain_rows[:, 2],
        gain_rows[:, 3],
        grad_up_weight,
        grad_up_bias,
        grad_down_weight,
        grad_bias_out,
        clipped_qkv,
    )


MESH = pl.DeviceIdType.MESH
NT = (((1,), (1,)), ((), ()))
f32 = jnp.float32
bf16 = jnp.bfloat16
CH = 8
NC = 16
SL = 1024
TOK = 2048
D = 1024


def dot(a, b):
    return jnp.dot(a, b, preferred_element_type=f32)


def dot_nt(a, b):
    return lax.dot_general(a, b, NT, preferred_element_type=f32)


def block_kernel(
    go_ref, ps_ref, x_ref, dy_ref, ws_ref, pw_ref, dw_ref,
    bo_ref, gh_ref, gr_ref, gp_ref, sr_ref, ds_ref,
    X, Y, NA, NM, WC, WPD, CT, ST, PK, LIM, SM, BV,
    Q, K, V, VT, KT, PT, ATT, AA, GP, DA, GG, DQ, DK, DV, HM, GN,
    TT, G, GY, GS, PDS, PDR, SROW, DSUM,
    TMP, LP, SB, RSB, SR, RR,
    w_s, w_r, wy_s, wy_r, pd_s, pd_r, ga_s, ga_r, rs_s, rs_r,
    gy_s, gy_r, gg_s, gg_r, gpd_s, gpd_r, sm_s, sm_r, dm_s, dm_r,
):
    d = lax.axis_index("dp")
    c = lax.axis_index("ctx")
    k = c // 2
    j = c % 2
    z = k // 2
    r = z + (k % 2) * (7 - 2 * z)
    head = 8 * j + k

    def ctx_of(pos, core):
        p = (pos + 16) % 8
        return 2 * (2 * p + (p // 4) * (15 - 4 * p)) + core

    right = (d, ctx_of(r + 1, j))
    left = (d, ctx_of(r - 1, j))
    sibling = (d, 2 * k + (1 - j))
    partner = (1 - d, c)

    def rcopy(src, dst, ss, rs, dev):
        return pltpu.make_async_remote_copy(
            src_ref=src, dst_ref=dst, send_sem=ss, recv_sem=rs,
            device_id=dev, device_id_type=MESH,
        )

    barrier = pltpu.get_barrier_semaphore()

    def hello(o, _):
        lin = (d * NC + c + o) % 32
        pl.semaphore_signal(barrier, inc=1, device_id=(lin // NC, lin % NC), device_id_type=MESH)
        return 0

    lax.fori_loop(1, 32, hello, 0)
    pl.semaphore_wait(barrier, 31)

    def w_copy(o, dst_c, row):
        return rcopy(
            ws_ref.at[8 * (dst_c % 2) + dst_c // 2],
            WC.at[pl.ds(pl.multiple_of(row, 32), 32)],
            w_s.at[o], w_r.at[o], (d, dst_c),
        )

    own_row = 32 * (NC * d + c)

    def w_send(o, _):
        w_copy(o, (c + o) % NC, own_row).start()
        return 0

    lax.fori_loop(1, NC, w_send, 0)

    class Gather:
        def __init__(self, buf, own, s, i):
            self.buf, self.own, self.s, self.i = buf, own, s, i

        def at(self, delta, core, lo=0, n=64):
            row = self.s * SL + 64 * ctx_of(r + delta, core) + lo
            return self.buf.at[pl.ds(pl.multiple_of(row, 32), n)]

        def ring(self, t, way):
            delta = -t if way == 0 else t
            region = self.at(delta, j) if t < 3 else self.at(delta, j, 32 * way, 32)
            slot = 4 * way + t
            return rcopy(region, region, ga_s.at[self.i, slot], ga_r.at[self.i, slot],
                         right if way == 0 else left)

        def arrival(self, t, way):
            delta = -(t + 1) if way == 0 else t + 1
            region = self.at(delta, j) if t < 3 else self.at(delta, j, 32 * way, 32)
            slot = 4 * way + t
            return rcopy(region, region, ga_s.at[self.i, slot], ga_r.at[self.i, slot],
                         right if way == 0 else left)

        def sib(self, slot, core):
            delta = (0, -1, -2, -3, 1, 2, 3, 4)[slot]
            region = self.at(delta, core)
            return rcopy(region, region, ga_s.at[self.i, 8 + slot], ga_r.at[self.i, 8 + slot], sibling)

        def start(self):
            row = self.s * SL + 64 * c
            self.buf[pl.ds(pl.multiple_of(row, 64), 64), :] = self.own[self.s * 64:self.s * 64 + 64, :]
            self.ring(0, 0).start()
            self.ring(0, 1).start()
            self.sib(0, j).start()

        def pump(self, t):
            for way in (0, 1):
                self.arrival(t - 1, way).wait_recv()
                if t < 4:
                    self.ring(t, way).start()
                    self.sib((t if way == 0 else 3 + t), j).start()
            if t == 4:
                self.sib(7, j).start()

        def finish(self):
            for slot in range(8):
                self.sib(slot, 1 - j).wait_recv()

        def drain(self):
            for t in range(4):
                self.ring(t, 0).wait_send()
                self.ring(t, 1).wait_send()
            for slot in range(8):
                self.sib(slot, j).wait_send()

    gx = [Gather(X, x_ref, s, s) for s in range(2)]
    gd = [Gather(Y, dy_ref, s, 2 + s) for s in range(2)]
    gx[0].start()
    gx[1].start()

    def pd_copies(jj, dst_dp):
        dev = (dst_dp, 2 * k + d)
        return (
            rcopy(pw_ref, WPD.at[pl.ds(256 + 32 * jj, 32)], pd_s.at[dst_dp, 0], pd_r.at[jj, 0], dev),
            rcopy(dw_ref, WPD.at[pl.ds(128 * jj, 128)], pd_s.at[dst_dp, 1], pd_r.at[jj, 1], dev),
        )

    here = d == j
    for e in range(2):
        @pl.when(jnp.logical_not(here & (d == e)))
        def _():
            for cp in pd_copies(j, e):
                cp.start()

    @pl.when(here)
    def _():
        WPD[pl.ds(256 + 32 * j, 32), :] = pw_ref[...]
        WPD[pl.ds(128 * j, 128), :] = dw_ref[...]
    WPD[320:384, :] = jnp.zeros((64, D), bf16)

    WC[pl.ds(pl.multiple_of(own_row, 32), 32), :] = ws_ref[head]

    def lane(shape):
        return lax.broadcasted_iota(jnp.int32, shape, len(shape) - 1)

    rows_i = lax.broadcasted_iota(jnp.int32, (SL, 128), 0)
    place = jnp.zeros((SL, 128), jnp.int32)
    cols_i = lane((8, SL))
    place_row = jnp.zeros((8, SL), jnp.int32)
    for b in range(NC):
        gob = go_ref[b]
        place = jnp.where((rows_i >> 6) == b, gob, place)
        place_row = jnp.where((cols_i >> 6) == b, gob, place_row)
    place = place * 64 + (rows_i & 63)
    place_row = place_row * 64 + (cols_i & 63)
    PK[...] = place
    for s in range(2):
        lim = place_row
        for p in range(PICS):
            st = ps_ref[s, p]
            lim = jnp.where((place_row >= st) & (place_row < st + PIC), st + (PIC - 1), lim)
        LIM[s] = lim

    def make_table(i, _):
        rows = pl.ds(pl.multiple_of(i * 128, 128), 128)
        ln = lane((128, 128))
        l64 = ln & 63
        freq = jnp.zeros((128, 128), f32)
        for q in range(ROT // 2):
            freq = jnp.where((l64 & 7) == q, float(rotary_base ** (-2.0 * q / ROT)), freq)
        ang = PK[rows, :].astype(f32) * freq
        CT[rows, :] = jnp.where(l64 < ROT, jnp.cos(ang), 1.0)
        sn = jnp.sin(ang)
        ST[rows, :] = jnp.where(l64 < ROT // 2, -sn, jnp.where(l64 < ROT, sn, 0.0))
        return 0

    lax.fori_loop(0, SL // 128, make_table, 0)

    half = pl.ds(pl.multiple_of(512 * d, 512), 512)
    other = pl.ds(pl.multiple_of(512 * (1 - d), 512), 512)

    def w_wait(o, _):
        src_c = (c - o + NC) % NC
        w_copy(o, (c + o) % NC, 32 * (NC * d + src_c)).wait_recv()
        return 0

    lax.fori_loop(1, NC, w_wait, 0)
    wy = rcopy(WC.at[half], WC.at[half], wy_s, wy_r, partner)
    wy.start()
    for t in range(1, 5):
        gx[0].pump(t)
        gx[1].pump(t)
    gd[0].start()
    gd[1].start()
    rcopy(WC.at[other], WC.at[other], wy_s, wy_r, partner).wait_recv()

    for jj in range(2):
        @pl.when(jnp.logical_not(here & (j == jj)))
        def _():
            for cp in pd_copies(jj, 0):
                cp.wait_recv()

    SM[...] = WC[:, 128:256].astype(f32).T[64:80, :]
    en = lane((16, 256))
    vrow = lax.broadcasted_iota(jnp.int32, (16, 256), 0)
    feat = lax.broadcasted_iota(jnp.int32, (D, 256), 0)
    jl = lane((D, 256))
    smb = SM[...].astype(bf16)

    def pick(e_big, e_small, div, first):
        n_big = div(e_big)
        onehot = jnp.where(feat == n_big, 1.0, 0.0).astype(bf16)
        got = dot(smb, onehot)
        width = 3 if first == 6 else 4
        return jnp.sum(jnp.where(vrow == first + e_small - width * div(e_small), got, 0.0), axis=0, keepdims=True)

    def e_qkv(ln):
        return SL * (ln >> 6) + HD * head + (ln & 63)

    bq = pick(e_qkv(jl), e_qkv(en), lambda e: (e * 43691) >> 17, 6)
    bq = jnp.where(lane((1, 256)) < 192, bq, 0.0)
    bu = pick(256 * head + jl, 256 * head + en, lambda e: e >> 2, 9)
    BV[0] = jnp.broadcast_to(bq, (8, 256))
    BV[1] = jnp.broadcast_to(bu, (8, 256))

    ln128 = lane((128, 128))
    low_half = ln128 < 64

    def turn(v, cs, sn, sign):
        l64 = lane(v.shape) & 63
        mate = jnp.where(l64 < ROT // 2, pltpu.roll(v, 120, 1), pltpu.roll(v, 8, 1))
        return v * cs + sign * (mate * sn)

    def normed_of(rows_value):
        x = rows_value.astype(f32)
        cen = x - jnp.mean(x, axis=1, keepdims=True)
        inv = lax.rsqrt(jnp.mean(cen * cen, axis=1, keepdims=True) + norm_eps)
        return cen * inv, inv

    def n_stage(i, _):
        rows = pl.ds(pl.multiple_of(i * 128, 128), 128)
        trow = pl.ds(pl.multiple_of((i % 8) * 128, 128), 128)
        nrm, _ = normed_of(X[rows, :])
        na = (nrm * SM[0:1, :] + SM[1:2, :]).astype(bf16)
        nm = (nrm * SM[2:3, :] + SM[3:4, :]).astype(bf16)
        NA[rows, :] = na
        NM[rows, :] = nm
        qkv = dot(na, WC[:, 0:256]) + BV[0, 0:1, :]
        up = dot(nm, WC[:, 256:512]) + BV[1, 0:1, :]
        rot = turn(qkv[:, 0:128], CT[trow, :], ST[trow, :], 1.0)
        Q[rows, :] = jnp.where(low_half, rot * 0.125, 0.0).astype(bf16)
        K[rows, :] = jnp.where(low_half, pltpu.roll(rot, 64, 1), 0.0).astype(bf16)
        V[rows, :] = jnp.where(low_half, qkv[:, 128:256], 0.0).astype(bf16)
        cdf = 0.5 * (1.0 + lax.erf(up * (2.0 ** -0.5)))
        AA[rows, 0:256] = (up * cdf).astype(bf16)
        GP[rows, :] = cdf + up * (jnp.exp(-0.5 * up * up) * ((2.0 * math.pi) ** -0.5))
        return 0

    for s in range(2):
        gx[s].finish()
        lax.fori_loop(8 * s, 8 * s + 8, n_stage, 0)
        for t in range(1, 3):
            gd[s].pump(t)

    for s in range(2):
        VT[s] = V[s * SL:s * SL + SL, :].astype(f32).T.astype(bf16)
        KT[s] = K[s * SL:s * SL + SL, :].astype(f32).T.astype(bf16)

    HM[...] = jnp.full((8, 256), masked_score, f32)

    def fwd(i, _):
        s = i // 4
        q0 = pl.multiple_of((i % 4) * 256, 256)
        rows = pl.ds(pl.multiple_of(i * 256, 256), 256)
        seq = pl.ds(pl.multiple_of(s * SL, SL), SL)
        st = dot_nt(K[seq, :], Q[rows, :])
        pk = PK[...]
        lim = LIM[s, 0:1, pl.ds(q0, 256)]
        masked = jnp.where(jnp.concatenate([pk, pk], axis=1) <= lim, st, masked_score)
        peak = jnp.max(masked, axis=0, keepdims=True)
        p = jnp.exp(masked - peak)
        tot = jnp.sum(p, axis=0, keepdims=True)
        pt = (p * (1.0 / tot)).astype(bf16)
        PT[i] = pt
        at = dot(VT[s], pt)
        ATT[i] = at
        AA[rows, 256:384] = at.T.astype(bf16)
        HM[...] = jnp.maximum(HM[...], jnp.broadcast_to(peak, (8, 256)))
        return 0

    for s in range(2):
        lax.fori_loop(4 * s, 4 * s + 4, fwd, 0)
        for t in range(3, 5):
            gd[s].pump(t)

    class Scatter:
        def __init__(self, i, s, partial):
            self.i, self.s, self.partial = i, s, partial

        def sib(self, slot):
            return rcopy(SB.at[self.s, slot], SR.at[self.i, slot],
                         rs_s.at[self.i, 8 + slot], rs_r.at[self.i, 8 + slot], sibling)

        def produce(self):
            def one(slot, _):
                mag = 3 - (slot + 1) // 2 + 1
                delta = mag * (2 * (slot % 2) - 1)
                row = self.s * SL + 64 * ctx_of(r + delta, 0)
                TMP[...] = self.partial(row)
                LP[self.s, slot] = TMP[pl.ds(pl.multiple_of(64 * j, 64), 64), :]
                SB[self.s, slot] = TMP[pl.ds(pl.multiple_of(64 * (1 - j), 64), 64), :].astype(bf16)
                self.sib(slot).start()
                return 0
            lax.fori_loop(0, 8, one, 0)

        def lane_sum(self, slot):
            self.sib(slot).wait_recv()
            return LP[self.s, slot] + SR[self.i, slot].astype(f32)

        def ring(self, t, way):
            slot = 4 * way + t
            n = 32 if t == 0 else 64
            return rcopy(RSB.at[self.s, slot, pl.ds(0, n)], RR.at[self.i, slot, pl.ds(0, n)],
                         rs_s.at[self.i, slot], rs_r.at[self.i, slot], right if way == 0 else left)

        def pump(self, t):
            if t == 0:
                v = self.lane_sum(0)
                for way in (0, 1):
                    RSB[self.s, 4 * way, 0:32, :] = v[32 * way:32 * way + 32].astype(bf16)
                    self.ring(0, way).start()
                return
            for way in (0, 1):
                v = self.lane_sum(2 * t - 1 + way)
                self.ring(t - 1, way).wait_recv()
                slot = 4 * way + t
                if t == 1:
                    got = RR[self.i, 4 * way, 0:32, :].astype(f32)
                    if way == 0:
                        RSB[self.s, slot, 0:32, :] = (v[0:32] + got).astype(bf16)
                        RSB[self.s, slot, 32:64, :] = v[32:64].astype(bf16)
                    else:
                        RSB[self.s, slot, 0:32, :] = v[0:32].astype(bf16)
                        RSB[self.s, slot, 32:64, :] = (v[32:64] + got).astype(bf16)
                else:
                    RSB[self.s, slot] = (v + RR[self.i, slot - 1].astype(f32)).astype(bf16)
                self.ring(t, way).start()

        def total(self):
            v = self.lane_sum(7)
            for way in (0, 1):
                self.ring(3, way).wait_recv()
                v = v + RR[self.i, 4 * way + 3].astype(f32)
            return v

        def drain(self):
            for slot in range(8):
                self.sib(slot).wait_send()
            for t in range(4):
                self.ring(t, 0).wait_send()
                self.ring(t, 1).wait_send()

    def out_partial(row):
        return dot(AA[pl.ds(pl.multiple_of(row, 128), 128), :], WPD[...])

    out = [Scatter(s, s, out_partial) for s in range(2)]
    for s in range(2):
        out[s].produce()
        out[s].pump(0)
    for s in range(2):
        out[s].pump(1)

    DSUM[d] = jnp.zeros((8, D), f32)

    def dy_stage(i, _):
        rows = pl.ds(pl.multiple_of(i * 128, 128), 128)
        dyb = Y[rows, :]
        back = dot_nt(dyb, WPD[...])
        GG[rows, 256:512] = (back[:, 0:256] * GP[rows, :]).astype(bf16)
        DA[rows, :] = back[:, 256:384].astype(bf16)
        DSUM[d] += jnp.broadcast_to(jnp.sum(dyb.astype(f32), axis=0, keepdims=True), (8, D))
        return 0

    for s in range(2):
        gd[s].finish()
        lax.fori_loop(8 * s, 8 * s + 8, dy_stage, 0)
        out[s].pump(2)
    dm = rcopy(DSUM.at[d], DSUM.at[d], dm_s, dm_r, partner)
    dm.start()

    def bwd(i, _):
        s = i // 4
        rows = pl.ds(pl.multiple_of(i * 256, 256), 256)
        seq = pl.ds(pl.multiple_of(s * SL, SL), SL)
        q0 = pl.ds(pl.multiple_of((i % 4) * 256, 256), 256)
        da = DA[rows, :]
        rd = jnp.sum(da.astype(f32).T * ATT[i], axis=0, keepdims=True)
        dpt = dot_nt(V[seq, :], da)
        pt = PT[i]
        ds = (pt.astype(f32) * (dpt - rd)).astype(bf16)
        DV[...] += dot(pt, da)
        DK[...] += dot(ds, Q[rows, :])
        DQ[q0, :] = dot(KT[s], ds).T * 0.125
        return 0

    def qkv_back(i, s):
        trow = pl.ds(pl.multiple_of(i * 128, 128), 128)
        rows = pl.ds(pl.multiple_of(s * SL + i * 128, 128), 128)
        both = DQ[trow, :] + pltpu.roll(DK[trow, :], 64, 1)
        GG[rows, 0:128] = turn(both, CT[trow, :], ST[trow, :], -1.0).astype(bf16)
        GG[rows, 128:256] = DV[trow, :].astype(bf16)
        return s

    GN[...] = jnp.zeros((8, D), f32)

    def g_partial(row):
        rows = pl.ds(pl.multiple_of(row, 128), 128)
        nrm, _ = normed_of(X[rows, :])
        gna = dot_nt(GG[rows, 0:256], WC[:, 0:256])
        gnm = dot_nt(GG[rows, 256:512], WC[:, 256:512])
        GN[0:1, :] += jnp.sum(gna * nrm, axis=0, keepdims=True)
        GN[1:2, :] += jnp.sum(gna, axis=0, keepdims=True)
        GN[2:3, :] += jnp.sum(gnm * nrm, axis=0, keepdims=True)
        GN[3:4, :] += jnp.sum(gnm, axis=0, keepdims=True)
        return gna * SM[0:1, :] + gnm * SM[2:3, :]

    grad = [Scatter(2 + s, s, g_partial) for s in range(2)]

    for s in range(2):
        DV[...] = jnp.zeros((SL, 128), f32)
        DK[...] = jnp.zeros((SL, 128), f32)
        lax.fori_loop(4 * s, 4 * s + 4, bwd, 0)
        lax.fori_loop(0, 8, qkv_back, s)
        out[s].pump(3)
        tot = out[s].total()
        bo_ref[s * 64:s * 64 + 64, :] = (
            x_ref[s * 64:s * 64 + 64, :].astype(f32) + tot + SM[4:5, :] + SM[5:6, :]
        ).astype(bf16)
        out[s].drain()
        grad[s].produce()
        grad[s].pump(0)

    def transpose_aa(i, _):
        rows = pl.ds(pl.multiple_of(i * 256, 256), 256)
        TT[0:384, rows] = AA[rows, :].T
        return 0

    lax.fori_loop(0, 8, transpose_aa, 0)

    def pd_grad(i, _):
        cols = pl.ds(pl.multiple_of(i * 256, 256), 256)
        PDS[:, cols] = dot(TT[0:384, :], Y[:, cols]).astype(bf16)
        return 0

    lax.fori_loop(0, 4, pd_grad, 0)

    def gpd_copies(jj, slot_dp):
        dev = (j, 2 * k + jj)
        return (
            rcopy(PDS.at[pl.ds(256 + 32 * jj, 32)], PDR.at[slot_dp, pl.ds(0, 32)],
                  gpd_s.at[jj, 0], gpd_r.at[slot_dp, 0], dev),
            rcopy(PDS.at[pl.ds(128 * jj, 128)], PDR.at[slot_dp, pl.ds(32, 128)],
                  gpd_s.at[jj, 1], gpd_r.at[slot_dp, 1], dev),
        )

    for jj in range(2):
        @pl.when(jnp.logical_not(here & (j == jj)))
        def _():
            for cp in gpd_copies(jj, d):
                cp.start()

    @pl.when(here)
    def _():
        PDR[d, 0:32, :] = PDS[pl.ds(256 + 32 * j, 32), :]
        PDR[d, 32:160, :] = PDS[pl.ds(128 * j, 128), :]

    for s in range(2):
        grad[s].pump(1)

    srow = jnp.zeros((1, 512), f32)
    for i in range(TOK // 256):
        srow = srow + jnp.sum(GG[i * 256:i * 256 + 256, :].astype(f32), axis=0, keepdims=True)
    hmax = jnp.max(HM[...], axis=1, keepdims=True)[0:1, :]
    SROW[...] = jnp.where(lane((1, 512)) == 192, hmax, srow)
    me = NC * d + c
    sr_ref[me] = SROW[...]

    def s_copy(o, slot):
        lin = (me + o) % 32
        return rcopy(SROW, sr_ref.at[slot], sm_s.at[o], sm_r.at[o], (lin // NC, lin % NC))

    def s_send(o, _):
        s_copy(o, me).start()
        return 0

    lax.fori_loop(1, 32, s_send, 0)

    def transpose_gg(i, _):
        rows = pl.ds(pl.multiple_of(i * 256, 256), 256)
        TT[:, rows] = GG[rows, :].T
        return 0

    lax.fori_loop(0, 8, transpose_gg, 0)

    def in_grad(i, _):
        cols = pl.ds(pl.multiple_of(i * 256, 256), 256)
        a = dot(TT[0:256, :], NA[:, cols])
        a = jnp.concatenate([a[0:192], GN[:, cols], a[200:256]], axis=0)
        G[cols, 0:256] = a.T.astype(bf16)
        G[cols, 256:512] = dot(TT[256:512, :], NM[:, cols]).T.astype(bf16)
        return 0

    lax.fori_loop(0, 4, in_grad, 0)
    for s in range(2):
        grad[s].pump(2)
    gy = rcopy(G.at[other], GY, gy_s, gy_r, partner)
    gy.start()
    for s in range(2):
        grad[s].pump(3)
    gy.wait_recv()
    GS[...] = (G[half, :].astype(f32) + GY[...].astype(f32)).astype(bf16)

    def g_copy(o, dst_c, slot):
        return rcopy(GS.at[pl.ds(pl.multiple_of(32 * dst_c, 32), 32)], gr_ref.at[slot],
                     gg_s.at[o], gg_r.at[o], (d, dst_c))

    def g_send(o, _):
        g_copy(o, (c + o) % NC, head).start()
        return 0

    lax.fori_loop(1, NC, g_send, 0)
    gr_ref[head] = GS[pl.ds(pl.multiple_of(32 * c, 32), 32), :]

    for s in range(2):
        tot = grad[s].total()
        own = slice(s * 64, s * 64 + 64)
        nrm, inv = normed_of(x_ref[own, :])
        gh_ref[own, :] = (
            dy_ref[own, :].astype(f32)
            + inv * (tot - jnp.mean(tot, axis=1, keepdims=True)
                     - nrm * jnp.mean(tot * nrm, axis=1, keepdims=True))
        ).astype(bf16)

    for e in range(2):
        @pl.when(jnp.logical_not(here & (d == e)))
        def _():
            for cp in gpd_copies(0, e):
                cp.wait_recv()
    gp_ref[...] = PDR[0].astype(f32) + PDR[1].astype(f32)

    rcopy(DSUM.at[1 - d], DSUM.at[1 - d], dm_s, dm_r, partner).wait_recv()
    ds_ref[...] = DSUM[0] + DSUM[1]

    def g_wait(o, _):
        src_c = (c - o + NC) % NC
        g_copy(o, (c + o) % NC, 8 * (src_c % 2) + src_c // 2).wait_recv()
        return 0

    lax.fori_loop(1, NC, g_wait, 0)

    def s_wait(o, _):
        s_copy(o, (me - o + 32) % 32).wait_recv()
        return 0

    lax.fori_loop(1, 32, s_wait, 0)

    def w_done(o, _):
        w_copy(o, (c + o) % NC, own_row).wait_send()
        g_copy(o, (c + o) % NC, head).wait_send()
        return 0

    lax.fori_loop(1, NC, w_done, 0)

    def s_done(o, _):
        s_copy(o, me).wait_send()
        return 0

    lax.fori_loop(1, 32, s_done, 0)
    wy.wait_send()
    gy.wait_send()
    dm.wait_send()
    for e in range(2):
        @pl.when(jnp.logical_not(here & (d == e)))
        def _():
            for cp in pd_copies(j, e):
                cp.wait_send()

        @pl.when(jnp.logical_not(here & (j == e)))
        def _():
            for cp in gpd_copies(e, d):
                cp.wait_send()
    for item in gx + gd + grad:
        item.drain()


def fast_shards(
    hidden_in, out_cotangent, attn_gain, attn_shift, qkv_weight, qkv_bias, proj_weight, proj_bias,
    mlp_gain, mlp_shift, up_weight, up_bias, down_weight, down_bias, picture_starts, group_order,
):
    rows = attn_gain.shape[0]
    small = jnp.concatenate(
        [
            jnp.stack([attn_gain, attn_shift, mlp_gain, mlp_shift, proj_bias, down_bias], axis=1),
            qkv_bias.reshape(rows, 3),
            up_bias.reshape(rows, 4),
            jnp.zeros((rows, 51), bf16),
        ],
        axis=1,
    )
    ws = jnp.concatenate(
        [
            qkv_weight.reshape(rows, 3, H, HD).transpose(2, 0, 1, 3).reshape(H, rows, 3 * HD),
            jnp.broadcast_to(small[None], (H, rows, 64)),
            up_weight.reshape(rows, H, 256).transpose(1, 0, 2),
        ],
        axis=2,
    )
    vm = pl.BlockSpec(memory_space=pltpu.VMEM)
    sm = pl.BlockSpec(memory_space=pltpu.SMEM)
    V_ = pltpu.VMEM
    dma = pltpu.SemaphoreType.DMA
    bo, gh, gr, gp, sr, ds = pl.pallas_call(
        block_kernel,
        out_shape=(
            jax.ShapeDtypeStruct((128, D), bf16),
            jax.ShapeDtypeStruct((128, D), bf16),
            jax.ShapeDtypeStruct((NC, 32, 512), bf16),
            jax.ShapeDtypeStruct((160, D), f32),
            jax.ShapeDtypeStruct((32, 1, 512), f32),
            jax.ShapeDtypeStruct((8, D), f32),
        ),
        in_specs=[sm, sm] + [vm] * 5,
        out_specs=(vm,) * 6,
        scratch_shapes=[
            V_((TOK, D), bf16), V_((TOK, D), bf16), V_((TOK, D), bf16), V_((TOK, D), bf16),
            V_((D, 512), bf16), V_((384, D), bf16),
            V_((SL, 128), f32), V_((SL, 128), f32), V_((SL, 128), jnp.int32),
            V_((2, 8, SL), jnp.int32), V_((16, D), f32), V_((2, 8, 256), f32),
            V_((TOK, 128), bf16), V_((TOK, 128), bf16), V_((TOK, 128), bf16),
            V_((2, 128, SL), bf16), V_((2, 128, SL), bf16),
            V_((8, SL, 256), bf16), V_((8, 128, 256), f32),
            V_((TOK, 384), bf16), V_((TOK, 256), f32), V_((TOK, 128), bf16), V_((TOK, 512), bf16),
            V_((SL, 128), f32), V_((SL, 128), f32), V_((SL, 128), f32),
            V_((8, 256), f32), V_((8, D), f32),
            V_((512, TOK), bf16), V_((D, 512), bf16), V_((512, 512), bf16), V_((512, 512), bf16),
            V_((384, D), bf16), V_((2, 160, D), bf16), V_((1, 512), f32), V_((2, 8, D), f32),
            V_((128, D), f32), V_((2, 8, 64, D), f32), V_((2, 8, 64, D), bf16),
            V_((2, 8, 64, D), bf16), V_((4, 8, 64, D), bf16), V_((4, 8, 64, D), bf16),
            dma((NC,)), dma((NC,)), dma, dma, dma((2, 2)), dma((2, 2)), dma((4, 16)), dma((4, 16)),
            dma((4, 16)), dma((4, 16)),
            dma, dma, dma((NC,)), dma((NC,)), dma((2, 2)), dma((2, 2)), dma((32,)), dma((32,)), dma, dma,
        ],
        compiler_params=pltpu.CompilerParams(
            collective_id=0, has_side_effects=True, vmem_limit_bytes=62 * 1024 * 1024
        ),
    )(
        group_order, picture_starts, hidden_in.reshape(128, D), out_cotangent.reshape(128, D),
        ws, proj_weight, down_weight,
    )
    me = NC * lax.axis_index("dp") + lax.axis_index("ctx")
    grf = gr.astype(f32)
    grad_qkv_weight = grf[:, :, :192].reshape(H, rows, 3, HD).transpose(1, 2, 0, 3).reshape(rows, 3 * D)
    grad_up_weight = grf[:, :, 256:].transpose(1, 0, 2).reshape(rows, 4096)
    gains = jnp.sum(grf[:, :, 192:196], axis=0)
    tab = sr.reshape(2, 8, 2, 512).transpose(2, 1, 0, 3).reshape(H, 2, 512)
    tsum = jnp.sum(tab, axis=1)
    qkv_b = tsum[:, :192].reshape(H, 3, HD).transpose(1, 0, 2).reshape(3 * D)
    up_b = tsum[:, 256:].reshape(4096)
    head_max = jnp.max(tab[:, :, 192], axis=1)
    grad_qkv_bias = lax.dynamic_slice(qkv_b, (96 * me,), (96,))
    grad_up_bias = lax.dynamic_slice(up_b, (128 * me,), (128,))
    grad_bias_out = lax.dynamic_slice(ds[0], (32 * me,), (32,))
    clip_ratio = jnp.sqrt(clip_bound / jnp.maximum(head_max, clip_bound))
    head_cols = jnp.repeat(clip_ratio, HD)
    factor = jnp.concatenate([head_cols, head_cols, jnp.ones((D,), f32)])
    clipped_qkv = qkv_weight.astype(f32) * factor[None, :]
    return (
        bo.reshape(2, 64, D), gh.reshape(2, 64, D), gains[:, 0], gains[:, 1],
        grad_qkv_weight, grad_qkv_bias, gp[:32], grad_bias_out, gains[:, 2], gains[:, 3],
        grad_up_weight, grad_up_bias, gp[32:], grad_bias_out, clipped_qkv,
    )


def solution(mesh):
    in_specs = (
        P("dp", "ctx", None),
        P("dp", "ctx", None),
        P(("dp", "ctx")),
        P(("dp", "ctx")),
        P(("dp", "ctx"), None),
        P(("dp", "ctx")),
        P(("dp", "ctx"), None),
        P(("dp", "ctx")),
        P(("dp", "ctx")),
        P(("dp", "ctx")),
        P(("dp", "ctx"), None),
        P(("dp", "ctx")),
        P(("dp", "ctx"), None),
        P(("dp", "ctx")),
        P("dp", None),
        P(),
    )
    out_specs = (
        P("dp", "ctx", None),
        P("dp", "ctx", None),
        P(("dp", "ctx")),
        P(("dp", "ctx")),
        P(("dp", "ctx"), None),
        P(("dp", "ctx")),
        P(("dp", "ctx"), None),
        P(("dp", "ctx")),
        P(("dp", "ctx")),
        P(("dp", "ctx")),
        P(("dp", "ctx"), None),
        P(("dp", "ctx")),
        P(("dp", "ctx"), None),
        P(("dp", "ctx")),
        P(("dp", "ctx"), None),
    )
    body = fast_shards if (mesh.shape["dp"], mesh.shape["ctx"]) == (2, H) else shards
    return jax.shard_map(body, mesh=mesh, in_specs=in_specs, out_specs=out_specs, check_vma=False)
```

```python
import math

import jax
import jax.numpy as jnp
from jax import lax
from jax.experimental import pallas as pl
from jax.experimental.pallas import tpu as pltpu
from jax.sharding import PartitionSpec as P

H = 16
HD = 64
ROT = 16
PIC = 256
PICS = 4


norm_eps = 1e-05
clip_bound = 8.0
rotary_base = 10000.0
masked_score = -1e30


def exact_gelu(values):
    return jax.nn.gelu(values, approximate=False)


def rotate(values, positions, turn_sign):
    half_rot = ROT // 2
    inv_freq = rotary_base ** (-2.0 * jnp.arange(half_rot, dtype=jnp.float32) / ROT)
    angles = positions.astype(jnp.float32)[:, None] * inv_freq[None, :]
    cosine = jnp.cos(angles)[None, :, None, :]
    sine_part = turn_sign * jnp.sin(angles)[None, :, None, :]
    lead_half = values[..., :half_rot]
    tail_half = values[..., half_rot:ROT]
    return jnp.concatenate(
        [
            lead_half * cosine - tail_half * sine_part,
            tail_half * cosine + lead_half * sine_part,
            values[..., ROT:],
        ],
        axis=-1,
    )


def positions_of(row_numbers, group_order, group_len):
    group_ids = row_numbers // group_len
    owners = jnp.arange(group_order.shape[0], dtype=jnp.int32)
    placed = jnp.sum(
        jnp.where(group_ids[:, None] == owners[None, :], group_order[None, :], 0), axis=1
    )
    return placed * group_len + row_numbers % group_len


def piece_ids(positions, picture_starts):
    inside = (positions[None, None, :] >= picture_starts[:, :, None]) & (
        positions[None, None, :] < picture_starts[:, :, None] + PIC
    )
    labels = jnp.arange(1, PICS + 1, dtype=jnp.int32)[None, :, None]
    return jnp.sum(jnp.where(inside, labels, 0), axis=1)


def allowed_for(query_pos, query_ids, key_pos, key_ids):
    causal = key_pos[None, None, :] <= query_pos[None, :, None]
    same_piece = (query_ids[:, :, None] == key_ids[:, None, :]) & (query_ids[:, :, None] > 0)
    return (causal | same_piece)[:, None]


def blocked(running, pieces, group_len, step_fn):
    piece_len = pieces[0].shape[1]
    step_len = math.gcd(piece_len, group_len)

    def one_block(current, block_index):
        row_begin = block_index * step_len
        parts = tuple(
            (lax.dynamic_slice_in_dim(member, row_begin, step_len, 1) for member in pieces)
        )
        return (step_fn(current, parts, row_begin), None)

    running, _ = lax.scan(one_block, running, jnp.arange(piece_len // step_len, dtype=jnp.int32))
    return running


def shards(
    hidden_in,
    out_cotangent,
    attn_gain,
    attn_shift,
    qkv_weight,
    qkv_bias,
    proj_weight,
    proj_bias,
    mlp_gain,
    mlp_shift,
    up_weight,
    up_bias,
    down_weight,
    down_bias,
    picture_starts,
    group_order,
):
    batch_size, group_len, model_dim = hidden_in.shape
    token_rows = batch_size * group_len
    shard_rows = attn_gain.shape[0]
    ff_dim = up_weight.shape[1]
    ff_ratio = ff_dim // model_dim
    score_scale = HD ** (-0.5)
    f32 = jnp.float32
    bf16 = jnp.bfloat16
    hidden = hidden_in.reshape(token_rows, model_dim).astype(f32)
    centered = hidden - jnp.mean(hidden, axis=1, keepdims=True)
    inv_std = lax.rsqrt(jnp.mean(centered * centered, axis=1, keepdims=True) + norm_eps)
    normed = centered * inv_std
    own_rows = lax.axis_index("ctx") * group_len + jnp.arange(group_len, dtype=jnp.int32)
    own_pos = positions_of(own_rows, group_order, group_len)
    own_ids = piece_ids(own_pos, picture_starts)
    small_local = jnp.concatenate(
        [
            jnp.stack([attn_gain, attn_shift, mlp_gain, mlp_shift, proj_bias, down_bias], axis=1),
            qkv_bias.reshape(shard_rows, 3),
            up_bias.reshape(shard_rows, ff_ratio),
        ],
        axis=1,
    )
    down_rows = down_weight.reshape(shard_rows, ff_ratio * model_dim)
    small_piece = lax.all_gather(small_local, ("dp", "ctx"), axis=0, tiled=True)
    qkv_piece = lax.all_gather(qkv_weight, ("dp", "ctx"), axis=0, tiled=True)
    up_piece = lax.all_gather(up_weight, ("dp", "ctx"), axis=0, tiled=True)
    piece_len = qkv_piece.shape[0]
    small_f = small_piece.astype(f32)
    attn_piece = (normed * small_f[:, 0] + small_f[:, 1]).astype(bf16)
    mlp_piece = (normed * small_f[:, 2] + small_f[:, 3]).astype(bf16)
    qkv_sum = jnp.dot(attn_piece, qkv_piece, preferred_element_type=f32)
    up_sum = jnp.dot(mlp_piece, up_piece, preferred_element_type=f32)
    bias_table = small_f
    qkv_sum, up_sum, norm_attn, norm_mlp, bias_table = (
        qkv_sum,
        up_sum,
        attn_piece,
        mlp_piece,
        bias_table,
    )
    qkv_full = qkv_sum + bias_table[:, 6:9].reshape(-1)
    up_pre = up_sum + bias_table[:, 9:].reshape(-1)
    split_heads = qkv_full.reshape(batch_size, group_len, 3, H, HD)
    queries = rotate(split_heads[:, :, 0], own_pos, 1.0).astype(bf16)
    key_rows = rotate(split_heads[:, :, 1], own_pos, 1.0).astype(bf16)
    value_rows = split_heads[:, :, 2].astype(bf16)
    query_flat = queries.reshape(batch_size, group_len, model_dim)
    key_flat = key_rows.reshape(batch_size, group_len, model_dim)
    value_flat = value_rows.reshape(batch_size, group_len, model_dim)

    def forward_step(running, parts, row_begin):
        key_part, value_part = parts
        piece_len = key_part.shape[1]
        key_pos = positions_of(
            row_begin + jnp.arange(piece_len, dtype=jnp.int32), group_order, group_len
        )
        allowed = allowed_for(own_pos, own_ids, key_pos, piece_ids(key_pos, picture_starts))
        row_peak, row_total, summed = running
        key_heads = key_part.reshape(batch_size, piece_len, H, HD)
        value_heads = value_part.reshape(batch_size, piece_len, H, HD)
        scores = (
            jnp.einsum("bqhd,bkhd->bhqk", queries, key_heads, preferred_element_type=f32)
            * score_scale
        )
        masked = jnp.where(allowed, scores, masked_score)
        new_peak = jnp.maximum(row_peak, jnp.max(masked, axis=-1))
        row_fade = jnp.exp(row_peak - new_peak)
        weights = jnp.where(allowed, jnp.exp(masked - new_peak[..., None]), 0.0)
        row_total = row_total * row_fade + jnp.sum(weights, axis=-1)
        summed = summed * row_fade[..., None] + jnp.einsum(
            "bhqk,bkhd->bhqd", weights.astype(bf16), value_heads, preferred_element_type=f32
        )
        return (new_peak, row_total, summed)

    start_attn = (
        jnp.full((batch_size, H, group_len), masked_score, f32),
        jnp.zeros((batch_size, H, group_len), f32),
        jnp.zeros((batch_size, H, group_len, HD), f32),
    )
    row_peak, row_total, summed = blocked(
        start_attn,
        (
            lax.all_gather(key_flat, "ctx", axis=1, tiled=True),
            lax.all_gather(value_flat, "ctx", axis=1, tiled=True),
        ),
        group_len,
        forward_step,
    )
    log_total = row_peak + jnp.log(row_total)
    attended = (summed / row_total[..., None]).transpose(0, 2, 1, 3)
    attended_low = attended.reshape(token_rows, model_dim).astype(bf16)
    head_max = lax.pmax(jnp.max(row_peak, axis=(0, 2)), ("dp", "ctx"))
    act_low = exact_gelu(up_pre).astype(bf16)
    proj_piece = lax.all_gather(proj_weight, ("dp", "ctx"), axis=0, tiled=True)
    down_piece = lax.all_gather(down_rows, ("dp", "ctx"), axis=0, tiled=True)
    piece_len = proj_piece.shape[0]
    mix_sum = jnp.dot(attended_low, proj_piece, preferred_element_type=f32)
    mix_sum = mix_sum + jnp.dot(
        act_low, down_piece.reshape(piece_len * ff_ratio, model_dim), preferred_element_type=f32
    )
    block_out = (
        (hidden + mix_sum + bias_table[:, 4] + bias_table[:, 5])
        .astype(bf16)
        .reshape(batch_size, group_len, model_dim)
    )
    grad_y = out_cotangent.reshape(token_rows, model_dim)
    grad_yf = grad_y.astype(f32)
    proj_piece = lax.all_gather(proj_weight, ("dp", "ctx"), axis=0, tiled=True)
    down_piece = lax.all_gather(down_rows, ("dp", "ctx"), axis=0, tiled=True)
    piece_len = proj_piece.shape[0]
    attn_part = jnp.einsum("rd,nd->rn", grad_y, proj_piece, preferred_element_type=f32)
    act_part = jnp.einsum(
        "rd,md->rm",
        grad_y,
        down_piece.reshape(piece_len * ff_ratio, model_dim),
        preferred_element_type=f32,
    )
    grad_attn = attn_part
    grad_act = act_part
    grad_attn, grad_act = (grad_attn, grad_act)
    _, gelu_back = jax.vjp(exact_gelu, up_pre)
    grad_up = gelu_back(grad_act)[0].astype(bf16)
    grad_attended = grad_attn.astype(bf16)
    out_sum = jnp.sum(grad_yf, axis=0)
    out_width = model_dim + ff_ratio * model_dim + 1
    grad_heads = grad_attended.reshape(batch_size, group_len, H, HD)
    row_dot = jnp.sum(grad_heads.astype(f32) * attended, axis=-1).transpose(0, 2, 1)

    def query_step(running, parts, row_begin):
        key_part, value_part = parts
        piece_len = key_part.shape[1]
        key_pos = positions_of(
            row_begin + jnp.arange(piece_len, dtype=jnp.int32), group_order, group_len
        )
        allowed = allowed_for(own_pos, own_ids, key_pos, piece_ids(key_pos, picture_starts))
        key_heads = key_part.reshape(batch_size, piece_len, H, HD)
        value_heads = value_part.reshape(batch_size, piece_len, H, HD)
        scores = (
            jnp.einsum("bqhd,bkhd->bhqk", queries, key_heads, preferred_element_type=f32)
            * score_scale
        )
        masked = jnp.where(allowed, scores, masked_score)
        prob_rows = jnp.where(allowed, jnp.exp(masked - log_total[..., None]), 0.0)
        grad_prob = jnp.einsum(
            "bqhd,bkhd->bhqk", grad_heads, value_heads, preferred_element_type=f32
        )
        grad_scores = (prob_rows * (grad_prob - row_dot[..., None])).astype(bf16)
        return running + jnp.einsum(
            "bhqk,bkhd->bhqd", grad_scores, key_heads, preferred_element_type=f32
        )

    grad_query = (
        blocked(
            jnp.zeros((batch_size, H, group_len, HD), f32),
            (
                lax.all_gather(key_flat, "ctx", axis=1, tiled=True),
                lax.all_gather(value_flat, "ctx", axis=1, tiled=True),
            ),
            group_len,
            query_step,
        )
        * score_scale
    )
    log_total_all, row_dot_all = (
        lax.all_gather(log_total, "ctx", axis=2, tiled=True),
        lax.all_gather(row_dot, "ctx", axis=2, tiled=True),
    )

    def key_step(running, parts, row_begin):
        query_part, grad_part = parts
        piece_len = query_part.shape[1]
        query_pos = positions_of(
            row_begin + jnp.arange(piece_len, dtype=jnp.int32), group_order, group_len
        )
        allowed = allowed_for(query_pos, piece_ids(query_pos, picture_starts), own_pos, own_ids)
        total_part = lax.dynamic_slice_in_dim(log_total_all, row_begin, piece_len, 2)
        dot_part = lax.dynamic_slice_in_dim(row_dot_all, row_begin, piece_len, 2)
        grad_key, grad_value = running
        query_heads = query_part.reshape(batch_size, piece_len, H, HD)
        grad_piece = grad_part.reshape(batch_size, piece_len, H, HD)
        scores = (
            jnp.einsum("bqhd,bkhd->bhqk", query_heads, key_rows, preferred_element_type=f32)
            * score_scale
        )
        masked = jnp.where(allowed, scores, masked_score)
        prob_rows = jnp.where(allowed, jnp.exp(masked - total_part[..., None]), 0.0)
        grad_value = grad_value + jnp.einsum(
            "bhqk,bqhd->bhkd", prob_rows.astype(bf16), grad_piece, preferred_element_type=f32
        )
        grad_prob = jnp.einsum(
            "bqhd,bkhd->bhqk", grad_piece, value_rows, preferred_element_type=f32
        )
        grad_scores = (prob_rows * (grad_prob - dot_part[..., None])).astype(bf16)
        grad_key = grad_key + jnp.einsum(
            "bhqk,bqhd->bhkd", grad_scores, query_heads, preferred_element_type=f32
        )
        return (grad_key, grad_value)

    start_keys = (
        jnp.zeros((batch_size, H, group_len, HD), f32),
        jnp.zeros((batch_size, H, group_len, HD), f32),
    )
    grad_key, grad_value = blocked(
        start_keys,
        (
            lax.all_gather(query_flat, "ctx", axis=1, tiled=True),
            lax.all_gather(
                grad_attended.reshape(batch_size, group_len, model_dim), "ctx", axis=1, tiled=True
            ),
        ),
        group_len,
        key_step,
    )
    grad_key = grad_key * score_scale
    grad_q_back = rotate(grad_query.transpose(0, 2, 1, 3), own_pos, -1.0)
    grad_k_back = rotate(grad_key.transpose(0, 2, 1, 3), own_pos, -1.0)
    grad_v_back = grad_value.transpose(0, 2, 1, 3)
    grad_qkv = (
        jnp.stack([grad_q_back, grad_k_back, grad_v_back], axis=2)
        .reshape(token_rows, 3 * model_dim)
        .astype(bf16)
    )
    qkv_piece = lax.all_gather(qkv_weight, ("dp", "ctx"), axis=0, tiled=True)
    up_piece = lax.all_gather(up_weight, ("dp", "ctx"), axis=0, tiled=True)
    attn_part = jnp.einsum("re,ne->rn", grad_qkv, qkv_piece, preferred_element_type=f32)
    mlp_part = jnp.einsum("rf,nf->rn", grad_up, up_piece, preferred_element_type=f32)
    grad_norm_attn = attn_part
    grad_norm_mlp = mlp_part
    grad_norm_attn, grad_norm_mlp = (grad_norm_attn, grad_norm_mlp)
    gain_table = bias_table[:, 0:4]
    grad_norm = grad_norm_attn * gain_table[:, 0] + grad_norm_mlp * gain_table[:, 2]
    grad_hidden_f = grad_yf + inv_std * (
        grad_norm
        - jnp.mean(grad_norm, axis=1, keepdims=True)
        - normed * jnp.mean(grad_norm * normed, axis=1, keepdims=True)
    )
    grad_hidden = grad_hidden_f.astype(bf16).reshape(batch_size, group_len, model_dim)
    gain_grads = jnp.stack(
        [
            jnp.sum(grad_norm_attn * normed, axis=0),
            jnp.sum(grad_norm_attn, axis=0),
            jnp.sum(grad_norm_mlp * normed, axis=0),
            jnp.sum(grad_norm_mlp, axis=0),
        ],
        axis=1,
    )
    in_small = jnp.concatenate(
        [
            jnp.sum(grad_qkv.astype(f32), axis=0).reshape(model_dim, 3),
            jnp.sum(grad_up.astype(f32), axis=0).reshape(model_dim, ff_ratio),
            gain_grads,
        ],
        axis=1,
    )
    proj_part = jnp.einsum("rn,rd->nd", attended_low, grad_y, preferred_element_type=f32)
    down_part = jnp.einsum("rm,rd->md", act_low, grad_y, preferred_element_type=f32).reshape(
        model_dim, ff_ratio * model_dim
    )
    qkv_part = jnp.einsum("rn,re->ne", norm_attn, grad_qkv, preferred_element_type=f32)
    up_part = jnp.einsum("rn,rf->nf", norm_mlp, grad_up, preferred_element_type=f32)
    every_rows = lax.psum_scatter(
        jnp.concatenate(
            [
                jnp.concatenate([proj_part, down_part, out_sum[:, None]], axis=1),
                jnp.concatenate([qkv_part, up_part, in_small], axis=1),
            ],
            axis=1,
        ),
        ("dp", "ctx"),
        scatter_dimension=0,
        tiled=True,
    )
    out_rows = every_rows[:, :out_width]
    in_rows = every_rows[:, out_width:]
    grad_proj_weight = out_rows[:, :model_dim]
    grad_down_weight = out_rows[:, model_dim : model_dim + ff_ratio * model_dim].reshape(
        shard_rows * ff_ratio, model_dim
    )
    grad_bias_out = out_rows[:, out_width - 1]
    qkv_width = 3 * model_dim
    grad_qkv_weight = in_rows[:, :qkv_width]
    grad_up_weight = in_rows[:, qkv_width : qkv_width + ff_dim]
    tail_cols = in_rows[:, qkv_width + ff_dim :]
    grad_qkv_bias = tail_cols[:, :3].reshape(-1)
    grad_up_bias = tail_cols[:, 3 : 3 + ff_ratio].reshape(-1)
    gain_rows = tail_cols[:, 3 + ff_ratio :]
    clip_ratio = jnp.sqrt(clip_bound / jnp.maximum(head_max, clip_bound))
    head_cols = jnp.repeat(clip_ratio, HD)
    factor = jnp.concatenate([head_cols, head_cols, jnp.ones((model_dim,), f32)])
    clipped_qkv = qkv_weight.astype(f32) * factor[None, :]
    return (
        block_out,
        grad_hidden,
        gain_rows[:, 0],
        gain_rows[:, 1],
        grad_qkv_weight,
        grad_qkv_bias,
        grad_proj_weight,
        grad_bias_out,
        gain_rows[:, 2],
        gain_rows[:, 3],
        grad_up_weight,
        grad_up_bias,
        grad_down_weight,
        grad_bias_out,
        clipped_qkv,
    )


MESH = pl.DeviceIdType.MESH
NT = (((1,), (1,)), ((), ()))
f32 = jnp.float32
bf16 = jnp.bfloat16
CH = 8
NC = 16
SL = 1024
TOK = 2048
D = 1024


def dot(a, b):
    return jnp.dot(a, b, preferred_element_type=f32)


def dot_nt(a, b):
    return lax.dot_general(a, b, NT, preferred_element_type=f32)


def block_kernel(
    go_ref, ps_ref, x_ref, dy_ref, qw_ref, uw_ref, pw_ref, dw_ref,
    ag_ref, as_ref, mg_ref, ms_ref, pb_ref, db_ref, qb_ref, ub_ref,
    bo_ref, gh_ref, gra_ref, grb_ref, gp_ref, sr_ref, ds_ref,
    QW, UW, V0, V1, V2, V3, V4, V5, V6, V7, WS,
    X, Y, NA, NM, WC, WPD, CT, ST, PK, LIM, SM, BV,
    Q, K, V, VT, KT, PT, ATT, AA, GP, DA, GG, DQ, DK, DV, HM, GN,
    TT, GA, GB, GYA, GYB, GSA, GSB, PDS, PDR, SROW, DSUM,
    TMP, LP, SB, RSB, SR, RR,
    in_s, w_s, w_r, wy_s, wy_r, pd_s, pd_r, ga_s, ga_r, rs_s, rs_r,
    gy_s, gy_r, gg_s, gg_r, gpd_s, gpd_r, sm_s, sm_r, dm_s, dm_r,
):
    d = lax.axis_index("dp")
    c = lax.axis_index("ctx")
    k = c // 2
    j = c % 2
    z = k // 2
    r = z + (k % 2) * (7 - 2 * z)
    head = 8 * j + k

    def ctx_of(pos, core):
        p = (pos + 16) % 8
        return 2 * (2 * p + (p // 4) * (15 - 4 * p)) + core

    right = (d, ctx_of(r + 1, j))
    left = (d, ctx_of(r - 1, j))
    sibling = (d, 2 * k + (1 - j))
    partner = (1 - d, c)

    def rcopy(src, dst, ss, rs, dev):
        return pltpu.make_async_remote_copy(
            src_ref=src, dst_ref=dst, send_sem=ss, recv_sem=rs,
            device_id=dev, device_id_type=MESH,
        )

    barrier = pltpu.get_barrier_semaphore()

    def hello(o, _):
        lin = (d * NC + c + o) % 32
        pl.semaphore_signal(barrier, inc=1, device_id=(lin // NC, lin % NC), device_id_type=MESH)
        return 0

    lax.fori_loop(1, 32, hello, 0)

    def own_rows(s):
        return pl.ds(pl.multiple_of(s * SL + 64 * c, 64), 64)

    vecs = (V0, V1, V2, V3, V4, V5, V6, V7)
    fetch = [pltpu.make_async_copy(qw_ref, QW, in_s.at[0]), pltpu.make_async_copy(uw_ref, UW, in_s.at[1])]
    for i, ref in enumerate((ag_ref, as_ref, mg_ref, ms_ref, pb_ref, db_ref)):
        fetch.append(pltpu.make_async_copy(ref, vecs[i], in_s.at[2 + i]))
    fetch.append(pltpu.make_async_copy(qb_ref, vecs[6], in_s.at[8]))
    fetch.append(pltpu.make_async_copy(ub_ref, vecs[7], in_s.at[9]))
    fetch_x = [pltpu.make_async_copy(x_ref.at[s], X.at[own_rows(s)], in_s.at[10 + s]) for s in range(2)]
    fetch_y = [pltpu.make_async_copy(dy_ref.at[s], Y.at[own_rows(s)], in_s.at[12 + s]) for s in range(2)]
    for cp in fetch + fetch_x + fetch_y:
        cp.start()
    for cp in fetch:
        cp.wait()

    def lane(shape):
        return lax.broadcasted_iota(jnp.int32, shape, len(shape) - 1)

    TMP[:, 0:128] = jnp.zeros((128, 128), f32)
    for i in range(6):
        TMP[64 + i:65 + i, 0:32] = vecs[i][...].astype(f32)
    TMP[0:1, 0:96] = V6[...].astype(f32)
    vq, vu = TMP[0:1, 0:128], V7[...].astype(f32)
    for i in range(3):
        TMP[70 + i:71 + i, 0:128] = pltpu.roll(vq, (128 - 32 * i) % 128, 1)
    for i in range(4):
        TMP[73 + i:74 + i, 0:128] = pltpu.roll(vu, (128 - 32 * i) % 128, 1)
    vcols = TMP[:, 0:128].T[0:32, :]
    low32 = lane((32, 128)) < 64
    for hp in range(H // 2):
        q2 = QW[:, 128 * hp:128 * hp + 128].astype(f32)
        k2 = QW[:, D + 128 * hp:D + 128 * hp + 128].astype(f32)
        v2 = QW[:, 2 * D + 128 * hp:2 * D + 128 * hp + 128].astype(f32)
        WS[2 * hp, :, 0:128] = jnp.where(low32, q2, pltpu.roll(k2, 64, 1)).astype(bf16)
        WS[2 * hp + 1, :, 0:128] = jnp.where(low32, pltpu.roll(q2, 64, 1), k2).astype(bf16)
        WS[2 * hp, :, 128:256] = jnp.where(low32, v2, vcols).astype(bf16)
        WS[2 * hp + 1, :, 128:256] = jnp.where(low32, pltpu.roll(v2, 64, 1), vcols).astype(bf16)
    for h in range(H):
        WS[h, :, 256:512] = UW[:, 256 * h:256 * h + 256]

    pl.semaphore_wait(barrier, 31)

    def w_copy(o, dst_c, row):
        return rcopy(
            WS.at[8 * (dst_c % 2) + dst_c // 2],
            WC.at[pl.ds(pl.multiple_of(row, 32), 32)],
            w_s.at[o], w_r.at[o], (d, dst_c),
        )

    own_row = 32 * (NC * d + c)

    def w_send(o, _):
        w_copy(o, (c + o) % NC, own_row).start()
        return 0

    lax.fori_loop(1, NC, w_send, 0)
    WC[pl.ds(pl.multiple_of(own_row, 32), 32), :] = WS[head]

    def wy_copy(o, plane):
        row = 32 * (NC * plane + (c - o + NC) % NC)
        region = WC.at[pl.ds(pl.multiple_of(row, 32), 32)]
        return rcopy(region, region, wy_s.at[o], wy_r.at[o], partner)

    wy_copy(0, d).start()

    class Gather:
        def __init__(self, buf, own, s, i):
            self.buf, self.own, self.s, self.i = buf, own, s, i

        def at(self, delta, core, lo=0, n=64):
            row = self.s * SL + 64 * ctx_of(r + delta, core) + lo
            return self.buf.at[pl.ds(pl.multiple_of(row, 32), n)]

        def ring(self, t, way):
            delta = -t if way == 0 else t
            region = self.at(delta, j) if t < 3 else self.at(delta, j, 32 * way, 32)
            slot = 4 * way + t
            return rcopy(region, region, ga_s.at[self.i, slot], ga_r.at[self.i, slot],
                         right if way == 0 else left)

        def arrival(self, t, way):
            delta = -(t + 1) if way == 0 else t + 1
            region = self.at(delta, j) if t < 3 else self.at(delta, j, 32 * way, 32)
            slot = 4 * way + t
            return rcopy(region, region, ga_s.at[self.i, slot], ga_r.at[self.i, slot],
                         right if way == 0 else left)

        def sib(self, slot, core):
            delta = (0, -1, -2, -3, 1, 2, 3, 4)[slot]
            region = self.at(delta, core)
            return rcopy(region, region, ga_s.at[self.i, 8 + slot], ga_r.at[self.i, 8 + slot], sibling)

        def start(self):
            self.own[self.s].wait()
            self.ring(0, 0).start()
            self.ring(0, 1).start()
            self.sib(0, j).start()

        def pump(self, t):
            for way in (0, 1):
                self.arrival(t - 1, way).wait_recv()
                if t < 4:
                    self.ring(t, way).start()
                    self.sib((t if way == 0 else 3 + t), j).start()
            if t == 4:
                self.sib(7, j).start()

        def ready(self, t):
            for slot in ((0,) if t == 0 else (t, 3 + t) if t < 4 else (7,)):
                self.sib(slot, 1 - j).wait_recv()

        def drain(self):
            for t in range(4):
                self.ring(t, 0).wait_send()
                self.ring(t, 1).wait_send()
            for slot in range(8):
                self.sib(slot, j).wait_send()

    gx = [Gather(X, fetch_x, s, s) for s in range(2)]
    gd = [Gather(Y, fetch_y, s, 2 + s) for s in range(2)]
    gx[0].start()
    gx[1].start()

    def pd_copies(jj, dst_dp):
        dev = (dst_dp, 2 * k + d)
        return (
            rcopy(pw_ref, WPD.at[pl.ds(256 + 32 * jj, 32)], pd_s.at[dst_dp, 0], pd_r.at[jj, 0], dev),
            rcopy(dw_ref, WPD.at[pl.ds(128 * jj, 128)], pd_s.at[dst_dp, 1], pd_r.at[jj, 1], dev),
        )

    here = d == j

    def pd_start():
        for e in range(2):
            @pl.when(jnp.logical_not(here & (d == e)))
            def _():
                for cp in pd_copies(j, e):
                    cp.start()

    local_pd = (
        pltpu.make_async_copy(pw_ref, WPD.at[pl.ds(256 + 32 * j, 32)], in_s.at[14]),
        pltpu.make_async_copy(dw_ref, WPD.at[pl.ds(128 * j, 128)], in_s.at[15]),
    )

    @pl.when(here)
    def _():
        for cp in local_pd:
            cp.start()
    WPD[320:384, :] = jnp.zeros((64, D), bf16)

    rows_i = lax.broadcasted_iota(jnp.int32, (SL, 128), 0)
    place = jnp.zeros((SL, 128), jnp.int32)
    cols_i = lane((8, SL))
    place_row = jnp.zeros((8, SL), jnp.int32)
    for b in range(NC):
        gob = go_ref[b]
        place = jnp.where((rows_i >> 6) == b, gob, place)
        place_row = jnp.where((cols_i >> 6) == b, gob, place_row)
    place = place * 64 + (rows_i & 63)
    place_row = place_row * 64 + (cols_i & 63)
    PK[...] = place
    for s in range(2):
        lim = place_row
        for p in range(PICS):
            st = ps_ref[s, p]
            lim = jnp.where((place_row >= st) & (place_row < st + PIC), st + (PIC - 1), lim)
        LIM[s] = lim

    def make_table(i, _):
        rows = pl.ds(pl.multiple_of(i * 128, 128), 128)
        ln = lane((128, 128))
        l64 = ln & 63
        freq = jnp.zeros((128, 128), f32)
        for q in range(ROT // 2):
            freq = jnp.where((l64 & 7) == q, float(rotary_base ** (-2.0 * q / ROT)), freq)
        ang = PK[rows, :].astype(f32) * freq
        CT[rows, :] = jnp.where(l64 < ROT, jnp.cos(ang), 1.0)
        sn = jnp.sin(ang)
        ST[rows, :] = jnp.where(l64 < ROT // 2, -sn, jnp.where(l64 < ROT, sn, 0.0))
        return 0

    lax.fori_loop(0, SL // 128, make_table, 0)

    half = pl.ds(pl.multiple_of(512 * d, 512), 512)
    other = pl.ds(pl.multiple_of(512 * (1 - d), 512), 512)

    def w_wait(o, _):
        src_c = (c - o + NC) % NC
        w_copy(o, (c + o) % NC, 32 * (NC * d + src_c)).wait_recv()
        wy_copy(o, d).start()
        return 0

    lax.fori_loop(1, NC, w_wait, 0)
    pd_start()
    gx[0].pump(1)
    gx[1].pump(1)

    def wy_wait(o, _):
        wy_copy(o, 1 - d).wait_recv()
        return 0

    lax.fori_loop(0, NC, wy_wait, 0)

    SM[...] = WC[:, 128:256].astype(f32).T[64:80, :]
    en = lane((16, 256))
    vrow = lax.broadcasted_iota(jnp.int32, (16, 256), 0)
    feat = lax.broadcasted_iota(jnp.int32, (D, 256), 0)
    jl = lane((D, 256))
    smb = SM[...].astype(bf16)

    def pick(e_big, e_small, div, first):
        onehot = jnp.where(feat == div(e_big)[0], 1.0, 0.0).astype(bf16)
        got = dot(smb, onehot)
        return jnp.sum(jnp.where(vrow == first + div(e_small)[1], got, 0.0), axis=0, keepdims=True)

    def place_qkv(e):
        owner = ((e >> 5) * 171) >> 9
        return 32 * owner + (e & 31), (e >> 5) - 3 * owner

    def place_up(e):
        return 32 * (e >> 7) + (e & 31), (e >> 5) & 3

    def e_qkv(ln):
        return SL * (ln >> 6) + HD * head + (ln & 63)

    bq = pick(e_qkv(jl), e_qkv(en), place_qkv, 6)
    bq = jnp.where(lane((1, 256)) < 192, bq, 0.0)
    bu = pick(256 * head + jl, 256 * head + en, place_up, 9)
    BV[0] = jnp.broadcast_to(bq, (8, 256))
    BV[1] = jnp.broadcast_to(bu, (8, 256))

    ln128 = lane((128, 128))
    low_half = ln128 < 64

    def turn(v, cs, sn, sign):
        l64 = lane(v.shape) & 63
        mate = jnp.where(l64 < ROT // 2, pltpu.roll(v, 120, 1), pltpu.roll(v, 8, 1))
        return v * cs + sign * (mate * sn)

    def normed_of(rows_value):
        x = rows_value.astype(f32)
        cen = x - jnp.mean(x, axis=1, keepdims=True)
        inv = lax.rsqrt(jnp.mean(cen * cen, axis=1, keepdims=True) + norm_eps)
        return cen * inv, inv

    def n_stage(i, _):
        rows = pl.ds(pl.multiple_of(i * 128, 128), 128)
        trow = pl.ds(pl.multiple_of((i % 8) * 128, 128), 128)
        nrm, _ = normed_of(X[rows, :])
        na = (nrm * SM[0:1, :] + SM[1:2, :]).astype(bf16)
        nm = (nrm * SM[2:3, :] + SM[3:4, :]).astype(bf16)
        NA[rows, :] = na
        NM[rows, :] = nm
        qkv = dot(na, WC[:, 0:256]) + BV[0, 0:1, :]
        up = dot(nm, WC[:, 256:512]) + BV[1, 0:1, :]
        rot = turn(qkv[:, 0:128], CT[trow, :], ST[trow, :], 1.0)
        Q[rows, :] = jnp.where(low_half, rot * 0.125, 0.0).astype(bf16)
        K[rows, :] = jnp.where(low_half, pltpu.roll(rot, 64, 1), 0.0).astype(bf16)
        V[rows, :] = jnp.where(low_half, qkv[:, 128:256], 0.0).astype(bf16)
        cdf = 0.5 * (1.0 + lax.erf(up * (2.0 ** -0.5)))
        AA[rows, 0:256] = (up * cdf).astype(bf16)
        GP[rows, :] = cdf + up * (jnp.exp(-0.5 * up * up) * ((2.0 * math.pi) ** -0.5))
        return 0

    def n_blocks(t):
        for s in range(2):
            gx[s].ready(t)
        count = 2 if t in (0, 4) else 4

        def one(i, _):
            s = i % 2
            delta = t * (1 - 2 * (i // 2))
            return n_stage(8 * s + ctx_of(r + delta, 0) // 2, 0)

        lax.fori_loop(0, count, one, 0)

    def dy_blocks(s, t):
        gd[s].ready(t)
        count = 1 if t in (0, 4) else 2

        def one(i, _):
            return dy_stage(8 * s + ctx_of(r + t * (1 - 2 * i), 0) // 2, 0)

        lax.fori_loop(0, count, one, 0)

    n_blocks(0)
    gx[0].pump(2)
    gx[1].pump(2)
    n_blocks(1)
    gd[0].start()
    gx[0].pump(3)
    gx[1].pump(3)
    n_blocks(2)
    gd[1].start()
    gx[0].pump(4)
    gx[1].pump(4)
    n_blocks(3)
    gd[0].pump(1)
    n_blocks(4)
    gd[1].pump(1)

    for s in range(2):
        VT[s] = V[s * SL:s * SL + SL, :].astype(f32).T.astype(bf16)
        KT[s] = K[s * SL:s * SL + SL, :].astype(f32).T.astype(bf16)

    HM[...] = jnp.full((8, 256), masked_score, f32)

    def fwd(i, _):
        s = i // 4
        q0 = pl.multiple_of((i % 4) * 256, 256)
        rows = pl.ds(pl.multiple_of(i * 256, 256), 256)
        seq = pl.ds(pl.multiple_of(s * SL, SL), SL)
        st = dot_nt(K[seq, :], Q[rows, :])
        pk = PK[...]
        lim = LIM[s, 0:1, pl.ds(q0, 256)]
        masked = jnp.where(jnp.concatenate([pk, pk], axis=1) <= lim, st, masked_score)
        peak = jnp.max(masked, axis=0, keepdims=True)
        p = jnp.exp(masked - peak)
        tot = jnp.sum(p, axis=0, keepdims=True)
        pt = (p * (1.0 / tot)).astype(bf16)
        PT[i] = pt
        at = dot(VT[s], pt)
        ATT[i] = at
        AA[rows, 256:384] = at.T.astype(bf16)
        HM[...] = jnp.maximum(HM[...], jnp.broadcast_to(peak, (8, 256)))
        return 0

    class Scatter:
        def __init__(self, i, s, partial):
            self.i, self.s, self.partial = i, s, partial

        def sib(self, slot):
            return rcopy(SB.at[self.s, slot], SR.at[self.i, slot],
                         rs_s.at[self.i, 8 + slot], rs_r.at[self.i, 8 + slot], sibling)

        def produce(self):
            def one(slot, _):
                mag = 3 - (slot + 1) // 2 + 1
                delta = mag * (2 * (slot % 2) - 1)
                row = self.s * SL + 64 * ctx_of(r + delta, 0)
                TMP[...] = self.partial(row)
                LP[self.s, slot] = TMP[pl.ds(pl.multiple_of(64 * j, 64), 64), :]
                SB[self.s, slot] = TMP[pl.ds(pl.multiple_of(64 * (1 - j), 64), 64), :].astype(bf16)
                self.sib(slot).start()
                return 0
            lax.fori_loop(0, 8, one, 0)

        def lane_sum(self, slot):
            self.sib(slot).wait_recv()
            return LP[self.s, slot] + SR[self.i, slot].astype(f32)

        def ring(self, t, way):
            slot = 4 * way + t
            n = 32 if t == 0 else 64
            return rcopy(RSB.at[self.s, slot, pl.ds(0, n)], RR.at[self.i, slot, pl.ds(0, n)],
                         rs_s.at[self.i, slot], rs_r.at[self.i, slot], right if way == 0 else left)

        def pump(self, t):
            if t == 0:
                v = self.lane_sum(0)
                for way in (0, 1):
                    RSB[self.s, 4 * way, 0:32, :] = v[32 * way:32 * way + 32].astype(bf16)
                    self.ring(0, way).start()
                return
            for way in (0, 1):
                v = self.lane_sum(2 * t - 1 + way)
                self.ring(t - 1, way).wait_recv()
                slot = 4 * way + t
                if t == 1:
                    got = RR[self.i, 4 * way, 0:32, :].astype(f32)
                    if way == 0:
                        RSB[self.s, slot, 0:32, :] = (v[0:32] + got).astype(bf16)
                        RSB[self.s, slot, 32:64, :] = v[32:64].astype(bf16)
                    else:
                        RSB[self.s, slot, 0:32, :] = v[0:32].astype(bf16)
                        RSB[self.s, slot, 32:64, :] = (v[32:64] + got).astype(bf16)
                else:
                    RSB[self.s, slot] = (v + RR[self.i, slot - 1].astype(f32)).astype(bf16)
                self.ring(t, way).start()

        def total(self):
            v = self.lane_sum(7)
            for way in (0, 1):
                self.ring(3, way).wait_recv()
                v = v + RR[self.i, 4 * way + 3].astype(f32)
            return v

        def drain(self):
            for slot in range(8):
                self.sib(slot).wait_send()
            for t in range(4):
                self.ring(t, 0).wait_send()
                self.ring(t, 1).wait_send()

    def out_partial(row):
        return dot(AA[pl.ds(pl.multiple_of(row, 128), 128), :], WPD[...])

    out = [Scatter(s, s, out_partial) for s in range(2)]
    DSUM[d] = jnp.zeros((8, D), f32)

    def dy_stage(i, _):
        rows = pl.ds(pl.multiple_of(i * 128, 128), 128)
        dyb = Y[rows, :]
        back = dot_nt(dyb, WPD[...])
        GG[rows, 256:512] = (back[:, 0:256] * GP[rows, :]).astype(bf16)
        DA[rows, :] = back[:, 256:384].astype(bf16)
        DSUM[d] += jnp.broadcast_to(jnp.sum(dyb.astype(f32), axis=0, keepdims=True), (8, D))
        return 0

    def bwd(i, _):
        s = i // 4
        rows = pl.ds(pl.multiple_of(i * 256, 256), 256)
        seq = pl.ds(pl.multiple_of(s * SL, SL), SL)
        q0 = pl.ds(pl.multiple_of((i % 4) * 256, 256), 256)
        da = DA[rows, :]
        rd = jnp.sum(da.astype(f32).T * ATT[i], axis=0, keepdims=True)
        dpt = dot_nt(V[seq, :], da)
        pt = PT[i]
        ds = (pt.astype(f32) * (dpt - rd)).astype(bf16)
        DV[...] += dot(pt, da)
        DK[...] += dot(ds, Q[rows, :])
        DQ[q0, :] = dot(KT[s], ds).T * 0.125
        return 0

    def qkv_back(i, s):
        trow = pl.ds(pl.multiple_of(i * 128, 128), 128)
        rows = pl.ds(pl.multiple_of(s * SL + i * 128, 128), 128)
        both = DQ[trow, :] + pltpu.roll(DK[trow, :], 64, 1)
        GG[rows, 0:128] = turn(both, CT[trow, :], ST[trow, :], -1.0).astype(bf16)
        GG[rows, 128:256] = DV[trow, :].astype(bf16)
        return s

    GN[...] = jnp.zeros((8, D), f32)

    def g_partial(row):
        rows = pl.ds(pl.multiple_of(row, 128), 128)
        nrm, _ = normed_of(X[rows, :])
        gna = dot_nt(GG[rows, 0:256], WC[:, 0:256])
        gnm = dot_nt(GG[rows, 256:512], WC[:, 256:512])
        GN[0:1, :] += jnp.sum(gna * nrm, axis=0, keepdims=True)
        GN[1:2, :] += jnp.sum(gna, axis=0, keepdims=True)
        GN[2:3, :] += jnp.sum(gnm * nrm, axis=0, keepdims=True)
        GN[3:4, :] += jnp.sum(gnm, axis=0, keepdims=True)
        return gna * SM[0:1, :] + gnm * SM[2:3, :]

    grad = [Scatter(2 + s, s, g_partial) for s in range(2)]

    def out_done(s):
        tot = out[s].total()
        bo_ref[s * 64:s * 64 + 64, :] = (
            X[own_rows(s), :].astype(f32) + tot + SM[4:5, :] + SM[5:6, :]
        ).astype(bf16)
        out[s].drain()

    def bwd_start():
        DV[...] = jnp.zeros((SL, 128), f32)
        DK[...] = jnp.zeros((SL, 128), f32)

    gd[0].pump(2)
    lax.fori_loop(0, 2, fwd, 0)
    for jj in range(2):
        @pl.when(jnp.logical_not(here & (j == jj)))
        def _():
            for cp in pd_copies(jj, 0):
                cp.wait_recv()

    @pl.when(here)
    def _():
        for cp in local_pd:
            cp.wait()

    gd[1].pump(2)
    lax.fori_loop(2, 4, fwd, 0)
    gd[0].pump(3)
    out[0].produce()
    out[0].pump(0)
    gd[1].pump(3)
    lax.fori_loop(4, 6, fwd, 0)
    gd[0].pump(4)
    out[0].pump(1)
    lax.fori_loop(6, 8, fwd, 0)
    gd[1].pump(4)
    out[1].produce()
    out[1].pump(0)
    out[0].pump(2)
    for t in range(5):
        dy_blocks(0, t)
    out[1].pump(1)
    for t in range(5):
        dy_blocks(1, t)
    dm = rcopy(DSUM.at[d], DSUM.at[d], dm_s, dm_r, partner)
    dm.start()
    out[0].pump(3)
    out[1].pump(2)
    bwd_start()
    lax.fori_loop(0, 4, bwd, 0)
    lax.fori_loop(0, 8, qkv_back, 0)
    out[1].pump(3)
    out_done(0)
    grad[0].produce()
    grad[0].pump(0)
    bwd_start()
    lax.fori_loop(4, 6, bwd, 0)
    grad[0].pump(1)
    out_done(1)
    lax.fori_loop(6, 8, bwd, 0)
    grad[0].pump(2)
    lax.fori_loop(0, 8, qkv_back, 1)
    grad[1].produce()
    grad[1].pump(0)
    grad[0].pump(3)

    def transpose_gg(i, _):
        rows = pl.ds(pl.multiple_of(i * 256, 256), 256)
        TT[:, rows] = GG[rows, :].T
        return 0

    lax.fori_loop(0, 8, transpose_gg, 0)

    def qkv_grad(i, _):
        cols = pl.ds(pl.multiple_of(i * 256, 256), 256)
        a = dot(TT[0:256, :], NA[:, cols])
        a = jnp.concatenate([a[0:192], GN[:, cols], a[200:256]], axis=0)
        GA[cols, :] = a.T.astype(bf16)
        return 0

    def up_grad(i, _):
        cols = pl.ds(pl.multiple_of(i * 256, 256), 256)
        GB[cols, :] = dot(TT[256:512, :], NM[:, cols]).T.astype(bf16)
        return 0

    lax.fori_loop(0, 4, qkv_grad, 0)
    gya = rcopy(GA.at[other], GYA, gy_s.at[0], gy_r.at[0], partner)
    gya.start()
    grad[1].pump(1)
    lax.fori_loop(0, 4, up_grad, 0)
    gyb = rcopy(GB.at[other], GYB, gy_s.at[1], gy_r.at[1], partner)
    gyb.start()

    def transpose_aa(i, _):
        rows = pl.ds(pl.multiple_of(i * 256, 256), 256)
        TT[0:384, rows] = AA[rows, :].T
        return 0

    lax.fori_loop(0, 8, transpose_aa, 0)

    def pd_grad(i, _):
        cols = pl.ds(pl.multiple_of(i * 256, 256), 256)
        PDS[:, cols] = dot(TT[0:384, :], Y[:, cols]).astype(bf16)
        return 0

    lax.fori_loop(0, 4, pd_grad, 0)

    def gpd_copies(jj, slot_dp):
        dev = (j, 2 * k + jj)
        return (
            rcopy(PDS.at[pl.ds(256 + 32 * jj, 32)], PDR.at[slot_dp, pl.ds(0, 32)],
                  gpd_s.at[jj, 0], gpd_r.at[slot_dp, 0], dev),
            rcopy(PDS.at[pl.ds(128 * jj, 128)], PDR.at[slot_dp, pl.ds(32, 128)],
                  gpd_s.at[jj, 1], gpd_r.at[slot_dp, 1], dev),
        )

    for jj in range(2):
        @pl.when(jnp.logical_not(here & (j == jj)))
        def _():
            for cp in gpd_copies(jj, d):
                cp.start()

    @pl.when(here)
    def _():
        PDR[d, 0:32, :] = PDS[pl.ds(256 + 32 * j, 32), :]
        PDR[d, 32:160, :] = PDS[pl.ds(128 * j, 128), :]

    grad[1].pump(2)

    srow = jnp.zeros((1, 512), f32)
    for i in range(TOK // 256):
        srow = srow + jnp.sum(GG[i * 256:i * 256 + 256, :].astype(f32), axis=0, keepdims=True)
    hmax = jnp.max(HM[...], axis=1, keepdims=True)[0:1, :]
    SROW[...] = jnp.where(lane((1, 512)) == 192, hmax, srow)
    me = NC * d + c
    sr_ref[me] = SROW[...]

    def s_copy(o, slot):
        lin = (me + o) % 32
        return rcopy(SROW, sr_ref.at[slot], sm_s.at[o], sm_r.at[o], (lin // NC, lin % NC))

    def s_send(o, _):
        s_copy(o, me).start()
        return 0

    lax.fori_loop(1, 32, s_send, 0)

    def g_copy(half_i, o, dst_c, slot):
        src, dst = ((GSA, gra_ref), (GSB, grb_ref))[half_i]
        return rcopy(src.at[pl.ds(pl.multiple_of(32 * dst_c, 32), 32)], dst.at[slot],
                     gg_s.at[half_i, o], gg_r.at[half_i, o], (d, dst_c))

    for half_i, (gy, G, GY, GS, gr_ref) in enumerate(((gya, GA, GYA, GSA, gra_ref), (gyb, GB, GYB, GSB, grb_ref))):
        gy.wait_recv()
        GS[...] = (G[half, :].astype(f32) + GY[...].astype(f32)).astype(bf16)

        def g_send(o, _):
            g_copy(half_i, o, (c + o) % NC, head).start()
            return 0

        lax.fori_loop(1, NC, g_send, 0)
        gr_ref[head] = GS[pl.ds(pl.multiple_of(32 * c, 32), 32), :]
    grad[1].pump(3)

    for s in range(2):
        tot = grad[s].total()
        own = slice(s * 64, s * 64 + 64)
        nrm, inv = normed_of(X[own_rows(s), :])
        gh_ref[own, :] = (
            Y[own_rows(s), :].astype(f32)
            + inv * (tot - jnp.mean(tot, axis=1, keepdims=True)
                     - nrm * jnp.mean(tot * nrm, axis=1, keepdims=True))
        ).astype(bf16)

    for e in range(2):
        @pl.when(jnp.logical_not(here & (d == e)))
        def _():
            for cp in gpd_copies(0, e):
                cp.wait_recv()
    gp_ref[...] = PDR[0].astype(f32) + PDR[1].astype(f32)

    rcopy(DSUM.at[1 - d], DSUM.at[1 - d], dm_s, dm_r, partner).wait_recv()
    ds_ref[...] = DSUM[0] + DSUM[1]

    def g_wait(o, _):
        src_c = (c - o + NC) % NC
        for half_i in range(2):
            g_copy(half_i, o, (c + o) % NC, 8 * (src_c % 2) + src_c // 2).wait_recv()
        return 0

    lax.fori_loop(1, NC, g_wait, 0)

    def s_wait(o, _):
        s_copy(o, (me - o + 32) % 32).wait_recv()
        return 0

    lax.fori_loop(1, 32, s_wait, 0)

    def w_done(o, _):
        w_copy(o, (c + o) % NC, own_row).wait_send()
        for half_i in range(2):
            g_copy(half_i, o, (c + o) % NC, head).wait_send()
        wy_copy(o, d).wait_send()
        return 0

    lax.fori_loop(1, NC, w_done, 0)

    def s_done(o, _):
        s_copy(o, me).wait_send()
        return 0

    lax.fori_loop(1, 32, s_done, 0)
    wy_copy(0, d).wait_send()
    gya.wait_send()
    gyb.wait_send()
    dm.wait_send()
    for e in range(2):
        @pl.when(jnp.logical_not(here & (d == e)))
        def _():
            for cp in pd_copies(j, e):
                cp.wait_send()

        @pl.when(jnp.logical_not(here & (j == e)))
        def _():
            for cp in gpd_copies(e, d):
                cp.wait_send()
    for item in gx + gd + grad:
        item.drain()


def finish_kernel(
    bo, gh, gra, grb, gp, sr, ds, qw,
    o_bo, o_gh, o_ag, o_as, o_qw, o_qb, o_pw, o_pb, o_mg, o_ms, o_uw, o_ub, o_dw, o_db, o_cq,
    B, F,
):
    me = NC * lax.axis_index("dp") + lax.axis_index("ctx")
    for s in range(2):
        o_bo[s] = bo[64 * s:64 * s + 64, :]
        o_gh[s] = gh[64 * s:64 * s + 64, :]
    o_pw[...] = gp[0:32, :]
    o_dw[...] = gp[32:160, :]
    low = lax.broadcasted_iota(jnp.int32, (32, 128), 1) < 64
    low1 = low[0:1]
    gains = jnp.zeros((32, 128), f32)
    for h in range(H):
        at = 2 * (h % 8) + h // 8
        one, two = sr[at], sr[NC + at]
        both = one + two
        peak = jnp.maximum(one, two)
        col = lax.broadcasted_iota(jnp.int32, (1, 512), 1)
        B[h:h + 1, :] = jnp.where(col == 192, peak, both)
        F[32 + 2 * h:33 + 2 * h, :] = both[:, 256:384]
        F[33 + 2 * h:34 + 2 * h, :] = both[:, 384:512]
        gains = gains + gra[h, :, 128:256].astype(f32)
        o_uw[:, 256 * h:256 * h + 256] = grb[h].astype(f32)
    top = B[:, 128:256]
    top = jnp.max(jnp.where(lax.broadcasted_iota(jnp.int32, (H, 128), 1) == 64, top, masked_score), axis=1, keepdims=True)
    ratio = jnp.broadcast_to(jnp.sqrt(clip_bound / jnp.maximum(top, clip_bound)), (H, 128))
    F[24:32, :] = jnp.zeros((8, 128), f32)
    for hp in range(H // 2):
        a, b = gra[2 * hp, :, 0:128].astype(f32), gra[2 * hp + 1, :, 0:128].astype(f32)
        va, vb = gra[2 * hp, :, 128:256].astype(f32), gra[2 * hp + 1, :, 128:256].astype(f32)
        o_qw[:, 128 * hp:128 * hp + 128] = jnp.where(low, a, pltpu.roll(b, 64, 1))
        o_qw[:, D + 128 * hp:D + 128 * hp + 128] = jnp.where(low, pltpu.roll(a, 64, 1), b)
        o_qw[:, 2 * D + 128 * hp:2 * D + 128 * hp + 128] = jnp.where(low, va, pltpu.roll(vb, 64, 1))
        ra, rb = B[2 * hp:2 * hp + 1, 0:128], B[2 * hp + 1:2 * hp + 2, 0:128]
        sa, sb = B[2 * hp:2 * hp + 1, 128:256], B[2 * hp + 1:2 * hp + 2, 128:256]
        F[hp:hp + 1, :] = jnp.where(low1, ra, pltpu.roll(rb, 64, 1))
        F[8 + hp:9 + hp, :] = jnp.where(low1, pltpu.roll(ra, 64, 1), rb)
        F[16 + hp:17 + hp, :] = jnp.where(low1, sa, pltpu.roll(sb, 64, 1))
        fac = jnp.where(low1, ratio[2 * hp:2 * hp + 1], ratio[2 * hp + 1:2 * hp + 2])
        for part in range(3):
            cols = slice(part * D + 128 * hp, part * D + 128 * hp + 128)
            w = qw[:, cols].astype(f32)
            o_cq[:, cols] = w * fac if part < 2 else w
    grows = jnp.concatenate([gains, jnp.zeros((96, 128), f32)], axis=0).T
    for i, o in enumerate((o_ag, o_as, o_mg, o_ms)):
        o[...] = grows[64 + i:65 + i, 0:32]
    row, shift = (96 * me) // 128, (96 * me) % 128
    turned = pltpu.roll(F[pl.ds(row, 1), :], (128 - shift) % 128, 1)
    after = pltpu.roll(F[pl.ds(row + 1, 1), :], (128 - shift) % 128, 1)
    col = lax.broadcasted_iota(jnp.int32, (1, 128), 1)
    o_qb[...] = jnp.where(col < 128 - shift, turned, after)[:, 0:96]
    o_ub[...] = F[pl.ds(32 + me, 1), :]
    dsum = ds[0:1, pl.ds(pl.multiple_of(128 * (me // 4), 128), 128)]
    dsum = pltpu.roll(dsum, (128 - 32 * (me % 4)) % 128, 1)[:, 0:32]
    o_pb[...] = dsum
    o_db[...] = dsum


def fast_shards(
    hidden_in, out_cotangent, attn_gain, attn_shift, qkv_weight, qkv_bias, proj_weight, proj_bias,
    mlp_gain, mlp_shift, up_weight, up_bias, down_weight, down_bias, picture_starts, group_order,
):
    vm = pl.BlockSpec(memory_space=pltpu.VMEM)
    sm = pl.BlockSpec(memory_space=pltpu.SMEM)
    hbm = pl.BlockSpec(memory_space=pl.ANY)
    V_ = pltpu.VMEM
    dma = pltpu.SemaphoreType.DMA

    def sds(shape, dtype=f32):
        return jax.ShapeDtypeStruct(shape, dtype)

    got = pl.pallas_call(
        block_kernel,
        out_shape=(
            sds((128, D), bf16), sds((128, D), bf16), sds((NC, 32, 256), bf16), sds((NC, 32, 256), bf16),
            sds((160, D)), sds((32, 1, 512)), sds((8, D)),
        ),
        in_specs=[sm, sm] + [hbm] * 14,
        out_specs=(vm,) * 7,
        scratch_shapes=[
            V_((32, 3 * D), bf16), V_((32, 4 * D), bf16), *(V_((1, n), bf16) for n in (32,) * 6 + (96, 128)), V_((NC, 32, 512), bf16),
            V_((TOK, D), bf16), V_((TOK, D), bf16), V_((TOK, D), bf16), V_((TOK, D), bf16),
            V_((D, 512), bf16), V_((384, D), bf16),
            V_((SL, 128), f32), V_((SL, 128), f32), V_((SL, 128), jnp.int32),
            V_((2, 8, SL), jnp.int32), V_((16, D), f32), V_((2, 8, 256), f32),
            V_((TOK, 128), bf16), V_((TOK, 128), bf16), V_((TOK, 128), bf16),
            V_((2, 128, SL), bf16), V_((2, 128, SL), bf16),
            V_((8, SL, 256), bf16), V_((8, 128, 256), f32),
            V_((TOK, 384), bf16), V_((TOK, 256), f32), V_((TOK, 128), bf16), V_((TOK, 512), bf16),
            V_((SL, 128), f32), V_((SL, 128), f32), V_((SL, 128), f32),
            V_((8, 256), f32), V_((8, D), f32),
            V_((512, TOK), bf16), V_((D, 256), bf16), V_((D, 256), bf16),
            V_((512, 256), bf16), V_((512, 256), bf16), V_((512, 256), bf16), V_((512, 256), bf16),
            V_((384, D), bf16), V_((2, 160, D), bf16), V_((1, 512), f32), V_((2, 8, D), f32),
            V_((128, D), f32), V_((2, 8, 64, D), f32), V_((2, 8, 64, D), bf16),
            V_((2, 8, 64, D), bf16), V_((4, 8, 64, D), bf16), V_((4, 8, 64, D), bf16),
            dma((16,)), dma((NC,)), dma((NC,)), dma((NC,)), dma((NC,)), dma((2, 2)), dma((2, 2)),
            dma((4, 16)), dma((4, 16)), dma((4, 16)), dma((4, 16)),
            dma((2,)), dma((2,)), dma((2, NC)), dma((2, NC)), dma((2, 2)), dma((2, 2)), dma((32,)), dma((32,)), dma, dma,
        ],
        compiler_params=pltpu.CompilerParams(
            collective_id=0, has_side_effects=True, vmem_limit_bytes=62 * 1024 * 1024
        ),
    )(
        group_order, picture_starts, hidden_in, out_cotangent, qkv_weight, up_weight, proj_weight, down_weight,
        *(v.reshape(1, -1) for v in (
            attn_gain, attn_shift, mlp_gain, mlp_shift, proj_bias, down_bias, qkv_bias, up_bias)),
    )
    r32 = sds((1, 32))
    outs = pl.pallas_call(
        finish_kernel,
        out_shape=(
            sds((2, 64, D), bf16), sds((2, 64, D), bf16), r32, r32, sds((32, 3 * D)), sds((1, 96)),
            sds((32, D)), r32, r32, r32, sds((32, 4 * D)), sds((1, 128)), sds((128, D)), r32, sds((32, 3 * D)),
        ),
        in_specs=[vm] * 8,
        out_specs=(vm,) * 15,
        scratch_shapes=[V_((H, 512), f32), V_((64, 128), f32)],
    )(*got, qkv_weight)
    return tuple(o.reshape(-1) if o.shape[0] == 1 else o for o in outs)


def solution(mesh):
    in_specs = (
        P("dp", "ctx", None),
        P("dp", "ctx", None),
        P(("dp", "ctx")),
        P(("dp", "ctx")),
        P(("dp", "ctx"), None),
        P(("dp", "ctx")),
        P(("dp", "ctx"), None),
        P(("dp", "ctx")),
        P(("dp", "ctx")),
        P(("dp", "ctx")),
        P(("dp", "ctx"), None),
        P(("dp", "ctx")),
        P(("dp", "ctx"), None),
        P(("dp", "ctx")),
        P("dp", None),
        P(),
    )
    out_specs = (
        P("dp", "ctx", None),
        P("dp", "ctx", None),
        P(("dp", "ctx")),
        P(("dp", "ctx")),
        P(("dp", "ctx"), None),
        P(("dp", "ctx")),
        P(("dp", "ctx"), None),
        P(("dp", "ctx")),
        P(("dp", "ctx")),
        P(("dp", "ctx")),
        P(("dp", "ctx"), None),
        P(("dp", "ctx")),
        P(("dp", "ctx"), None),
        P(("dp", "ctx")),
        P(("dp", "ctx"), None),
    )
    body = fast_shards if (mesh.shape["dp"], mesh.shape["ctx"]) == (2, H) else shards
    return jax.shard_map(body, mesh=mesh, in_specs=in_specs, out_specs=out_specs, check_vma=False)
```

```python
import math

import jax
import jax.numpy as jnp
from jax import lax
from jax.experimental import pallas as pl
from jax.experimental.pallas import tpu as pltpu
from jax.sharding import PartitionSpec as P

H = 16
HD = 64
ROT = 16
PIC = 256
PICS = 4


norm_eps = 1e-05
clip_bound = 8.0
rotary_base = 10000.0
masked_score = -1e30


def exact_gelu(values):
    return jax.nn.gelu(values, approximate=False)


def rotate(values, positions, turn_sign):
    half_rot = ROT // 2
    inv_freq = rotary_base ** (-2.0 * jnp.arange(half_rot, dtype=jnp.float32) / ROT)
    angles = positions.astype(jnp.float32)[:, None] * inv_freq[None, :]
    cosine = jnp.cos(angles)[None, :, None, :]
    sine_part = turn_sign * jnp.sin(angles)[None, :, None, :]
    lead_half = values[..., :half_rot]
    tail_half = values[..., half_rot:ROT]
    return jnp.concatenate(
        [
            lead_half * cosine - tail_half * sine_part,
            tail_half * cosine + lead_half * sine_part,
            values[..., ROT:],
        ],
        axis=-1,
    )


def positions_of(row_numbers, group_order, group_len):
    group_ids = row_numbers // group_len
    owners = jnp.arange(group_order.shape[0], dtype=jnp.int32)
    placed = jnp.sum(
        jnp.where(group_ids[:, None] == owners[None, :], group_order[None, :], 0), axis=1
    )
    return placed * group_len + row_numbers % group_len


def piece_ids(positions, picture_starts):
    inside = (positions[None, None, :] >= picture_starts[:, :, None]) & (
        positions[None, None, :] < picture_starts[:, :, None] + PIC
    )
    labels = jnp.arange(1, PICS + 1, dtype=jnp.int32)[None, :, None]
    return jnp.sum(jnp.where(inside, labels, 0), axis=1)


def allowed_for(query_pos, query_ids, key_pos, key_ids):
    causal = key_pos[None, None, :] <= query_pos[None, :, None]
    same_piece = (query_ids[:, :, None] == key_ids[:, None, :]) & (query_ids[:, :, None] > 0)
    return (causal | same_piece)[:, None]


def blocked(running, pieces, group_len, step_fn):
    piece_len = pieces[0].shape[1]
    step_len = math.gcd(piece_len, group_len)

    def one_block(current, block_index):
        row_begin = block_index * step_len
        parts = tuple(
            (lax.dynamic_slice_in_dim(member, row_begin, step_len, 1) for member in pieces)
        )
        return (step_fn(current, parts, row_begin), None)

    running, _ = lax.scan(one_block, running, jnp.arange(piece_len // step_len, dtype=jnp.int32))
    return running


def shards(
    hidden_in,
    out_cotangent,
    attn_gain,
    attn_shift,
    qkv_weight,
    qkv_bias,
    proj_weight,
    proj_bias,
    mlp_gain,
    mlp_shift,
    up_weight,
    up_bias,
    down_weight,
    down_bias,
    picture_starts,
    group_order,
):
    batch_size, group_len, model_dim = hidden_in.shape
    token_rows = batch_size * group_len
    shard_rows = attn_gain.shape[0]
    ff_dim = up_weight.shape[1]
    ff_ratio = ff_dim // model_dim
    score_scale = HD ** (-0.5)
    f32 = jnp.float32
    bf16 = jnp.bfloat16
    hidden = hidden_in.reshape(token_rows, model_dim).astype(f32)
    centered = hidden - jnp.mean(hidden, axis=1, keepdims=True)
    inv_std = lax.rsqrt(jnp.mean(centered * centered, axis=1, keepdims=True) + norm_eps)
    normed = centered * inv_std
    own_rows = lax.axis_index("ctx") * group_len + jnp.arange(group_len, dtype=jnp.int32)
    own_pos = positions_of(own_rows, group_order, group_len)
    own_ids = piece_ids(own_pos, picture_starts)
    small_local = jnp.concatenate(
        [
            jnp.stack([attn_gain, attn_shift, mlp_gain, mlp_shift, proj_bias, down_bias], axis=1),
            qkv_bias.reshape(shard_rows, 3),
            up_bias.reshape(shard_rows, ff_ratio),
        ],
        axis=1,
    )
    down_rows = down_weight.reshape(shard_rows, ff_ratio * model_dim)
    small_piece = lax.all_gather(small_local, ("dp", "ctx"), axis=0, tiled=True)
    qkv_piece = lax.all_gather(qkv_weight, ("dp", "ctx"), axis=0, tiled=True)
    up_piece = lax.all_gather(up_weight, ("dp", "ctx"), axis=0, tiled=True)
    piece_len = qkv_piece.shape[0]
    small_f = small_piece.astype(f32)
    attn_piece = (normed * small_f[:, 0] + small_f[:, 1]).astype(bf16)
    mlp_piece = (normed * small_f[:, 2] + small_f[:, 3]).astype(bf16)
    qkv_sum = jnp.dot(attn_piece, qkv_piece, preferred_element_type=f32)
    up_sum = jnp.dot(mlp_piece, up_piece, preferred_element_type=f32)
    bias_table = small_f
    qkv_sum, up_sum, norm_attn, norm_mlp, bias_table = (
        qkv_sum,
        up_sum,
        attn_piece,
        mlp_piece,
        bias_table,
    )
    qkv_full = qkv_sum + bias_table[:, 6:9].reshape(-1)
    up_pre = up_sum + bias_table[:, 9:].reshape(-1)
    split_heads = qkv_full.reshape(batch_size, group_len, 3, H, HD)
    queries = rotate(split_heads[:, :, 0], own_pos, 1.0).astype(bf16)
    key_rows = rotate(split_heads[:, :, 1], own_pos, 1.0).astype(bf16)
    value_rows = split_heads[:, :, 2].astype(bf16)
    query_flat = queries.reshape(batch_size, group_len, model_dim)
    key_flat = key_rows.reshape(batch_size, group_len, model_dim)
    value_flat = value_rows.reshape(batch_size, group_len, model_dim)

    def forward_step(running, parts, row_begin):
        key_part, value_part = parts
        piece_len = key_part.shape[1]
        key_pos = positions_of(
            row_begin + jnp.arange(piece_len, dtype=jnp.int32), group_order, group_len
        )
        allowed = allowed_for(own_pos, own_ids, key_pos, piece_ids(key_pos, picture_starts))
        row_peak, row_total, summed = running
        key_heads = key_part.reshape(batch_size, piece_len, H, HD)
        value_heads = value_part.reshape(batch_size, piece_len, H, HD)
        scores = (
            jnp.einsum("bqhd,bkhd->bhqk", queries, key_heads, preferred_element_type=f32)
            * score_scale
        )
        masked = jnp.where(allowed, scores, masked_score)
        new_peak = jnp.maximum(row_peak, jnp.max(masked, axis=-1))
        row_fade = jnp.exp(row_peak - new_peak)
        weights = jnp.where(allowed, jnp.exp(masked - new_peak[..., None]), 0.0)
        row_total = row_total * row_fade + jnp.sum(weights, axis=-1)
        summed = summed * row_fade[..., None] + jnp.einsum(
            "bhqk,bkhd->bhqd", weights.astype(bf16), value_heads, preferred_element_type=f32
        )
        return (new_peak, row_total, summed)

    start_attn = (
        jnp.full((batch_size, H, group_len), masked_score, f32),
        jnp.zeros((batch_size, H, group_len), f32),
        jnp.zeros((batch_size, H, group_len, HD), f32),
    )
    row_peak, row_total, summed = blocked(
        start_attn,
        (
            lax.all_gather(key_flat, "ctx", axis=1, tiled=True),
            lax.all_gather(value_flat, "ctx", axis=1, tiled=True),
        ),
        group_len,
        forward_step,
    )
    log_total = row_peak + jnp.log(row_total)
    attended = (summed / row_total[..., None]).transpose(0, 2, 1, 3)
    attended_low = attended.reshape(token_rows, model_dim).astype(bf16)
    head_max = lax.pmax(jnp.max(row_peak, axis=(0, 2)), ("dp", "ctx"))
    act_low = exact_gelu(up_pre).astype(bf16)
    proj_piece = lax.all_gather(proj_weight, ("dp", "ctx"), axis=0, tiled=True)
    down_piece = lax.all_gather(down_rows, ("dp", "ctx"), axis=0, tiled=True)
    piece_len = proj_piece.shape[0]
    mix_sum = jnp.dot(attended_low, proj_piece, preferred_element_type=f32)
    mix_sum = mix_sum + jnp.dot(
        act_low, down_piece.reshape(piece_len * ff_ratio, model_dim), preferred_element_type=f32
    )
    block_out = (
        (hidden + mix_sum + bias_table[:, 4] + bias_table[:, 5])
        .astype(bf16)
        .reshape(batch_size, group_len, model_dim)
    )
    grad_y = out_cotangent.reshape(token_rows, model_dim)
    grad_yf = grad_y.astype(f32)
    proj_piece = lax.all_gather(proj_weight, ("dp", "ctx"), axis=0, tiled=True)
    down_piece = lax.all_gather(down_rows, ("dp", "ctx"), axis=0, tiled=True)
    piece_len = proj_piece.shape[0]
    attn_part = jnp.einsum("rd,nd->rn", grad_y, proj_piece, preferred_element_type=f32)
    act_part = jnp.einsum(
        "rd,md->rm",
        grad_y,
        down_piece.reshape(piece_len * ff_ratio, model_dim),
        preferred_element_type=f32,
    )
    grad_attn = attn_part
    grad_act = act_part
    grad_attn, grad_act = (grad_attn, grad_act)
    _, gelu_back = jax.vjp(exact_gelu, up_pre)
    grad_up = gelu_back(grad_act)[0].astype(bf16)
    grad_attended = grad_attn.astype(bf16)
    out_sum = jnp.sum(grad_yf, axis=0)
    out_width = model_dim + ff_ratio * model_dim + 1
    grad_heads = grad_attended.reshape(batch_size, group_len, H, HD)
    row_dot = jnp.sum(grad_heads.astype(f32) * attended, axis=-1).transpose(0, 2, 1)

    def query_step(running, parts, row_begin):
        key_part, value_part = parts
        piece_len = key_part.shape[1]
        key_pos = positions_of(
            row_begin + jnp.arange(piece_len, dtype=jnp.int32), group_order, group_len
        )
        allowed = allowed_for(own_pos, own_ids, key_pos, piece_ids(key_pos, picture_starts))
        key_heads = key_part.reshape(batch_size, piece_len, H, HD)
        value_heads = value_part.reshape(batch_size, piece_len, H, HD)
        scores = (
            jnp.einsum("bqhd,bkhd->bhqk", queries, key_heads, preferred_element_type=f32)
            * score_scale
        )
        masked = jnp.where(allowed, scores, masked_score)
        prob_rows = jnp.where(allowed, jnp.exp(masked - log_total[..., None]), 0.0)
        grad_prob = jnp.einsum(
            "bqhd,bkhd->bhqk", grad_heads, value_heads, preferred_element_type=f32
        )
        grad_scores = (prob_rows * (grad_prob - row_dot[..., None])).astype(bf16)
        return running + jnp.einsum(
            "bhqk,bkhd->bhqd", grad_scores, key_heads, preferred_element_type=f32
        )

    grad_query = (
        blocked(
            jnp.zeros((batch_size, H, group_len, HD), f32),
            (
                lax.all_gather(key_flat, "ctx", axis=1, tiled=True),
                lax.all_gather(value_flat, "ctx", axis=1, tiled=True),
            ),
            group_len,
            query_step,
        )
        * score_scale
    )
    log_total_all, row_dot_all = (
        lax.all_gather(log_total, "ctx", axis=2, tiled=True),
        lax.all_gather(row_dot, "ctx", axis=2, tiled=True),
    )

    def key_step(running, parts, row_begin):
        query_part, grad_part = parts
        piece_len = query_part.shape[1]
        query_pos = positions_of(
            row_begin + jnp.arange(piece_len, dtype=jnp.int32), group_order, group_len
        )
        allowed = allowed_for(query_pos, piece_ids(query_pos, picture_starts), own_pos, own_ids)
        total_part = lax.dynamic_slice_in_dim(log_total_all, row_begin, piece_len, 2)
        dot_part = lax.dynamic_slice_in_dim(row_dot_all, row_begin, piece_len, 2)
        grad_key, grad_value = running
        query_heads = query_part.reshape(batch_size, piece_len, H, HD)
        grad_piece = grad_part.reshape(batch_size, piece_len, H, HD)
        scores = (
            jnp.einsum("bqhd,bkhd->bhqk", query_heads, key_rows, preferred_element_type=f32)
            * score_scale
        )
        masked = jnp.where(allowed, scores, masked_score)
        prob_rows = jnp.where(allowed, jnp.exp(masked - total_part[..., None]), 0.0)
        grad_value = grad_value + jnp.einsum(
            "bhqk,bqhd->bhkd", prob_rows.astype(bf16), grad_piece, preferred_element_type=f32
        )
        grad_prob = jnp.einsum(
            "bqhd,bkhd->bhqk", grad_piece, value_rows, preferred_element_type=f32
        )
        grad_scores = (prob_rows * (grad_prob - dot_part[..., None])).astype(bf16)
        grad_key = grad_key + jnp.einsum(
            "bhqk,bqhd->bhkd", grad_scores, query_heads, preferred_element_type=f32
        )
        return (grad_key, grad_value)

    start_keys = (
        jnp.zeros((batch_size, H, group_len, HD), f32),
        jnp.zeros((batch_size, H, group_len, HD), f32),
    )
    grad_key, grad_value = blocked(
        start_keys,
        (
            lax.all_gather(query_flat, "ctx", axis=1, tiled=True),
            lax.all_gather(
                grad_attended.reshape(batch_size, group_len, model_dim), "ctx", axis=1, tiled=True
            ),
        ),
        group_len,
        key_step,
    )
    grad_key = grad_key * score_scale
    grad_q_back = rotate(grad_query.transpose(0, 2, 1, 3), own_pos, -1.0)
    grad_k_back = rotate(grad_key.transpose(0, 2, 1, 3), own_pos, -1.0)
    grad_v_back = grad_value.transpose(0, 2, 1, 3)
    grad_qkv = (
        jnp.stack([grad_q_back, grad_k_back, grad_v_back], axis=2)
        .reshape(token_rows, 3 * model_dim)
        .astype(bf16)
    )
    qkv_piece = lax.all_gather(qkv_weight, ("dp", "ctx"), axis=0, tiled=True)
    up_piece = lax.all_gather(up_weight, ("dp", "ctx"), axis=0, tiled=True)
    attn_part = jnp.einsum("re,ne->rn", grad_qkv, qkv_piece, preferred_element_type=f32)
    mlp_part = jnp.einsum("rf,nf->rn", grad_up, up_piece, preferred_element_type=f32)
    grad_norm_attn = attn_part
    grad_norm_mlp = mlp_part
    grad_norm_attn, grad_norm_mlp = (grad_norm_attn, grad_norm_mlp)
    gain_table = bias_table[:, 0:4]
    grad_norm = grad_norm_attn * gain_table[:, 0] + grad_norm_mlp * gain_table[:, 2]
    grad_hidden_f = grad_yf + inv_std * (
        grad_norm
        - jnp.mean(grad_norm, axis=1, keepdims=True)
        - normed * jnp.mean(grad_norm * normed, axis=1, keepdims=True)
    )
    grad_hidden = grad_hidden_f.astype(bf16).reshape(batch_size, group_len, model_dim)
    gain_grads = jnp.stack(
        [
            jnp.sum(grad_norm_attn * normed, axis=0),
            jnp.sum(grad_norm_attn, axis=0),
            jnp.sum(grad_norm_mlp * normed, axis=0),
            jnp.sum(grad_norm_mlp, axis=0),
        ],
        axis=1,
    )
    in_small = jnp.concatenate(
        [
            jnp.sum(grad_qkv.astype(f32), axis=0).reshape(model_dim, 3),
            jnp.sum(grad_up.astype(f32), axis=0).reshape(model_dim, ff_ratio),
            gain_grads,
        ],
        axis=1,
    )
    proj_part = jnp.einsum("rn,rd->nd", attended_low, grad_y, preferred_element_type=f32)
    down_part = jnp.einsum("rm,rd->md", act_low, grad_y, preferred_element_type=f32).reshape(
        model_dim, ff_ratio * model_dim
    )
    qkv_part = jnp.einsum("rn,re->ne", norm_attn, grad_qkv, preferred_element_type=f32)
    up_part = jnp.einsum("rn,rf->nf", norm_mlp, grad_up, preferred_element_type=f32)
    every_rows = lax.psum_scatter(
        jnp.concatenate(
            [
                jnp.concatenate([proj_part, down_part, out_sum[:, None]], axis=1),
                jnp.concatenate([qkv_part, up_part, in_small], axis=1),
            ],
            axis=1,
        ),
        ("dp", "ctx"),
        scatter_dimension=0,
        tiled=True,
    )
    out_rows = every_rows[:, :out_width]
    in_rows = every_rows[:, out_width:]
    grad_proj_weight = out_rows[:, :model_dim]
    grad_down_weight = out_rows[:, model_dim : model_dim + ff_ratio * model_dim].reshape(
        shard_rows * ff_ratio, model_dim
    )
    grad_bias_out = out_rows[:, out_width - 1]
    qkv_width = 3 * model_dim
    grad_qkv_weight = in_rows[:, :qkv_width]
    grad_up_weight = in_rows[:, qkv_width : qkv_width + ff_dim]
    tail_cols = in_rows[:, qkv_width + ff_dim :]
    grad_qkv_bias = tail_cols[:, :3].reshape(-1)
    grad_up_bias = tail_cols[:, 3 : 3 + ff_ratio].reshape(-1)
    gain_rows = tail_cols[:, 3 + ff_ratio :]
    clip_ratio = jnp.sqrt(clip_bound / jnp.maximum(head_max, clip_bound))
    head_cols = jnp.repeat(clip_ratio, HD)
    factor = jnp.concatenate([head_cols, head_cols, jnp.ones((model_dim,), f32)])
    clipped_qkv = qkv_weight.astype(f32) * factor[None, :]
    return (
        block_out,
        grad_hidden,
        gain_rows[:, 0],
        gain_rows[:, 1],
        grad_qkv_weight,
        grad_qkv_bias,
        grad_proj_weight,
        grad_bias_out,
        gain_rows[:, 2],
        gain_rows[:, 3],
        grad_up_weight,
        grad_up_bias,
        grad_down_weight,
        grad_bias_out,
        clipped_qkv,
    )


MESH = pl.DeviceIdType.MESH
NT = (((1,), (1,)), ((), ()))
f32 = jnp.float32
bf16 = jnp.bfloat16
CH = 8
NC = 16
SL = 1024
TOK = 2048
D = 1024


def dot(a, b):
    return jnp.dot(a, b, preferred_element_type=f32)


def dot_nt(a, b):
    return lax.dot_general(a, b, NT, preferred_element_type=f32)


def block_kernel(
    go_ref, ps_ref, x_ref, dy_ref, qw_ref, uw_ref, pw_ref, dw_ref,
    ag_ref, as_ref, mg_ref, ms_ref, pb_ref, db_ref, qb_ref, ub_ref,
    bo_ref, gh_ref, gra_ref, grb_ref, gp_ref, sr_ref, ds_ref,
    QW, UW, V0, V1, V2, V3, V4, V5, V6, V7, WS,
    X, Y, NA, NM, WC, WPD, CT, ST, PK, LIM, SM, BV,
    Q, K, V, VT, KT, PT, ATT, AA, GP, DA, GG, DQ, DK, DV, HM, GN,
    TT, GA, GB, GYA, GYB, PDS, SROW, DSUM,
    TMP, LP, SB, RSB, SR, RR,
    in_s, w_s, w_r, wy_s, wy_r, pd_s, pd_r, ga_s, ga_r, rs_s, rs_r,
    gy_s, gy_r, gg_s, gg_r, gpd_s, gpd_r, sm_s, sm_r, dm_s, dm_r,
):
    d = lax.axis_index("dp")
    c = lax.axis_index("ctx")
    k = c // 2
    j = c % 2
    z = k // 2
    r = z + (k % 2) * (7 - 2 * z)
    head = 8 * j + k

    def ctx_of(pos, core):
        p = (pos + 16) % 8
        return 2 * (2 * p + (p // 4) * (15 - 4 * p)) + core

    right = (d, ctx_of(r + 1, j))
    left = (d, ctx_of(r - 1, j))
    sibling = (d, 2 * k + (1 - j))
    partner = (1 - d, c)

    def rcopy(src, dst, ss, rs, dev):
        return pltpu.make_async_remote_copy(
            src_ref=src, dst_ref=dst, send_sem=ss, recv_sem=rs,
            device_id=dev, device_id_type=MESH,
        )

    barrier = pltpu.get_barrier_semaphore()

    def hello(o, _):
        lin = (d * NC + c + o) % 32
        pl.semaphore_signal(barrier, inc=1, device_id=(lin // NC, lin % NC), device_id_type=MESH)
        return 0

    lax.fori_loop(1, 32, hello, 0)

    def own_rows(s):
        return pl.ds(pl.multiple_of(s * SL + 64 * c, 64), 64)

    vecs = (V0, V1, V2, V3, V4, V5, V6, V7)
    fetch = [pltpu.make_async_copy(qw_ref, QW, in_s.at[0]), pltpu.make_async_copy(uw_ref, UW, in_s.at[1])]
    for i, ref in enumerate((ag_ref, as_ref, mg_ref, ms_ref, pb_ref, db_ref)):
        fetch.append(pltpu.make_async_copy(ref, vecs[i], in_s.at[2 + i]))
    fetch.append(pltpu.make_async_copy(qb_ref, vecs[6], in_s.at[8]))
    fetch.append(pltpu.make_async_copy(ub_ref, vecs[7], in_s.at[9]))
    fetch_x = [pltpu.make_async_copy(x_ref.at[s], X.at[own_rows(s)], in_s.at[10 + s]) for s in range(2)]
    fetch_y = [pltpu.make_async_copy(dy_ref.at[s], Y.at[own_rows(s)], in_s.at[12 + s]) for s in range(2)]
    for cp in fetch + fetch_x + fetch_y:
        cp.start()
    pl.semaphore_wait(barrier, 31)

    class Gather:
        def __init__(self, buf, own, s, i):
            self.buf, self.own, self.s, self.i = buf, own, s, i

        def at(self, delta, core):
            row = self.s * SL + 64 * ctx_of(r + delta, core)
            return self.buf.at[pl.ds(pl.multiple_of(row, 64), 64)]

        def ring(self, t, way, back=0):
            region = self.at((t + back) * (2 * way - 1), j)
            slot = 4 * way + t
            return rcopy(region, region, ga_s.at[self.i, slot], ga_r.at[self.i, slot],
                         left if way else right)

        def steps(self, way):
            return 4 if way == self.s else 3

        def sib(self, slot, core):
            delta = (0, -1, -2, -3, 1, 2, 3, 4)[slot]
            region = self.at(delta, core)
            return rcopy(region, region, ga_s.at[self.i, 8 + slot], ga_r.at[self.i, 8 + slot], sibling)

        def start(self):
            self.own[self.s].wait()
            self.ring(0, 0).start()
            self.ring(0, 1).start()
            self.sib(0, j).start()

        def pump(self, t):
            for way in (0, 1):
                if t <= self.steps(way):
                    self.ring(t - 1, way, 1).wait_recv()
                    if t < self.steps(way):
                        self.ring(t, way).start()
                    self.sib(7 if t == 4 else t + 3 * way, j).start()

        def ready(self, t):
            for slot in ((0,) if t == 0 else (t, 3 + t) if t < 4 else (7,)):
                self.sib(slot, 1 - j).wait_recv()

        def drain(self):
            for way in (0, 1):
                for t in range(self.steps(way)):
                    self.ring(t, way).wait_send()
            for slot in range(8):
                self.sib(slot, j).wait_send()

    gx = [Gather(X, fetch_x, s, s) for s in range(2)]
    gd = [Gather(Y, fetch_y, s, 2 + s) for s in range(2)]
    gx[0].start()
    for cp in fetch:
        cp.wait()

    def lane(shape):
        return lax.broadcasted_iota(jnp.int32, shape, len(shape) - 1)

    TMP[:, 0:128] = jnp.zeros((128, 128), f32)
    for i in range(6):
        TMP[64 + i:65 + i, 0:32] = vecs[i][...].astype(f32)
    TMP[0:1, 0:96] = V6[...].astype(f32)
    vq, vu = TMP[0:1, 0:128], V7[...].astype(f32)
    for i in range(3):
        TMP[70 + i:71 + i, 0:128] = pltpu.roll(vq, (128 - 32 * i) % 128, 1)
    for i in range(4):
        TMP[73 + i:74 + i, 0:128] = pltpu.roll(vu, (128 - 32 * i) % 128, 1)
    vcols = TMP[:, 0:128].T[0:32, :]
    low32 = lane((32, 128)) < 64
    for hp in range(H // 2):
        q2 = QW[:, 128 * hp:128 * hp + 128].astype(f32)
        k2 = QW[:, D + 128 * hp:D + 128 * hp + 128].astype(f32)
        v2 = QW[:, 2 * D + 128 * hp:2 * D + 128 * hp + 128].astype(f32)
        WS[2 * hp, :, 0:128] = jnp.where(low32, q2, pltpu.roll(k2, 64, 1)).astype(bf16)
        WS[2 * hp + 1, :, 0:128] = jnp.where(low32, pltpu.roll(q2, 64, 1), k2).astype(bf16)
        WS[2 * hp, :, 128:256] = jnp.where(low32, v2, vcols).astype(bf16)
        WS[2 * hp + 1, :, 128:256] = jnp.where(low32, pltpu.roll(v2, 64, 1), vcols).astype(bf16)
    for h in range(H):
        WS[h, :, 256:512] = UW[:, 256 * h:256 * h + 256]

    def w_copy(o, dst_c, row):
        return rcopy(
            WS.at[8 * (dst_c % 2) + dst_c // 2],
            WC.at[pl.ds(pl.multiple_of(row, 32), 32)],
            w_s.at[o], w_r.at[o], (d, dst_c),
        )

    own_row = 32 * (NC * d + c)

    def w_send(o, _):
        w_copy(o, (c + o) % NC, own_row).start()
        return 0

    lax.fori_loop(1, NC, w_send, 0)
    WC[pl.ds(pl.multiple_of(own_row, 32), 32), :] = WS[head]

    def wy_copy(o, plane):
        row = 32 * (NC * plane + (c - o + NC) % NC)
        region = WC.at[pl.ds(pl.multiple_of(row, 32), 32)]
        return rcopy(region, region, wy_s.at[o], wy_r.at[o], partner)

    wy_copy(0, d).start()
    gx[1].start()

    def pd_copies(jj, dst_dp):
        dev = (dst_dp, 2 * k + d)
        return (
            rcopy(pw_ref, WPD.at[pl.ds(256 + 32 * jj, 32)], pd_s.at[dst_dp, 0], pd_r.at[jj, 0], dev),
            rcopy(dw_ref, WPD.at[pl.ds(128 * jj, 128)], pd_s.at[dst_dp, 1], pd_r.at[jj, 1], dev),
        )

    here = d == j

    def pd_start():
        for e in range(2):
            @pl.when(jnp.logical_not(here & (d == e)))
            def _():
                for cp in pd_copies(j, e):
                    cp.start()

    local_pd = (
        pltpu.make_async_copy(pw_ref, WPD.at[pl.ds(256 + 32 * j, 32)], in_s.at[14]),
        pltpu.make_async_copy(dw_ref, WPD.at[pl.ds(128 * j, 128)], in_s.at[15]),
    )

    @pl.when(here)
    def _():
        for cp in local_pd:
            cp.start()
    WPD[320:384, :] = jnp.zeros((64, D), bf16)

    rows_i = lax.broadcasted_iota(jnp.int32, (SL, 128), 0)
    place = jnp.zeros((SL, 128), jnp.int32)
    cols_i = lane((8, SL))
    place_row = jnp.zeros((8, SL), jnp.int32)
    for b in range(NC):
        gob = go_ref[b]
        place = jnp.where((rows_i >> 6) == b, gob, place)
        place_row = jnp.where((cols_i >> 6) == b, gob, place_row)
    place = place * 64 + (rows_i & 63)
    place_row = place_row * 64 + (cols_i & 63)
    PK[...] = place
    for s in range(2):
        lim = place_row
        for p in range(PICS):
            st = ps_ref[s, p]
            lim = jnp.where((place_row >= st) & (place_row < st + PIC), st + (PIC - 1), lim)
        LIM[s] = lim

    def make_table(i, _):
        rows = pl.ds(pl.multiple_of(i * 128, 128), 128)
        ln = lane((128, 128))
        l64 = ln & 63
        freq = jnp.zeros((128, 128), f32)
        for q in range(ROT // 2):
            freq = jnp.where((l64 & 7) == q, float(rotary_base ** (-2.0 * q / ROT)), freq)
        ang = PK[rows, :].astype(f32) * freq
        CT[rows, :] = jnp.where(l64 < ROT, jnp.cos(ang), 1.0)
        sn = jnp.sin(ang)
        ST[rows, :] = jnp.where(l64 < ROT // 2, -sn, jnp.where(l64 < ROT, sn, 0.0))
        return 0

    lax.fori_loop(0, SL // 128, make_table, 0)

    half = pl.ds(pl.multiple_of(512 * d, 512), 512)
    other = pl.ds(pl.multiple_of(512 * (1 - d), 512), 512)

    def w_wait(o, _):
        src_c = (c - o + NC) % NC
        w_copy(o, (c + o) % NC, 32 * (NC * d + src_c)).wait_recv()
        wy_copy(o, d).start()
        return 0

    lax.fori_loop(1, NC, w_wait, 0)
    pd_start()
    gx[0].pump(1)

    def wy_wait(o, _):
        wy_copy(o, 1 - d).wait_recv()
        return 0

    lax.fori_loop(0, NC, wy_wait, 0)

    SM[...] = WC[:, 128:256].astype(f32).T[64:80, :]
    en = lane((16, 256))
    vrow = lax.broadcasted_iota(jnp.int32, (16, 256), 0)
    feat = lax.broadcasted_iota(jnp.int32, (D, 256), 0)
    jl = lane((D, 256))
    smb = SM[...].astype(bf16)

    def pick(e_big, e_small, div, first):
        onehot = jnp.where(feat == div(e_big)[0], 1.0, 0.0).astype(bf16)
        got = dot(smb, onehot)
        return jnp.sum(jnp.where(vrow == first + div(e_small)[1], got, 0.0), axis=0, keepdims=True)

    def place_qkv(e):
        owner = ((e >> 5) * 171) >> 9
        return 32 * owner + (e & 31), (e >> 5) - 3 * owner

    def place_up(e):
        return 32 * (e >> 7) + (e & 31), (e >> 5) & 3

    def e_qkv(ln):
        return SL * (ln >> 6) + HD * head + (ln & 63)

    bq = pick(e_qkv(jl), e_qkv(en), place_qkv, 6)
    bq = jnp.where(lane((1, 256)) < 192, bq, 0.0)
    bu = pick(256 * head + jl, 256 * head + en, place_up, 9)
    BV[0] = jnp.broadcast_to(bq, (8, 256))
    BV[1] = jnp.broadcast_to(bu, (8, 256))

    def turn(v, cs, sn, sign):
        l64 = lane(v.shape) & 63
        mate = jnp.where(l64 < ROT // 2, pltpu.roll(v, 120, 1), pltpu.roll(v, 8, 1))
        return v * cs + sign * (mate * sn)

    def normed_of(rows_value):
        x = rows_value.astype(f32)
        cen = x - jnp.mean(x, axis=1, keepdims=True)
        inv = lax.rsqrt(jnp.mean(cen * cen, axis=1, keepdims=True) + norm_eps)
        return cen * inv, inv

    def chip_rows(s, deltas):
        return [pl.ds(pl.multiple_of(s * SL + 64 * ctx_of(r + e, 0), 128), 128) for e in deltas]

    def load(ref, rows, lo=0, hi=None):
        parts = [ref[x, lo:hi] for x in rows]
        return parts[0] if len(parts) == 1 else jnp.concatenate(parts, axis=0)

    def store(ref, rows, value, lo=0, hi=None):
        for i, x in enumerate(rows):
            ref[x, lo:hi] = value[128 * i:128 * i + 128]

    def n_stage(s, deltas):
        rows, trow = chip_rows(s, deltas), chip_rows(0, deltas)
        low = lane((128 * len(rows), 128)) < 64
        nrm, _ = normed_of(load(X, rows))
        na = (nrm * SM[0:1, :] + SM[1:2, :]).astype(bf16)
        nm = (nrm * SM[2:3, :] + SM[3:4, :]).astype(bf16)
        store(NA, rows, na)
        store(NM, rows, nm)
        qkv = dot(na, WC[:, 0:256]) + BV[0, 0:1, :]
        up = dot(nm, WC[:, 256:512]) + BV[1, 0:1, :]
        rot = turn(qkv[:, 0:128], load(CT, trow), load(ST, trow), 1.0)
        store(Q, rows, jnp.where(low, rot * 0.125, 0.0).astype(bf16))
        store(K, rows, jnp.where(low, pltpu.roll(rot, 64, 1), 0.0).astype(bf16))
        store(V, rows, jnp.where(low, qkv[:, 128:256], 0.0).astype(bf16))
        cdf = 0.5 * (1.0 + lax.erf(up * (2.0 ** -0.5)))
        store(AA, rows, (up * cdf).astype(bf16), 0, 256)
        store(GP, rows, cdf + up * (jnp.exp(-0.5 * up * up) * ((2.0 * math.pi) ** -0.5)))

    def n_blocks(s, t):
        gx[s].ready(t)
        n_stage(s, (t,) if t in (0, 4) else (t, -t))

    def dy_blocks(s, t):
        if t == 0:
            gd[s].ready(4)
        gd[s].ready(t)
        dy_stage(s, (0, 4) if t == 0 else (t, -t))

    def turn_kv(s):
        VT[s] = V[s * SL:s * SL + SL, :].astype(f32).T[0:64, :].astype(bf16)
        KT[s] = K[s * SL:s * SL + SL, :].astype(f32).T[0:64, :].astype(bf16)

    HM[...] = jnp.full((8, 256), masked_score, f32)

    def fwd(i, _):
        s = i // 4
        q0 = pl.multiple_of((i % 4) * 256, 256)
        rows = pl.ds(pl.multiple_of(i * 256, 256), 256)
        seq = pl.ds(pl.multiple_of(s * SL, SL), SL)
        st = dot_nt(K[seq, :], Q[rows, :])
        pk = PK[...]
        lim = LIM[s, 0:1, pl.ds(q0, 256)]
        masked = jnp.where(jnp.concatenate([pk, pk], axis=1) <= lim, st, masked_score)
        peak = jnp.max(masked, axis=0, keepdims=True)
        p = jnp.exp(masked - peak)
        tot = jnp.sum(p, axis=0, keepdims=True)
        pt = (p * (1.0 / tot)).astype(bf16)
        PT[i] = pt
        at = dot(VT[s], pt)
        ATT[i] = at
        AA[rows, 256:384] = jnp.concatenate([at, jnp.zeros((64, 256), f32)], axis=0).T.astype(bf16)
        HM[...] = jnp.maximum(HM[...], jnp.broadcast_to(peak, (8, 256)))
        return 0

    class Scatter:
        def __init__(self, i, s, group, partial):
            self.i, self.s, self.g, self.partial = i, s, group, partial

        def sib(self, slot):
            return rcopy(SB.at[self.g, slot], SR.at[self.i, slot],
                         rs_s.at[self.i, 8 + slot], rs_r.at[self.i, 8 + slot], sibling)

        def produce(self, p):
            value = self.partial(self.s, (4, 0) if p == 0 else (4 - p, p - 4))
            for i, slot in enumerate((0, 7) if p == 0 else (2 * p - 1, 2 * p)):
                TMP[...] = value[128 * i:128 * i + 128]
                LP[self.g, slot] = TMP[pl.ds(pl.multiple_of(64 * j, 64), 64), :]
                SB[self.g, slot] = TMP[pl.ds(pl.multiple_of(64 * (1 - j), 64), 64), :].astype(bf16)
                self.sib(slot).start()

        def lane_sum(self, slot):
            self.sib(slot).wait_recv()
            return LP[self.g, slot] + SR[self.i, slot].astype(f32)

        def ring(self, t, way):
            slot = 4 * way + t
            return rcopy(RSB.at[self.g, slot], RR.at[self.i, slot],
                         rs_s.at[self.i, slot], rs_r.at[self.i, slot], left if way else right)

        def pump(self, t):
            for way in (self.s,) if t == 0 else (0, 1):
                slot = 4 * way + t
                v = self.lane_sum(2 * t - 1 + way if t else 0)
                if t > 1 or (t == 1 and way == self.s):
                    self.ring(t - 1, way).wait_recv()
                    v = v + RR[self.i, slot - 1].astype(f32)
                RSB[self.g, slot] = v.astype(bf16)
                self.ring(t, way).start()

        def total(self):
            v = self.lane_sum(7)
            for way in (0, 1):
                self.ring(3, way).wait_recv()
                v = v + RR[self.i, 4 * way + 3].astype(f32)
            return v

        def drain(self):
            for slot in range(8):
                self.sib(slot).wait_send()
            for way in (0, 1):
                for t in range(0 if way == self.s else 1, 4):
                    self.ring(t, way).wait_send()

    def out_partial(s, deltas):
        return dot(load(AA, chip_rows(s, deltas)), WPD[...])

    out = [Scatter(s, s, s, out_partial) for s in range(2)]
    DSUM[d] = jnp.zeros((8, D), f32)

    def dy_stage(s, deltas):
        rows = chip_rows(s, deltas)
        dyb = load(Y, rows)
        back = dot_nt(dyb, WPD[...])
        store(GG, rows, (back[:, 0:256] * load(GP, rows)).astype(bf16), 256, 512)
        store(DA, rows, back[:, 256:384].astype(bf16))
        DSUM[d] += jnp.broadcast_to(jnp.sum(dyb.astype(f32), axis=0, keepdims=True), (8, D))

    def bwd(i, _):
        s = i // 4
        rows = pl.ds(pl.multiple_of(i * 256, 256), 256)
        seq = pl.ds(pl.multiple_of(s * SL, SL), SL)
        q0 = pl.ds(pl.multiple_of((i % 4) * 256, 256), 256)
        da = DA[rows, :]
        rd = jnp.sum(da.astype(f32).T[0:64, :] * ATT[i], axis=0, keepdims=True)
        dpt = dot_nt(V[seq, :], da)
        pt = PT[i]
        ds = (pt.astype(f32) * (dpt - rd)).astype(bf16)
        DV[...] += dot(pt, da)
        DK[...] += dot(ds, Q[rows, :])
        DQ[q0, :] = jnp.concatenate([dot(KT[s], ds), jnp.zeros((64, 256), f32)], axis=0).T * 0.125
        return 0

    def qkv_back(i, s):
        trow = pl.ds(pl.multiple_of(i * 128, 128), 128)
        rows = pl.ds(pl.multiple_of(s * SL + i * 128, 128), 128)
        both = DQ[trow, :] + pltpu.roll(DK[trow, :], 64, 1)
        GG[rows, 0:128] = turn(both, CT[trow, :], ST[trow, :], -1.0).astype(bf16)
        GG[rows, 128:256] = DV[trow, :].astype(bf16)
        return s

    GN[...] = jnp.zeros((8, D), f32)

    def g_partial(s, deltas):
        rows = chip_rows(s, deltas)
        nrm, _ = normed_of(load(X, rows))
        gna = dot_nt(load(GG, rows, 0, 256), WC[:, 0:256])
        gnm = dot_nt(load(GG, rows, 256, 512), WC[:, 256:512])
        GN[0:1, :] += jnp.sum(gna * nrm, axis=0, keepdims=True)
        GN[1:2, :] += jnp.sum(gna, axis=0, keepdims=True)
        GN[2:3, :] += jnp.sum(gnm * nrm, axis=0, keepdims=True)
        GN[3:4, :] += jnp.sum(gnm, axis=0, keepdims=True)
        return gna * SM[0:1, :] + gnm * SM[2:3, :]

    grad = [Scatter(2 + s, s, s, g_partial) for s in range(2)]

    def out_done(s):
        tot = out[s].total()
        bo_ref[s * 64:s * 64 + 64, :] = (
            X[own_rows(s), :].astype(f32) + tot + SM[4:5, :] + SM[5:6, :]
        ).astype(bf16)
        out[s].drain()

    def bwd_start():
        DV[...] = jnp.zeros((SL, 128), f32)
        DK[...] = jnp.zeros((SL, 128), f32)

    def transpose_gg(lo):
        def one(i, _):
            rows = pl.ds(pl.multiple_of(i * 256, 256), 256)
            TT[0:256, rows] = GG[rows, lo:lo + 256].T
            return 0
        lax.fori_loop(0, 8, one, 0)

    def qkv_grad(i, _):
        cols = pl.ds(pl.multiple_of(i * 256, 256), 256)
        a = dot(TT[0:256, :], NA[:, cols])
        a = jnp.concatenate([a[0:192], GN[:, cols], a[200:256]], axis=0)
        GA[cols, :] = a.T.astype(bf16)
        return 0

    def up_grad(i, _):
        cols = pl.ds(pl.multiple_of(i * 256, 256), 256)
        GB[cols, :] = dot(TT[0:256, :], NM[:, cols]).T.astype(bf16)
        return 0

    gya = rcopy(GA.at[other], GYA, gy_s.at[0], gy_r.at[0], partner)
    gyb = rcopy(GB.at[other], GYB, gy_s.at[1], gy_r.at[1], partner)

    def up_weights():
        transpose_gg(256)
        lax.fori_loop(0, 4, up_grad, 0)
        gyb.start()

    def qkv_weights():
        transpose_gg(0)
        lax.fori_loop(0, 4, qkv_grad, 0)
        gya.start()

    def transpose_aa(i, _):
        rows = pl.ds(pl.multiple_of(i * 256, 256), 256)
        TT[:, rows] = AA[rows, :].T
        return 0

    def pd_grad(i, _):
        cols = pl.ds(pl.multiple_of(i * 256, 256), 256)
        PDS[:, cols] = dot(TT[...], Y[:, cols]).astype(bf16)
        return 0

    def gpd_copies(jj, slot_dp):
        dev = (j, 2 * k + jj)
        return (
            rcopy(PDS.at[pl.ds(256 + 32 * jj, 32)], gp_ref.at[slot_dp, pl.ds(0, 32)],
                  gpd_s.at[jj, 0], gpd_r.at[slot_dp, 0], dev),
            rcopy(PDS.at[pl.ds(128 * jj, 128)], gp_ref.at[slot_dp, pl.ds(32, 128)],
                  gpd_s.at[jj, 1], gpd_r.at[slot_dp, 1], dev),
        )

    def pd_weights():
        lax.fori_loop(0, 8, transpose_aa, 0)
        lax.fori_loop(0, 4, pd_grad, 0)
        for jj in range(2):
            @pl.when(jnp.logical_not(here & (j == jj)))
            def _():
                for cp in gpd_copies(jj, d):
                    cp.start()

        @pl.when(here)
        def _():
            gp_ref[d, 0:32, :] = PDS[pl.ds(256 + 32 * j, 32), :]
            gp_ref[d, 32:160, :] = PDS[pl.ds(128 * j, 128), :]

    def g_copy(half_i, o, dst_c, slot):
        src, dst = ((GA, gra_ref), (GB, grb_ref))[half_i]
        return rcopy(src.at[pl.ds(pl.multiple_of(512 * d + 32 * dst_c, 32), 32)], dst.at[slot],
                     gg_s.at[half_i, o], gg_r.at[half_i, o], (d, dst_c))

    def weights_out(half_i):
        gy, G, GY, gr_ref = ((gya, GA, GYA, gra_ref), (gyb, GB, GYB, grb_ref))[half_i]
        gy.wait_recv()
        G[half, :] = (G[half, :].astype(f32) + GY[...].astype(f32)).astype(bf16)

        def g_send(o, _):
            g_copy(half_i, o, (c + o) % NC, head).start()
            return 0

        lax.fori_loop(1, NC, g_send, 0)
        gr_ref[head] = G[pl.ds(pl.multiple_of(512 * d + 32 * c, 32), 32), :]

    def pd_ready():
        for jj in range(2):
            @pl.when(jnp.logical_not(here & (j == jj)))
            def _():
                for cp in pd_copies(jj, 0):
                    cp.wait_recv()

        @pl.when(here)
        def _():
            for cp in local_pd:
                cp.wait()

    def fwd_tiles(lo, hi):
        lax.fori_loop(lo, hi, fwd, 0)

    def bwd_tiles(lo, hi):
        lax.fori_loop(lo, hi, bwd, 0)

    dm = rcopy(DSUM.at[d], DSUM.at[d], dm_s, dm_r, partner)

    me = NC * d + c

    def s_copy(o, slot):
        lin = (me + o) % 32
        return rcopy(SROW, sr_ref.at[slot], sm_s.at[o], sm_r.at[o], (lin // NC, lin % NC))

    def token_sums():
        srow = jnp.zeros((1, 512), f32)
        for i in range(TOK // 256):
            srow = srow + jnp.sum(GG[i * 256:i * 256 + 256, :].astype(f32), axis=0, keepdims=True)
        hmax = jnp.max(HM[...], axis=1, keepdims=True)[0:1, :]
        SROW[...] = jnp.where(lane((1, 512)) == 192, hmax, srow)
        sr_ref[me] = SROW[...]

        def s_send(o, _):
            s_copy(o, me).start()
            return 0

        lax.fori_loop(1, 32, s_send, 0)

    def grad_done(s):
        tot = grad[s].total()
        own = slice(s * 64, s * 64 + 64)
        nrm, inv = normed_of(X[own_rows(s), :])
        gh_ref[own, :] = (
            Y[own_rows(s), :].astype(f32)
            + inv * (tot - jnp.mean(tot, axis=1, keepdims=True)
                     - nrm * jnp.mean(tot * nrm, axis=1, keepdims=True))
        ).astype(bf16)

    gx[1].pump(1)
    gx[0].pump(2)
    gx[1].pump(2)
    n_blocks(0, 2)
    n_blocks(1, 1)
    gx[0].pump(3)
    gd[0].start()
    n_blocks(0, 0)
    gx[1].pump(3)
    n_blocks(0, 3)
    gd[1].start()
    n_blocks(0, 1)
    n_blocks(1, 3)
    gx[0].pump(4)
    n_blocks(1, 2)
    n_blocks(0, 4)
    gd[0].pump(1)
    n_blocks(1, 0)
    turn_kv(0)
    fwd_tiles(0, 2)
    gd[1].pump(1)
    fwd_tiles(2, 4)
    pd_ready()
    out[0].produce(0)
    out[0].produce(1)
    gx[1].pump(4)
    out[0].produce(2)
    gd[0].pump(2)
    n_blocks(1, 4)
    gd[1].pump(2)
    dy_blocks(0, 2)
    turn_kv(1)
    out[0].pump(0)
    out[0].produce(3)
    fwd_tiles(4, 6)
    gd[0].pump(3)
    fwd_tiles(6, 8)
    gd[1].pump(3)
    dy_blocks(1, 1)
    out[1].produce(0)
    out[1].pump(0)
    out[1].produce(1)
    out[0].pump(1)
    dy_blocks(0, 1)
    out[1].produce(2)
    dy_blocks(1, 2)
    gd[1].pump(4)
    dy_blocks(0, 3)
    dy_blocks(1, 0)
    gd[0].pump(4)
    dy_blocks(1, 3)
    dy_blocks(0, 0)
    out[1].pump(1)
    bwd_start()
    up_weights()
    out[0].pump(2)
    bwd_tiles(0, 2)
    out[1].pump(2)
    out[1].produce(3)
    bwd_tiles(2, 4)
    lax.fori_loop(0, 8, qkv_back, 0)
    out[0].pump(3)
    dm.start()
    bwd_start()
    bwd_tiles(4, 6)
    out[1].pump(3)
    bwd_tiles(6, 8)
    weights_out(1)
    lax.fori_loop(0, 8, qkv_back, 1)
    out_done(0)
    out_done(1)
    grad[1].produce(0)
    grad[0].produce(0)
    grad[1].pump(0)
    grad[0].produce(1)
    grad[0].pump(0)
    grad[1].produce(1)
    grad[0].produce(2)
    grad[0].produce(3)
    grad[1].pump(1)
    grad[0].pump(1)
    grad[1].produce(2)
    grad[1].pump(2)
    grad[1].produce(3)
    qkv_weights()
    grad[0].pump(2)
    grad[1].pump(3)
    pd_weights()
    grad[0].pump(3)
    weights_out(0)
    grad_done(0)
    token_sums()
    grad_done(1)

    for e in range(2):
        @pl.when(jnp.logical_not(here & (d == e)))
        def _():
            for cp in gpd_copies(0, e):
                cp.wait_recv()

    rcopy(DSUM.at[1 - d], DSUM.at[1 - d], dm_s, dm_r, partner).wait_recv()
    ds_ref[...] = DSUM[0] + DSUM[1]

    def g_wait(o, _):
        src_c = (c - o + NC) % NC
        for half_i in range(2):
            g_copy(half_i, o, (c + o) % NC, 8 * (src_c % 2) + src_c // 2).wait_recv()
        return 0

    lax.fori_loop(1, NC, g_wait, 0)

    def s_wait(o, _):
        s_copy(o, (me - o + 32) % 32).wait_recv()
        return 0

    lax.fori_loop(1, 32, s_wait, 0)

    def w_done(o, _):
        w_copy(o, (c + o) % NC, own_row).wait_send()
        for half_i in range(2):
            g_copy(half_i, o, (c + o) % NC, head).wait_send()
        wy_copy(o, d).wait_send()
        return 0

    lax.fori_loop(1, NC, w_done, 0)

    def s_done(o, _):
        s_copy(o, me).wait_send()
        return 0

    lax.fori_loop(1, 32, s_done, 0)
    wy_copy(0, d).wait_send()
    gya.wait_send()
    gyb.wait_send()
    dm.wait_send()
    for e in range(2):
        @pl.when(jnp.logical_not(here & (d == e)))
        def _():
            for cp in pd_copies(j, e):
                cp.wait_send()

        @pl.when(jnp.logical_not(here & (j == e)))
        def _():
            for cp in gpd_copies(e, d):
                cp.wait_send()
    for item in gx + gd + grad:
        item.drain()


def finish_kernel(
    bo, gh, gra, grb, gp, sr, ds, qw,
    o_bo, o_gh, o_ag, o_as, o_qw, o_qb, o_pw, o_pb, o_mg, o_ms, o_uw, o_ub, o_dw, o_db, o_cq,
    B, F,
):
    me = NC * lax.axis_index("dp") + lax.axis_index("ctx")
    for s in range(2):
        o_bo[s] = bo[64 * s:64 * s + 64, :]
        o_gh[s] = gh[64 * s:64 * s + 64, :]
    o_pw[...] = gp[0, 0:32, :].astype(f32) + gp[1, 0:32, :].astype(f32)
    o_dw[...] = gp[0, 32:160, :].astype(f32) + gp[1, 32:160, :].astype(f32)
    low = lax.broadcasted_iota(jnp.int32, (32, 128), 1) < 64
    low1 = low[0:1]
    gains = jnp.zeros((32, 128), f32)
    for h in range(H):
        at = 2 * (h % 8) + h // 8
        one, two = sr[at], sr[NC + at]
        both = one + two
        peak = jnp.maximum(one, two)
        col = lax.broadcasted_iota(jnp.int32, (1, 512), 1)
        B[h:h + 1, :] = jnp.where(col == 192, peak, both)
        F[32 + 2 * h:33 + 2 * h, :] = both[:, 256:384]
        F[33 + 2 * h:34 + 2 * h, :] = both[:, 384:512]
        gains = gains + gra[h, :, 128:256].astype(f32)
        o_uw[:, 256 * h:256 * h + 256] = grb[h].astype(f32)
    top = B[:, 128:256]
    top = jnp.max(jnp.where(lax.broadcasted_iota(jnp.int32, (H, 128), 1) == 64, top, masked_score), axis=1, keepdims=True)
    ratio = jnp.broadcast_to(jnp.sqrt(clip_bound / jnp.maximum(top, clip_bound)), (H, 128))
    F[24:32, :] = jnp.zeros((8, 128), f32)
    for hp in range(H // 2):
        a, b = gra[2 * hp, :, 0:128].astype(f32), gra[2 * hp + 1, :, 0:128].astype(f32)
        va, vb = gra[2 * hp, :, 128:256].astype(f32), gra[2 * hp + 1, :, 128:256].astype(f32)
        o_qw[:, 128 * hp:128 * hp + 128] = jnp.where(low, a, pltpu.roll(b, 64, 1))
        o_qw[:, D + 128 * hp:D + 128 * hp + 128] = jnp.where(low, pltpu.roll(a, 64, 1), b)
        o_qw[:, 2 * D + 128 * hp:2 * D + 128 * hp + 128] = jnp.where(low, va, pltpu.roll(vb, 64, 1))
        ra, rb = B[2 * hp:2 * hp + 1, 0:128], B[2 * hp + 1:2 * hp + 2, 0:128]
        sa, sb = B[2 * hp:2 * hp + 1, 128:256], B[2 * hp + 1:2 * hp + 2, 128:256]
        F[hp:hp + 1, :] = jnp.where(low1, ra, pltpu.roll(rb, 64, 1))
        F[8 + hp:9 + hp, :] = jnp.where(low1, pltpu.roll(ra, 64, 1), rb)
        F[16 + hp:17 + hp, :] = jnp.where(low1, sa, pltpu.roll(sb, 64, 1))
        fac = jnp.where(low1, ratio[2 * hp:2 * hp + 1], ratio[2 * hp + 1:2 * hp + 2])
        for part in range(3):
            cols = slice(part * D + 128 * hp, part * D + 128 * hp + 128)
            w = qw[:, cols].astype(f32)
            o_cq[:, cols] = w * fac if part < 2 else w
    grows = jnp.concatenate([gains, jnp.zeros((96, 128), f32)], axis=0).T
    for i, o in enumerate((o_ag, o_as, o_mg, o_ms)):
        o[...] = grows[64 + i:65 + i, 0:32]
    row, shift = (96 * me) // 128, (96 * me) % 128
    turned = pltpu.roll(F[pl.ds(row, 1), :], (128 - shift) % 128, 1)
    after = pltpu.roll(F[pl.ds(row + 1, 1), :], (128 - shift) % 128, 1)
    col = lax.broadcasted_iota(jnp.int32, (1, 128), 1)
    o_qb[...] = jnp.where(col < 128 - shift, turned, after)[:, 0:96]
    o_ub[...] = F[pl.ds(32 + me, 1), :]
    dsum = ds[0:1, pl.ds(pl.multiple_of(128 * (me // 4), 128), 128)]
    dsum = pltpu.roll(dsum, (128 - 32 * (me % 4)) % 128, 1)[:, 0:32]
    o_pb[...] = dsum
    o_db[...] = dsum


def fast_shards(
    hidden_in, out_cotangent, attn_gain, attn_shift, qkv_weight, qkv_bias, proj_weight, proj_bias,
    mlp_gain, mlp_shift, up_weight, up_bias, down_weight, down_bias, picture_starts, group_order,
):
    vm = pl.BlockSpec(memory_space=pltpu.VMEM)
    sm = pl.BlockSpec(memory_space=pltpu.SMEM)
    hbm = pl.BlockSpec(memory_space=pl.ANY)
    V_ = pltpu.VMEM
    dma = pltpu.SemaphoreType.DMA

    def sds(shape, dtype=f32):
        return jax.ShapeDtypeStruct(shape, dtype)

    got = pl.pallas_call(
        block_kernel,
        out_shape=(
            sds((128, D), bf16), sds((128, D), bf16), sds((NC, 32, 256), bf16), sds((NC, 32, 256), bf16),
            sds((2, 160, D), bf16), sds((32, 1, 512)), sds((8, D)),
        ),
        in_specs=[sm, sm] + [hbm] * 14,
        out_specs=(vm,) * 7,
        scratch_shapes=[
            V_((32, 3 * D), bf16), V_((32, 4 * D), bf16), *(V_((1, n), bf16) for n in (32,) * 6 + (96, 128)), V_((NC, 32, 512), bf16),
            V_((TOK, D), bf16), V_((TOK, D), bf16), V_((TOK, D), bf16), V_((TOK, D), bf16),
            V_((D, 512), bf16), V_((384, D), bf16),
            V_((SL, 128), f32), V_((SL, 128), f32), V_((SL, 128), jnp.int32),
            V_((2, 8, SL), jnp.int32), V_((16, D), f32), V_((2, 8, 256), f32),
            V_((TOK, 128), bf16), V_((TOK, 128), bf16), V_((TOK, 128), bf16),
            V_((2, 64, SL), bf16), V_((2, 64, SL), bf16),
            V_((8, SL, 256), bf16), V_((8, 64, 256), f32),
            V_((TOK, 384), bf16), V_((TOK, 256), f32), V_((TOK, 128), bf16), V_((TOK, 512), bf16),
            V_((SL, 128), f32), V_((SL, 128), f32), V_((SL, 128), f32),
            V_((8, 256), f32), V_((8, D), f32),
            V_((384, TOK), bf16), V_((D, 256), bf16), V_((D, 256), bf16),
            V_((512, 256), bf16), V_((512, 256), bf16),
            V_((384, D), bf16), V_((1, 512), f32), V_((2, 8, D), f32),
            V_((128, D), f32), V_((2, 8, 64, D), f32), V_((2, 8, 64, D), bf16),
            V_((2, 8, 64, D), bf16), V_((4, 8, 64, D), bf16), V_((4, 8, 64, D), bf16),
            dma((16,)), dma((NC,)), dma((NC,)), dma((NC,)), dma((NC,)), dma((2, 2)), dma((2, 2)),
            dma((4, 16)), dma((4, 16)), dma((4, 16)), dma((4, 16)),
            dma((2,)), dma((2,)), dma((2, NC)), dma((2, NC)), dma((2, 2)), dma((2, 2)), dma((32,)), dma((32,)), dma, dma,
        ],
        compiler_params=pltpu.CompilerParams(
            collective_id=0, has_side_effects=True, vmem_limit_bytes=63 * 1024 * 1024
        ),
    )(
        group_order, picture_starts, hidden_in, out_cotangent, qkv_weight, up_weight, proj_weight, down_weight,
        *(v.reshape(1, -1) for v in (
            attn_gain, attn_shift, mlp_gain, mlp_shift, proj_bias, down_bias, qkv_bias, up_bias)),
    )
    r32 = sds((1, 32))
    outs = pl.pallas_call(
        finish_kernel,
        out_shape=(
            sds((2, 64, D), bf16), sds((2, 64, D), bf16), r32, r32, sds((32, 3 * D)), sds((1, 96)),
            sds((32, D)), r32, r32, r32, sds((32, 4 * D)), sds((1, 128)), sds((128, D)), r32, sds((32, 3 * D)),
        ),
        in_specs=[vm] * 8,
        out_specs=(vm,) * 15,
        scratch_shapes=[V_((H, 512), f32), V_((64, 128), f32)],
    )(*got, qkv_weight)
    return tuple(o.reshape(-1) if o.shape[0] == 1 else o for o in outs)


def solution(mesh):
    in_specs = (
        P("dp", "ctx", None),
        P("dp", "ctx", None),
        P(("dp", "ctx")),
        P(("dp", "ctx")),
        P(("dp", "ctx"), None),
        P(("dp", "ctx")),
        P(("dp", "ctx"), None),
        P(("dp", "ctx")),
        P(("dp", "ctx")),
        P(("dp", "ctx")),
        P(("dp", "ctx"), None),
        P(("dp", "ctx")),
        P(("dp", "ctx"), None),
        P(("dp", "ctx")),
        P("dp", None),
        P(),
    )
    out_specs = (
        P("dp", "ctx", None),
        P("dp", "ctx", None),
        P(("dp", "ctx")),
        P(("dp", "ctx")),
        P(("dp", "ctx"), None),
        P(("dp", "ctx")),
        P(("dp", "ctx"), None),
        P(("dp", "ctx")),
        P(("dp", "ctx")),
        P(("dp", "ctx")),
        P(("dp", "ctx"), None),
        P(("dp", "ctx")),
        P(("dp", "ctx"), None),
        P(("dp", "ctx")),
        P(("dp", "ctx"), None),
    )
    body = fast_shards if (mesh.shape["dp"], mesh.shape["ctx"]) == (2, H) else shards
    return jax.shard_map(body, mesh=mesh, in_specs=in_specs, out_specs=out_specs, check_vma=False)
```

```python
import math

import jax
import jax.numpy as jnp
from jax import lax
from jax.experimental import pallas as pl
from jax.experimental.pallas import tpu as pltpu
from jax.sharding import PartitionSpec as P

H = 16
HD = 64
ROT = 16
PIC = 256
PICS = 4


norm_eps = 1e-05
clip_bound = 8.0
rotary_base = 10000.0
masked_score = -1e30


def exact_gelu(values):
    return jax.nn.gelu(values, approximate=False)


def rotate(values, positions, turn_sign):
    half_rot = ROT // 2
    inv_freq = rotary_base ** (-2.0 * jnp.arange(half_rot, dtype=jnp.float32) / ROT)
    angles = positions.astype(jnp.float32)[:, None] * inv_freq[None, :]
    cosine = jnp.cos(angles)[None, :, None, :]
    sine_part = turn_sign * jnp.sin(angles)[None, :, None, :]
    lead_half = values[..., :half_rot]
    tail_half = values[..., half_rot:ROT]
    return jnp.concatenate(
        [
            lead_half * cosine - tail_half * sine_part,
            tail_half * cosine + lead_half * sine_part,
            values[..., ROT:],
        ],
        axis=-1,
    )


def positions_of(row_numbers, group_order, group_len):
    group_ids = row_numbers // group_len
    owners = jnp.arange(group_order.shape[0], dtype=jnp.int32)
    placed = jnp.sum(
        jnp.where(group_ids[:, None] == owners[None, :], group_order[None, :], 0), axis=1
    )
    return placed * group_len + row_numbers % group_len


def piece_ids(positions, picture_starts):
    inside = (positions[None, None, :] >= picture_starts[:, :, None]) & (
        positions[None, None, :] < picture_starts[:, :, None] + PIC
    )
    labels = jnp.arange(1, PICS + 1, dtype=jnp.int32)[None, :, None]
    return jnp.sum(jnp.where(inside, labels, 0), axis=1)


def allowed_for(query_pos, query_ids, key_pos, key_ids):
    causal = key_pos[None, None, :] <= query_pos[None, :, None]
    same_piece = (query_ids[:, :, None] == key_ids[:, None, :]) & (query_ids[:, :, None] > 0)
    return (causal | same_piece)[:, None]


def blocked(running, pieces, group_len, step_fn):
    piece_len = pieces[0].shape[1]
    step_len = math.gcd(piece_len, group_len)

    def one_block(current, block_index):
        row_begin = block_index * step_len
        parts = tuple(
            (lax.dynamic_slice_in_dim(member, row_begin, step_len, 1) for member in pieces)
        )
        return (step_fn(current, parts, row_begin), None)

    running, _ = lax.scan(one_block, running, jnp.arange(piece_len // step_len, dtype=jnp.int32))
    return running


def shards(
    hidden_in,
    out_cotangent,
    attn_gain,
    attn_shift,
    qkv_weight,
    qkv_bias,
    proj_weight,
    proj_bias,
    mlp_gain,
    mlp_shift,
    up_weight,
    up_bias,
    down_weight,
    down_bias,
    picture_starts,
    group_order,
):
    batch_size, group_len, model_dim = hidden_in.shape
    token_rows = batch_size * group_len
    shard_rows = attn_gain.shape[0]
    ff_dim = up_weight.shape[1]
    ff_ratio = ff_dim // model_dim
    score_scale = HD ** (-0.5)
    f32 = jnp.float32
    bf16 = jnp.bfloat16
    hidden = hidden_in.reshape(token_rows, model_dim).astype(f32)
    centered = hidden - jnp.mean(hidden, axis=1, keepdims=True)
    inv_std = lax.rsqrt(jnp.mean(centered * centered, axis=1, keepdims=True) + norm_eps)
    normed = centered * inv_std
    own_rows = lax.axis_index("ctx") * group_len + jnp.arange(group_len, dtype=jnp.int32)
    own_pos = positions_of(own_rows, group_order, group_len)
    own_ids = piece_ids(own_pos, picture_starts)
    small_local = jnp.concatenate(
        [
            jnp.stack([attn_gain, attn_shift, mlp_gain, mlp_shift, proj_bias, down_bias], axis=1),
            qkv_bias.reshape(shard_rows, 3),
            up_bias.reshape(shard_rows, ff_ratio),
        ],
        axis=1,
    )
    down_rows = down_weight.reshape(shard_rows, ff_ratio * model_dim)
    small_piece = lax.all_gather(small_local, ("dp", "ctx"), axis=0, tiled=True)
    qkv_piece = lax.all_gather(qkv_weight, ("dp", "ctx"), axis=0, tiled=True)
    up_piece = lax.all_gather(up_weight, ("dp", "ctx"), axis=0, tiled=True)
    piece_len = qkv_piece.shape[0]
    small_f = small_piece.astype(f32)
    attn_piece = (normed * small_f[:, 0] + small_f[:, 1]).astype(bf16)
    mlp_piece = (normed * small_f[:, 2] + small_f[:, 3]).astype(bf16)
    qkv_sum = jnp.dot(attn_piece, qkv_piece, preferred_element_type=f32)
    up_sum = jnp.dot(mlp_piece, up_piece, preferred_element_type=f32)
    bias_table = small_f
    qkv_sum, up_sum, norm_attn, norm_mlp, bias_table = (
        qkv_sum,
        up_sum,
        attn_piece,
        mlp_piece,
        bias_table,
    )
    qkv_full = qkv_sum + bias_table[:, 6:9].reshape(-1)
    up_pre = up_sum + bias_table[:, 9:].reshape(-1)
    split_heads = qkv_full.reshape(batch_size, group_len, 3, H, HD)
    queries = rotate(split_heads[:, :, 0], own_pos, 1.0).astype(bf16)
    key_rows = rotate(split_heads[:, :, 1], own_pos, 1.0).astype(bf16)
    value_rows = split_heads[:, :, 2].astype(bf16)
    query_flat = queries.reshape(batch_size, group_len, model_dim)
    key_flat = key_rows.reshape(batch_size, group_len, model_dim)
    value_flat = value_rows.reshape(batch_size, group_len, model_dim)

    def forward_step(running, parts, row_begin):
        key_part, value_part = parts
        piece_len = key_part.shape[1]
        key_pos = positions_of(
            row_begin + jnp.arange(piece_len, dtype=jnp.int32), group_order, group_len
        )
        allowed = allowed_for(own_pos, own_ids, key_pos, piece_ids(key_pos, picture_starts))
        row_peak, row_total, summed = running
        key_heads = key_part.reshape(batch_size, piece_len, H, HD)
        value_heads = value_part.reshape(batch_size, piece_len, H, HD)
        scores = (
            jnp.einsum("bqhd,bkhd->bhqk", queries, key_heads, preferred_element_type=f32)
            * score_scale
        )
        masked = jnp.where(allowed, scores, masked_score)
        new_peak = jnp.maximum(row_peak, jnp.max(masked, axis=-1))
        row_fade = jnp.exp(row_peak - new_peak)
        weights = jnp.where(allowed, jnp.exp(masked - new_peak[..., None]), 0.0)
        row_total = row_total * row_fade + jnp.sum(weights, axis=-1)
        summed = summed * row_fade[..., None] + jnp.einsum(
            "bhqk,bkhd->bhqd", weights.astype(bf16), value_heads, preferred_element_type=f32
        )
        return (new_peak, row_total, summed)

    start_attn = (
        jnp.full((batch_size, H, group_len), masked_score, f32),
        jnp.zeros((batch_size, H, group_len), f32),
        jnp.zeros((batch_size, H, group_len, HD), f32),
    )
    row_peak, row_total, summed = blocked(
        start_attn,
        (
            lax.all_gather(key_flat, "ctx", axis=1, tiled=True),
            lax.all_gather(value_flat, "ctx", axis=1, tiled=True),
        ),
        group_len,
        forward_step,
    )
    log_total = row_peak + jnp.log(row_total)
    attended = (summed / row_total[..., None]).transpose(0, 2, 1, 3)
    attended_low = attended.reshape(token_rows, model_dim).astype(bf16)
    head_max = lax.pmax(jnp.max(row_peak, axis=(0, 2)), ("dp", "ctx"))
    act_low = exact_gelu(up_pre).astype(bf16)
    proj_piece = lax.all_gather(proj_weight, ("dp", "ctx"), axis=0, tiled=True)
    down_piece = lax.all_gather(down_rows, ("dp", "ctx"), axis=0, tiled=True)
    piece_len = proj_piece.shape[0]
    mix_sum = jnp.dot(attended_low, proj_piece, preferred_element_type=f32)
    mix_sum = mix_sum + jnp.dot(
        act_low, down_piece.reshape(piece_len * ff_ratio, model_dim), preferred_element_type=f32
    )
    block_out = (
        (hidden + mix_sum + bias_table[:, 4] + bias_table[:, 5])
        .astype(bf16)
        .reshape(batch_size, group_len, model_dim)
    )
    grad_y = out_cotangent.reshape(token_rows, model_dim)
    grad_yf = grad_y.astype(f32)
    proj_piece = lax.all_gather(proj_weight, ("dp", "ctx"), axis=0, tiled=True)
    down_piece = lax.all_gather(down_rows, ("dp", "ctx"), axis=0, tiled=True)
    piece_len = proj_piece.shape[0]
    attn_part = jnp.einsum("rd,nd->rn", grad_y, proj_piece, preferred_element_type=f32)
    act_part = jnp.einsum(
        "rd,md->rm",
        grad_y,
        down_piece.reshape(piece_len * ff_ratio, model_dim),
        preferred_element_type=f32,
    )
    grad_attn = attn_part
    grad_act = act_part
    grad_attn, grad_act = (grad_attn, grad_act)
    _, gelu_back = jax.vjp(exact_gelu, up_pre)
    grad_up = gelu_back(grad_act)[0].astype(bf16)
    grad_attended = grad_attn.astype(bf16)
    out_sum = jnp.sum(grad_yf, axis=0)
    out_width = model_dim + ff_ratio * model_dim + 1
    grad_heads = grad_attended.reshape(batch_size, group_len, H, HD)
    row_dot = jnp.sum(grad_heads.astype(f32) * attended, axis=-1).transpose(0, 2, 1)

    def query_step(running, parts, row_begin):
        key_part, value_part = parts
        piece_len = key_part.shape[1]
        key_pos = positions_of(
            row_begin + jnp.arange(piece_len, dtype=jnp.int32), group_order, group_len
        )
        allowed = allowed_for(own_pos, own_ids, key_pos, piece_ids(key_pos, picture_starts))
        key_heads = key_part.reshape(batch_size, piece_len, H, HD)
        value_heads = value_part.reshape(batch_size, piece_len, H, HD)
        scores = (
            jnp.einsum("bqhd,bkhd->bhqk", queries, key_heads, preferred_element_type=f32)
            * score_scale
        )
        masked = jnp.where(allowed, scores, masked_score)
        prob_rows = jnp.where(allowed, jnp.exp(masked - log_total[..., None]), 0.0)
        grad_prob = jnp.einsum(
            "bqhd,bkhd->bhqk", grad_heads, value_heads, preferred_element_type=f32
        )
        grad_scores = (prob_rows * (grad_prob - row_dot[..., None])).astype(bf16)
        return running + jnp.einsum(
            "bhqk,bkhd->bhqd", grad_scores, key_heads, preferred_element_type=f32
        )

    grad_query = (
        blocked(
            jnp.zeros((batch_size, H, group_len, HD), f32),
            (
                lax.all_gather(key_flat, "ctx", axis=1, tiled=True),
                lax.all_gather(value_flat, "ctx", axis=1, tiled=True),
            ),
            group_len,
            query_step,
        )
        * score_scale
    )
    log_total_all, row_dot_all = (
        lax.all_gather(log_total, "ctx", axis=2, tiled=True),
        lax.all_gather(row_dot, "ctx", axis=2, tiled=True),
    )

    def key_step(running, parts, row_begin):
        query_part, grad_part = parts
        piece_len = query_part.shape[1]
        query_pos = positions_of(
            row_begin + jnp.arange(piece_len, dtype=jnp.int32), group_order, group_len
        )
        allowed = allowed_for(query_pos, piece_ids(query_pos, picture_starts), own_pos, own_ids)
        total_part = lax.dynamic_slice_in_dim(log_total_all, row_begin, piece_len, 2)
        dot_part = lax.dynamic_slice_in_dim(row_dot_all, row_begin, piece_len, 2)
        grad_key, grad_value = running
        query_heads = query_part.reshape(batch_size, piece_len, H, HD)
        grad_piece = grad_part.reshape(batch_size, piece_len, H, HD)
        scores = (
            jnp.einsum("bqhd,bkhd->bhqk", query_heads, key_rows, preferred_element_type=f32)
            * score_scale
        )
        masked = jnp.where(allowed, scores, masked_score)
        prob_rows = jnp.where(allowed, jnp.exp(masked - total_part[..., None]), 0.0)
        grad_value = grad_value + jnp.einsum(
            "bhqk,bqhd->bhkd", prob_rows.astype(bf16), grad_piece, preferred_element_type=f32
        )
        grad_prob = jnp.einsum(
            "bqhd,bkhd->bhqk", grad_piece, value_rows, preferred_element_type=f32
        )
        grad_scores = (prob_rows * (grad_prob - dot_part[..., None])).astype(bf16)
        grad_key = grad_key + jnp.einsum(
            "bhqk,bqhd->bhkd", grad_scores, query_heads, preferred_element_type=f32
        )
        return (grad_key, grad_value)

    start_keys = (
        jnp.zeros((batch_size, H, group_len, HD), f32),
        jnp.zeros((batch_size, H, group_len, HD), f32),
    )
    grad_key, grad_value = blocked(
        start_keys,
        (
            lax.all_gather(query_flat, "ctx", axis=1, tiled=True),
            lax.all_gather(
                grad_attended.reshape(batch_size, group_len, model_dim), "ctx", axis=1, tiled=True
            ),
        ),
        group_len,
        key_step,
    )
    grad_key = grad_key * score_scale
    grad_q_back = rotate(grad_query.transpose(0, 2, 1, 3), own_pos, -1.0)
    grad_k_back = rotate(grad_key.transpose(0, 2, 1, 3), own_pos, -1.0)
    grad_v_back = grad_value.transpose(0, 2, 1, 3)
    grad_qkv = (
        jnp.stack([grad_q_back, grad_k_back, grad_v_back], axis=2)
        .reshape(token_rows, 3 * model_dim)
        .astype(bf16)
    )
    qkv_piece = lax.all_gather(qkv_weight, ("dp", "ctx"), axis=0, tiled=True)
    up_piece = lax.all_gather(up_weight, ("dp", "ctx"), axis=0, tiled=True)
    attn_part = jnp.einsum("re,ne->rn", grad_qkv, qkv_piece, preferred_element_type=f32)
    mlp_part = jnp.einsum("rf,nf->rn", grad_up, up_piece, preferred_element_type=f32)
    grad_norm_attn = attn_part
    grad_norm_mlp = mlp_part
    grad_norm_attn, grad_norm_mlp = (grad_norm_attn, grad_norm_mlp)
    gain_table = bias_table[:, 0:4]
    grad_norm = grad_norm_attn * gain_table[:, 0] + grad_norm_mlp * gain_table[:, 2]
    grad_hidden_f = grad_yf + inv_std * (
        grad_norm
        - jnp.mean(grad_norm, axis=1, keepdims=True)
        - normed * jnp.mean(grad_norm * normed, axis=1, keepdims=True)
    )
    grad_hidden = grad_hidden_f.astype(bf16).reshape(batch_size, group_len, model_dim)
    gain_grads = jnp.stack(
        [
            jnp.sum(grad_norm_attn * normed, axis=0),
            jnp.sum(grad_norm_attn, axis=0),
            jnp.sum(grad_norm_mlp * normed, axis=0),
            jnp.sum(grad_norm_mlp, axis=0),
        ],
        axis=1,
    )
    in_small = jnp.concatenate(
        [
            jnp.sum(grad_qkv.astype(f32), axis=0).reshape(model_dim, 3),
            jnp.sum(grad_up.astype(f32), axis=0).reshape(model_dim, ff_ratio),
            gain_grads,
        ],
        axis=1,
    )
    proj_part = jnp.einsum("rn,rd->nd", attended_low, grad_y, preferred_element_type=f32)
    down_part = jnp.einsum("rm,rd->md", act_low, grad_y, preferred_element_type=f32).reshape(
        model_dim, ff_ratio * model_dim
    )
    qkv_part = jnp.einsum("rn,re->ne", norm_attn, grad_qkv, preferred_element_type=f32)
    up_part = jnp.einsum("rn,rf->nf", norm_mlp, grad_up, preferred_element_type=f32)
    every_rows = lax.psum_scatter(
        jnp.concatenate(
            [
                jnp.concatenate([proj_part, down_part, out_sum[:, None]], axis=1),
                jnp.concatenate([qkv_part, up_part, in_small], axis=1),
            ],
            axis=1,
        ),
        ("dp", "ctx"),
        scatter_dimension=0,
        tiled=True,
    )
    out_rows = every_rows[:, :out_width]
    in_rows = every_rows[:, out_width:]
    grad_proj_weight = out_rows[:, :model_dim]
    grad_down_weight = out_rows[:, model_dim : model_dim + ff_ratio * model_dim].reshape(
        shard_rows * ff_ratio, model_dim
    )
    grad_bias_out = out_rows[:, out_width - 1]
    qkv_width = 3 * model_dim
    grad_qkv_weight = in_rows[:, :qkv_width]
    grad_up_weight = in_rows[:, qkv_width : qkv_width + ff_dim]
    tail_cols = in_rows[:, qkv_width + ff_dim :]
    grad_qkv_bias = tail_cols[:, :3].reshape(-1)
    grad_up_bias = tail_cols[:, 3 : 3 + ff_ratio].reshape(-1)
    gain_rows = tail_cols[:, 3 + ff_ratio :]
    clip_ratio = jnp.sqrt(clip_bound / jnp.maximum(head_max, clip_bound))
    head_cols = jnp.repeat(clip_ratio, HD)
    factor = jnp.concatenate([head_cols, head_cols, jnp.ones((model_dim,), f32)])
    clipped_qkv = qkv_weight.astype(f32) * factor[None, :]
    return (
        block_out,
        grad_hidden,
        gain_rows[:, 0],
        gain_rows[:, 1],
        grad_qkv_weight,
        grad_qkv_bias,
        grad_proj_weight,
        grad_bias_out,
        gain_rows[:, 2],
        gain_rows[:, 3],
        grad_up_weight,
        grad_up_bias,
        grad_down_weight,
        grad_bias_out,
        clipped_qkv,
    )


MESH = pl.DeviceIdType.MESH
NT = (((1,), (1,)), ((), ()))
f32 = jnp.float32
bf16 = jnp.bfloat16
CH = 8
NC = 16
SL = 1024
TOK = 2048
D = 1024


def dot(a, b):
    return jnp.dot(a, b, preferred_element_type=f32)


def dot_nt(a, b):
    return lax.dot_general(a, b, NT, preferred_element_type=f32)


def block_kernel(
    go_ref, ps_ref, x_ref, dy_ref, qw_ref, uw_ref, pw_ref, dw_ref,
    ag_ref, as_ref, mg_ref, ms_ref, pb_ref, db_ref, qb_ref, ub_ref,
    bo_ref, gh_ref, gra_ref, grb_ref, gp_ref, sr_ref, ds_ref,
    QW, UW, V0, V1, V2, V3, V4, V5, V6, V7, WS,
    X, Y, NA, NM, WC, WPD, CT, ST, PK, LIM, SM, BV,
    Q, K, V, VT, KT, PT, ATT, AA, GP, DA, GG, DQ, DK, DV, HM, GN,
    TT, GA, GB, GYA, GYB, PDS, SROW, DSUM,
    TMP, LP, SB, RSB, SR, RR,
    in_s, w_s, w_r, wy_s, wy_r, pd_s, pd_r, ga_s, ga_r, rs_s, rs_r,
    gy_s, gy_r, gg_s, gg_r, gpd_s, gpd_r, sm_s, sm_r, dm_s, dm_r,
):
    d = lax.axis_index("dp")
    c = lax.axis_index("ctx")
    k = c // 2
    j = c % 2
    z = k // 2
    r = z + (k % 2) * (7 - 2 * z)
    head = 8 * j + k

    def ctx_of(pos, core):
        p = (pos + 16) % 8
        return 2 * (2 * p + (p // 4) * (15 - 4 * p)) + core

    right = (d, ctx_of(r + 1, j))
    left = (d, ctx_of(r - 1, j))
    sibling = (d, 2 * k + (1 - j))
    partner = (1 - d, c)

    def rcopy(src, dst, ss, rs, dev):
        return pltpu.make_async_remote_copy(
            src_ref=src, dst_ref=dst, send_sem=ss, recv_sem=rs,
            device_id=dev, device_id_type=MESH,
        )

    barrier = pltpu.get_barrier_semaphore()

    def hello(o, _):
        lin = (d * NC + c + o) % 32
        pl.semaphore_signal(barrier, inc=1, device_id=(lin // NC, lin % NC), device_id_type=MESH)
        return 0

    lax.fori_loop(1, 32, hello, 0)

    def own_rows(s):
        return pl.ds(pl.multiple_of(s * SL + 64 * c, 64), 64)

    vecs = (V0, V1, V2, V3, V4, V5, V6, V7)
    fetch = [pltpu.make_async_copy(qw_ref, QW, in_s.at[0]), pltpu.make_async_copy(uw_ref, UW, in_s.at[1])]
    for i, ref in enumerate((ag_ref, as_ref, mg_ref, ms_ref, pb_ref, db_ref)):
        fetch.append(pltpu.make_async_copy(ref, vecs[i], in_s.at[2 + i]))
    fetch.append(pltpu.make_async_copy(qb_ref, vecs[6], in_s.at[8]))
    fetch.append(pltpu.make_async_copy(ub_ref, vecs[7], in_s.at[9]))
    fetch_x = [pltpu.make_async_copy(x_ref.at[s], X.at[own_rows(s)], in_s.at[10 + s]) for s in range(2)]
    fetch_y = [pltpu.make_async_copy(dy_ref.at[s], Y.at[own_rows(s)], in_s.at[12 + s]) for s in range(2)]
    for cp in fetch + fetch_x + fetch_y:
        cp.start()
    pl.semaphore_wait(barrier, 31)

    class Gather:
        def __init__(self, buf, own, s, i):
            self.buf, self.own, self.s, self.i = buf, own, s, i

        def at(self, delta, core):
            row = self.s * SL + 64 * ctx_of(r + delta, core)
            return self.buf.at[pl.ds(pl.multiple_of(row, 64), 64)]

        def ring(self, t, way, back=0):
            region = self.at((t + back) * (2 * way - 1), j)
            slot = 4 * way + t
            return rcopy(region, region, ga_s.at[self.i, slot], ga_r.at[self.i, slot],
                         left if way else right)

        def steps(self, way):
            return 4 if way == self.s else 3

        def sib(self, slot, core):
            delta = (0, -1, -2, -3, 1, 2, 3, 4)[slot]
            region = self.at(delta, core)
            return rcopy(region, region, ga_s.at[self.i, 8 + slot], ga_r.at[self.i, 8 + slot], sibling)

        def start(self):
            self.own[self.s].wait()
            self.ring(0, 0).start()
            self.ring(0, 1).start()
            self.sib(0, j).start()

        def pump(self, t):
            for way in (0, 1):
                if t <= self.steps(way):
                    self.ring(t - 1, way, 1).wait_recv()
                    if t < self.steps(way):
                        self.ring(t, way).start()
                    self.sib(7 if t == 4 else t + 3 * way, j).start()

        def ready(self, t):
            for slot in ((0,) if t == 0 else (t, 3 + t) if t < 4 else (7,)):
                self.sib(slot, 1 - j).wait_recv()

        def drain(self):
            for way in (0, 1):
                for t in range(self.steps(way)):
                    self.ring(t, way).wait_send()
            for slot in range(8):
                self.sib(slot, j).wait_send()

    gx = [Gather(X, fetch_x, s, s) for s in range(2)]
    gd = [Gather(Y, fetch_y, s, 2 + s) for s in range(2)]
    gx[0].start()
    for cp in fetch:
        cp.wait()

    def lane(shape):
        return lax.broadcasted_iota(jnp.int32, shape, len(shape) - 1)

    TMP[:, 0:128] = jnp.zeros((128, 128), f32)
    for i in range(6):
        TMP[64 + i:65 + i, 0:32] = vecs[i][...].astype(f32)
    TMP[0:1, 0:96] = V6[...].astype(f32)
    vq, vu = TMP[0:1, 0:128], V7[...].astype(f32)
    for i in range(3):
        TMP[70 + i:71 + i, 0:128] = pltpu.roll(vq, (128 - 32 * i) % 128, 1)
    for i in range(4):
        TMP[73 + i:74 + i, 0:128] = pltpu.roll(vu, (128 - 32 * i) % 128, 1)
    vcols = TMP[:, 0:128].T[0:32, :]
    low32 = lane((32, 128)) < 64
    for hp in range(H // 2):
        q2 = QW[:, 128 * hp:128 * hp + 128].astype(f32)
        k2 = QW[:, D + 128 * hp:D + 128 * hp + 128].astype(f32)
        v2 = QW[:, 2 * D + 128 * hp:2 * D + 128 * hp + 128].astype(f32)
        WS[2 * hp, :, 0:128] = jnp.where(low32, q2, pltpu.roll(k2, 64, 1)).astype(bf16)
        WS[2 * hp + 1, :, 0:128] = jnp.where(low32, pltpu.roll(q2, 64, 1), k2).astype(bf16)
        WS[2 * hp, :, 128:256] = jnp.where(low32, v2, vcols).astype(bf16)
        WS[2 * hp + 1, :, 128:256] = jnp.where(low32, pltpu.roll(v2, 64, 1), vcols).astype(bf16)
    for h in range(H):
        WS[h, :, 256:512] = UW[:, 256 * h:256 * h + 256]

    def w_copy(o, dst_c, row):
        return rcopy(
            WS.at[8 * (dst_c % 2) + dst_c // 2],
            WC.at[pl.ds(pl.multiple_of(row, 32), 32)],
            w_s.at[o], w_r.at[o], (d, dst_c),
        )

    own_row = 32 * (NC * d + c)

    def w_send(o, _):
        w_copy(o, (c + o) % NC, own_row).start()
        return 0

    lax.fori_loop(1, NC, w_send, 0)
    WC[pl.ds(pl.multiple_of(own_row, 32), 32), :] = WS[head]

    def wy_copy(o, plane):
        row = 32 * (NC * plane + (c - o + NC) % NC)
        region = WC.at[pl.ds(pl.multiple_of(row, 32), 32)]
        return rcopy(region, region, wy_s.at[o], wy_r.at[o], partner)

    wy_copy(0, d).start()
    gx[1].start()

    def pd_copies(jj, dst_dp):
        dev = (dst_dp, 2 * k + d)
        return (
            rcopy(pw_ref, WPD.at[pl.ds(256 + 32 * jj, 32)], pd_s.at[dst_dp, 0], pd_r.at[jj, 0], dev),
            rcopy(dw_ref, WPD.at[pl.ds(128 * jj, 128)], pd_s.at[dst_dp, 1], pd_r.at[jj, 1], dev),
        )

    here = d == j

    def pd_start():
        for e in range(2):
            @pl.when(jnp.logical_not(here & (d == e)))
            def _():
                for cp in pd_copies(j, e):
                    cp.start()

    local_pd = (
        pltpu.make_async_copy(pw_ref, WPD.at[pl.ds(256 + 32 * j, 32)], in_s.at[14]),
        pltpu.make_async_copy(dw_ref, WPD.at[pl.ds(128 * j, 128)], in_s.at[15]),
    )

    @pl.when(here)
    def _():
        for cp in local_pd:
            cp.start()
    WPD[320:384, :] = jnp.zeros((64, D), bf16)

    rows_i = lax.broadcasted_iota(jnp.int32, (SL, 128), 0)
    place = jnp.zeros((SL, 128), jnp.int32)
    cols_i = lane((8, SL))
    place_row = jnp.zeros((8, SL), jnp.int32)
    for b in range(NC):
        gob = go_ref[b]
        place = jnp.where((rows_i >> 6) == b, gob, place)
        place_row = jnp.where((cols_i >> 6) == b, gob, place_row)
    place = place * 64 + (rows_i & 63)
    place_row = place_row * 64 + (cols_i & 63)
    PK[...] = place
    for s in range(2):
        lim = place_row
        for p in range(PICS):
            st = ps_ref[s, p]
            lim = jnp.where((place_row >= st) & (place_row < st + PIC), st + (PIC - 1), lim)
        LIM[s] = lim

    def make_table(i, _):
        rows = pl.ds(pl.multiple_of(i * 128, 128), 128)
        ln = lane((128, 128))
        l64 = ln & 63
        freq = jnp.zeros((128, 128), f32)
        for q in range(ROT // 2):
            freq = jnp.where((l64 & 7) == q, float(rotary_base ** (-2.0 * q / ROT)), freq)
        ang = PK[rows, :].astype(f32) * freq
        CT[rows, :] = jnp.where(l64 < ROT, jnp.cos(ang), 1.0)
        sn = jnp.sin(ang)
        ST[rows, :] = jnp.where(l64 < ROT // 2, -sn, jnp.where(l64 < ROT, sn, 0.0))
        return 0

    lax.fori_loop(0, SL // 128, make_table, 0)

    half = pl.ds(pl.multiple_of(512 * d, 512), 512)
    other = pl.ds(pl.multiple_of(512 * (1 - d), 512), 512)

    def w_wait(o, _):
        src_c = (c - o + NC) % NC
        w_copy(o, (c + o) % NC, 32 * (NC * d + src_c)).wait_recv()
        wy_copy(o, d).start()
        return 0

    lax.fori_loop(1, NC, w_wait, 0)
    pd_start()
    gx[0].pump(1)

    def wy_wait(o, _):
        wy_copy(o, 1 - d).wait_recv()
        return 0

    lax.fori_loop(0, NC, wy_wait, 0)

    SM[...] = WC[:, 128:256].astype(f32).T[64:80, :]
    en = lane((16, 256))
    vrow = lax.broadcasted_iota(jnp.int32, (16, 256), 0)
    feat = lax.broadcasted_iota(jnp.int32, (D, 256), 0)
    jl = lane((D, 256))
    smb = SM[...].astype(bf16)

    def pick(e_big, e_small, div, first):
        onehot = jnp.where(feat == div(e_big)[0], 1.0, 0.0).astype(bf16)
        got = dot(smb, onehot)
        return jnp.sum(jnp.where(vrow == first + div(e_small)[1], got, 0.0), axis=0, keepdims=True)

    def place_qkv(e):
        owner = ((e >> 5) * 171) >> 9
        return 32 * owner + (e & 31), (e >> 5) - 3 * owner

    def place_up(e):
        return 32 * (e >> 7) + (e & 31), (e >> 5) & 3

    def e_qkv(ln):
        return SL * (ln >> 6) + HD * head + (ln & 63)

    bq = pick(e_qkv(jl), e_qkv(en), place_qkv, 6)
    bq = jnp.where(lane((1, 256)) < 192, bq, 0.0)
    bu = pick(256 * head + jl, 256 * head + en, place_up, 9)
    BV[0] = jnp.broadcast_to(bq, (8, 256))
    BV[1] = jnp.broadcast_to(bu, (8, 256))

    def turn(v, cs, sn, sign):
        l64 = lane(v.shape) & 63
        mate = jnp.where(l64 < ROT // 2, pltpu.roll(v, 120, 1), pltpu.roll(v, 8, 1))
        return v * cs + sign * (mate * sn)

    def normed_of(rows_value):
        x = rows_value.astype(f32)
        cen = x - jnp.mean(x, axis=1, keepdims=True)
        inv = lax.rsqrt(jnp.mean(cen * cen, axis=1, keepdims=True) + norm_eps)
        return cen * inv, inv

    def chip_rows(s, deltas):
        return [pl.ds(pl.multiple_of(s * SL + 64 * ctx_of(r + e, 0), 128), 128) for e in deltas]

    def load(ref, rows, lo=0, hi=None):
        parts = [ref[x, lo:hi] for x in rows]
        return parts[0] if len(parts) == 1 else jnp.concatenate(parts, axis=0)

    def store(ref, rows, value, lo=0, hi=None):
        for i, x in enumerate(rows):
            ref[x, lo:hi] = value[128 * i:128 * i + 128]

    def n_stage(s, deltas):
        rows, trow = chip_rows(s, deltas), chip_rows(0, deltas)
        low = lane((128 * len(rows), 128)) < 64
        nrm, _ = normed_of(load(X, rows))
        na = (nrm * SM[0:1, :] + SM[1:2, :]).astype(bf16)
        nm = (nrm * SM[2:3, :] + SM[3:4, :]).astype(bf16)
        store(NA, rows, na)
        store(NM, rows, nm)
        qkv = dot(na, WC[:, 0:256]) + BV[0, 0:1, :]
        up = dot(nm, WC[:, 256:512]) + BV[1, 0:1, :]
        rot = turn(qkv[:, 0:128], load(CT, trow), load(ST, trow), 1.0)
        store(Q, rows, jnp.where(low, rot * 0.125, 0.0).astype(bf16))
        store(K, rows, jnp.where(low, pltpu.roll(rot, 64, 1), 0.0).astype(bf16))
        store(V, rows, jnp.where(low, qkv[:, 128:256], 0.0).astype(bf16))
        cdf = 0.5 * (1.0 + lax.erf(up * (2.0 ** -0.5)))
        store(AA, rows, (up * cdf).astype(bf16), 0, 256)
        store(GP, rows, cdf + up * (jnp.exp(-0.5 * up * up) * ((2.0 * math.pi) ** -0.5)))

    def n_blocks(s, t):
        gx[s].ready(t)
        n_stage(s, (t,) if t in (0, 4) else (t, -t))

    def dy_blocks(s, t):
        if t == 0:
            gd[s].ready(4)
        gd[s].ready(t)
        dy_stage(s, (0, 4) if t == 0 else (t, -t))

    def turn_kv(s):
        VT[s] = V[s * SL:s * SL + SL, :].astype(f32).T[0:64, :].astype(bf16)
        KT[s] = K[s * SL:s * SL + SL, :].astype(f32).T[0:64, :].astype(bf16)

    HM[...] = jnp.full((8, 256), masked_score, f32)

    def fwd(i, _):
        s = i // 4
        q0 = pl.multiple_of((i % 4) * 256, 256)
        rows = pl.ds(pl.multiple_of(i * 256, 256), 256)
        seq = pl.ds(pl.multiple_of(s * SL, SL), SL)
        st = dot_nt(K[seq, :], Q[rows, :])
        pk = PK[...]
        lim = LIM[s, 0:1, pl.ds(q0, 256)]
        masked = jnp.where(jnp.concatenate([pk, pk], axis=1) <= lim, st, masked_score)
        peak = jnp.max(masked, axis=0, keepdims=True)
        p = jnp.exp(masked - peak)
        tot = jnp.sum(p, axis=0, keepdims=True)
        pt = (p * (1.0 / tot)).astype(bf16)
        PT[i] = pt
        at = dot(VT[s], pt)
        ATT[i] = at
        AA[rows, 256:384] = jnp.concatenate([at, jnp.zeros((64, 256), f32)], axis=0).T.astype(bf16)
        HM[...] = jnp.maximum(HM[...], jnp.broadcast_to(peak, (8, 256)))
        return 0

    class Scatter:
        def __init__(self, i, s, group, partial):
            self.i, self.s, self.g, self.partial = i, s, group, partial

        def sib(self, slot):
            return rcopy(SB.at[self.g, slot], SR.at[self.i, slot],
                         rs_s.at[self.i, 8 + slot], rs_r.at[self.i, 8 + slot], sibling)

        def produce(self, p):
            value = self.partial(self.s, (4, 0) if p == 0 else (4 - p, p - 4))
            for i, slot in enumerate((0, 7) if p == 0 else (2 * p - 1, 2 * p)):
                TMP[...] = value[128 * i:128 * i + 128]
                LP[self.g, slot] = TMP[pl.ds(pl.multiple_of(64 * j, 64), 64), :]
                SB[self.g, slot] = TMP[pl.ds(pl.multiple_of(64 * (1 - j), 64), 64), :].astype(bf16)
                self.sib(slot).start()

        def lane_sum(self, slot):
            self.sib(slot).wait_recv()
            return LP[self.g, slot] + SR[self.i, slot].astype(f32)

        def ring(self, t, way):
            slot = 4 * way + t
            return rcopy(RSB.at[self.g, slot], RR.at[self.i, slot],
                         rs_s.at[self.i, slot], rs_r.at[self.i, slot], left if way else right)

        def pump(self, t):
            for way in (self.s,) if t == 0 else (0, 1):
                slot = 4 * way + t
                v = self.lane_sum(2 * t - 1 + way if t else 0)
                if t > 1 or (t == 1 and way == self.s):
                    self.ring(t - 1, way).wait_recv()
                    v = v + RR[self.i, slot - 1].astype(f32)
                RSB[self.g, slot] = v.astype(bf16)
                self.ring(t, way).start()

        def total(self):
            v = self.lane_sum(7)
            for way in (0, 1):
                self.ring(3, way).wait_recv()
                v = v + RR[self.i, 4 * way + 3].astype(f32)
            return v

        def drain(self):
            for slot in range(8):
                self.sib(slot).wait_send()
            for way in (0, 1):
                for t in range(0 if way == self.s else 1, 4):
                    self.ring(t, way).wait_send()

    def out_partial(s, deltas):
        return dot(load(AA, chip_rows(s, deltas)), WPD[...])

    out = [Scatter(s, s, s, out_partial) for s in range(2)]
    DSUM[d] = jnp.zeros((8, D), f32)

    def dy_stage(s, deltas):
        rows = chip_rows(s, deltas)
        dyb = load(Y, rows)
        back = dot_nt(dyb, WPD[...])
        store(GG, rows, (back[:, 0:256] * load(GP, rows)).astype(bf16), 256, 512)
        store(DA, rows, back[:, 256:384].astype(bf16))
        DSUM[d] += jnp.broadcast_to(jnp.sum(dyb.astype(f32), axis=0, keepdims=True), (8, D))

    def bwd(i, _):
        s = i // 4
        rows = pl.ds(pl.multiple_of(i * 256, 256), 256)
        seq = pl.ds(pl.multiple_of(s * SL, SL), SL)
        q0 = pl.ds(pl.multiple_of((i % 4) * 256, 256), 256)
        da = DA[rows, :]
        rd = jnp.sum(da.astype(f32).T[0:64, :] * ATT[i], axis=0, keepdims=True)
        dpt = dot_nt(V[seq, :], da)
        pt = PT[i]
        ds = (pt.astype(f32) * (dpt - rd)).astype(bf16)
        DV[...] += dot(pt, da)
        DK[...] += dot(ds, Q[rows, :])
        DQ[q0, :] = jnp.concatenate([dot(KT[s], ds), jnp.zeros((64, 256), f32)], axis=0).T * 0.125
        return 0

    def qkv_back(i, s):
        trow = pl.ds(pl.multiple_of(i * 128, 128), 128)
        rows = pl.ds(pl.multiple_of(s * SL + i * 128, 128), 128)
        both = DQ[trow, :] + pltpu.roll(DK[trow, :], 64, 1)
        GG[rows, 0:128] = turn(both, CT[trow, :], ST[trow, :], -1.0).astype(bf16)
        GG[rows, 128:256] = DV[trow, :].astype(bf16)
        return s

    GN[...] = jnp.zeros((8, D), f32)

    def g_partial(s, deltas):
        rows = chip_rows(s, deltas)
        nrm, _ = normed_of(load(X, rows))
        gna = dot_nt(load(GG, rows, 0, 256), WC[:, 0:256])
        gnm = dot_nt(load(GG, rows, 256, 512), WC[:, 256:512])
        GN[0:1, :] += jnp.sum(gna * nrm, axis=0, keepdims=True)
        GN[1:2, :] += jnp.sum(gna, axis=0, keepdims=True)
        GN[2:3, :] += jnp.sum(gnm * nrm, axis=0, keepdims=True)
        GN[3:4, :] += jnp.sum(gnm, axis=0, keepdims=True)
        return gna * SM[0:1, :] + gnm * SM[2:3, :]

    grad = [Scatter(2 + s, s, s, g_partial) for s in range(2)]

    def out_done(s):
        tot = out[s].total()
        bo_ref[s * 64:s * 64 + 64, :] = (
            X[own_rows(s), :].astype(f32) + tot + SM[4:5, :] + SM[5:6, :]
        ).astype(bf16)
        out[s].drain()

    def bwd_start():
        DV[...] = jnp.zeros((SL, 128), f32)
        DK[...] = jnp.zeros((SL, 128), f32)

    def transpose_gg(lo):
        def one(i, _):
            rows = pl.ds(pl.multiple_of(i * 256, 256), 256)
            TT[0:256, rows] = GG[rows, lo:lo + 256].T
            return 0
        lax.fori_loop(0, 8, one, 0)

    def qkv_grad(i, _):
        cols = pl.ds(pl.multiple_of(i * 256, 256), 256)
        a = dot(TT[0:256, :], NA[:, cols])
        a = jnp.concatenate([a[0:192], GN[:, cols], a[200:256]], axis=0)
        GA[cols, :] = a.T.astype(bf16)
        return 0

    def up_grad(i, _):
        cols = pl.ds(pl.multiple_of(i * 256, 256), 256)
        GB[cols, :] = dot(TT[0:256, :], NM[:, cols]).T.astype(bf16)
        return 0

    gya = rcopy(GA.at[other], GYA, gy_s.at[0], gy_r.at[0], partner)
    gyb = rcopy(GB.at[other], GYB, gy_s.at[1], gy_r.at[1], partner)

    def up_weights():
        transpose_gg(256)
        lax.fori_loop(0, 4, up_grad, 0)
        gyb.start()

    def qkv_weights():
        transpose_gg(0)
        lax.fori_loop(0, 4, qkv_grad, 0)
        gya.start()

    def transpose_aa(i, _):
        rows = pl.ds(pl.multiple_of(i * 256, 256), 256)
        TT[:, rows] = AA[rows, :].T
        return 0

    def pd_grad(i, _):
        cols = pl.ds(pl.multiple_of(i * 256, 256), 256)
        PDS[:, cols] = dot(TT[...], Y[:, cols]).astype(bf16)
        return 0

    def gpd_copies(jj, slot_dp):
        dev = (j, 2 * k + jj)
        return (
            rcopy(PDS.at[pl.ds(256 + 32 * jj, 32)], gp_ref.at[slot_dp, pl.ds(0, 32)],
                  gpd_s.at[jj, 0], gpd_r.at[slot_dp, 0], dev),
            rcopy(PDS.at[pl.ds(128 * jj, 128)], gp_ref.at[slot_dp, pl.ds(32, 128)],
                  gpd_s.at[jj, 1], gpd_r.at[slot_dp, 1], dev),
        )

    def pd_weights():
        lax.fori_loop(0, 8, transpose_aa, 0)
        lax.fori_loop(0, 4, pd_grad, 0)
        for jj in range(2):
            @pl.when(jnp.logical_not(here & (j == jj)))
            def _():
                for cp in gpd_copies(jj, d):
                    cp.start()

        @pl.when(here)
        def _():
            gp_ref[d, 0:32, :] = PDS[pl.ds(256 + 32 * j, 32), :]
            gp_ref[d, 32:160, :] = PDS[pl.ds(128 * j, 128), :]

    def g_copy(half_i, o, dst_c, slot):
        src, dst = ((GA, gra_ref), (GB, grb_ref))[half_i]
        return rcopy(src.at[pl.ds(pl.multiple_of(512 * d + 32 * dst_c, 32), 32)], dst.at[slot],
                     gg_s.at[half_i, o], gg_r.at[half_i, o], (d, dst_c))

    def weights_out(half_i):
        gy, G, GY, gr_ref = ((gya, GA, GYA, gra_ref), (gyb, GB, GYB, grb_ref))[half_i]
        gy.wait_recv()
        G[half, :] = (G[half, :].astype(f32) + GY[...].astype(f32)).astype(bf16)

        def g_send(o, _):
            g_copy(half_i, o, (c + o) % NC, head).start()
            return 0

        lax.fori_loop(1, NC, g_send, 0)
        gr_ref[head] = G[pl.ds(pl.multiple_of(512 * d + 32 * c, 32), 32), :]

    def pd_ready():
        for jj in range(2):
            @pl.when(jnp.logical_not(here & (j == jj)))
            def _():
                for cp in pd_copies(jj, 0):
                    cp.wait_recv()

        @pl.when(here)
        def _():
            for cp in local_pd:
                cp.wait()

    def fwd_tiles(lo, hi):
        lax.fori_loop(lo, hi, fwd, 0)

    def bwd_tiles(lo, hi):
        lax.fori_loop(lo, hi, bwd, 0)

    dm = rcopy(DSUM.at[d], DSUM.at[d], dm_s, dm_r, partner)

    me = NC * d + c

    def s_copy(o, slot):
        lin = (me + o) % 32
        return rcopy(SROW, sr_ref.at[slot], sm_s.at[o], sm_r.at[o], (lin // NC, lin % NC))

    def token_sums():
        srow = jnp.zeros((1, 512), f32)
        for i in range(TOK // 256):
            srow = srow + jnp.sum(GG[i * 256:i * 256 + 256, :].astype(f32), axis=0, keepdims=True)
        hmax = jnp.max(HM[...], axis=1, keepdims=True)[0:1, :]
        SROW[...] = jnp.where(lane((1, 512)) == 192, hmax, srow)
        sr_ref[me] = SROW[...]

        def s_send(o, _):
            s_copy(o, me).start()
            return 0

        lax.fori_loop(1, 32, s_send, 0)

    def grad_done(s):
        tot = grad[s].total()
        own = slice(s * 64, s * 64 + 64)
        nrm, inv = normed_of(X[own_rows(s), :])
        gh_ref[own, :] = (
            Y[own_rows(s), :].astype(f32)
            + inv * (tot - jnp.mean(tot, axis=1, keepdims=True)
                     - nrm * jnp.mean(tot * nrm, axis=1, keepdims=True))
        ).astype(bf16)

    gx[1].pump(1)
    gx[0].pump(2)
    n_blocks(1, 0)
    n_blocks(0, 1)
    gx[1].pump(2)
    n_blocks(0, 2)
    n_blocks(1, 1)
    gx[0].pump(3)
    gd[0].start()
    n_blocks(0, 0)
    pd_ready()
    n_blocks(0, 3)
    gx[1].pump(3)
    n_blocks(1, 3)
    gx[0].pump(4)
    n_blocks(1, 2)
    gd[1].start()
    n_blocks(0, 4)
    turn_kv(0)
    fwd_tiles(0, 2)
    gd[0].pump(1)
    gx[1].pump(4)
    fwd_tiles(2, 4)
    gd[1].pump(1)
    n_blocks(1, 4)
    turn_kv(1)
    fwd_tiles(4, 6)
    gd[0].pump(2)
    fwd_tiles(6, 8)
    out[0].produce(0)
    out[0].produce(1)
    dy_blocks(1, 1)
    gd[1].pump(2)
    out[0].produce(2)
    out[0].produce(3)
    out[1].produce(0)
    out[0].pump(0)
    dy_blocks(0, 1)
    out[1].produce(1)
    out[1].pump(0)
    gd[0].pump(3)
    out[1].produce(2)
    out[1].produce(3)
    gd[1].pump(3)
    dy_blocks(0, 2)
    out[0].pump(1)
    out[1].pump(1)
    dy_blocks(1, 2)
    gd[1].pump(4)
    gd[0].pump(4)
    dy_blocks(1, 0)
    dy_blocks(0, 0)
    dy_blocks(1, 3)
    dy_blocks(0, 3)
    bwd_start()
    out[0].pump(2)
    up_weights()
    out[1].pump(2)
    bwd_tiles(0, 2)
    bwd_tiles(2, 4)
    out[0].pump(3)
    lax.fori_loop(0, 8, qkv_back, 0)
    out[1].pump(3)
    bwd_start()
    bwd_tiles(4, 6)
    bwd_tiles(6, 8)
    weights_out(1)
    out_done(0)
    grad[0].produce(0)
    grad[0].produce(1)
    out_done(1)
    grad[0].pump(0)
    lax.fori_loop(0, 8, qkv_back, 1)
    grad[1].produce(0)
    grad[1].produce(1)
    grad[1].pump(0)
    grad[0].produce(2)
    grad[0].pump(1)
    grad[1].produce(2)
    grad[1].pump(1)
    grad[1].produce(3)
    grad[0].produce(3)
    qkv_weights()
    grad[0].pump(2)
    grad[1].pump(2)
    pd_weights()
    dm.start()
    grad[0].pump(3)
    token_sums()
    grad[1].pump(3)
    weights_out(0)
    grad_done(1)
    grad_done(0)

    for e in range(2):
        @pl.when(jnp.logical_not(here & (d == e)))
        def _():
            for cp in gpd_copies(0, e):
                cp.wait_recv()

    rcopy(DSUM.at[1 - d], DSUM.at[1 - d], dm_s, dm_r, partner).wait_recv()
    ds_ref[...] = DSUM[0] + DSUM[1]

    def g_wait(o, _):
        src_c = (c - o + NC) % NC
        for half_i in range(2):
            g_copy(half_i, o, (c + o) % NC, 8 * (src_c % 2) + src_c // 2).wait_recv()
        return 0

    lax.fori_loop(1, NC, g_wait, 0)

    def s_wait(o, _):
        s_copy(o, (me - o + 32) % 32).wait_recv()
        return 0

    lax.fori_loop(1, 32, s_wait, 0)

    def w_done(o, _):
        w_copy(o, (c + o) % NC, own_row).wait_send()
        for half_i in range(2):
            g_copy(half_i, o, (c + o) % NC, head).wait_send()
        wy_copy(o, d).wait_send()
        return 0

    lax.fori_loop(1, NC, w_done, 0)

    def s_done(o, _):
        s_copy(o, me).wait_send()
        return 0

    lax.fori_loop(1, 32, s_done, 0)
    wy_copy(0, d).wait_send()
    gya.wait_send()
    gyb.wait_send()
    dm.wait_send()
    for e in range(2):
        @pl.when(jnp.logical_not(here & (d == e)))
        def _():
            for cp in pd_copies(j, e):
                cp.wait_send()

        @pl.when(jnp.logical_not(here & (j == e)))
        def _():
            for cp in gpd_copies(e, d):
                cp.wait_send()
    for item in gx + gd + grad:
        item.drain()


def finish_kernel(
    bo, gh, gra, grb, gp, sr, ds, qw,
    o_bo, o_gh, o_ag, o_as, o_qw, o_qb, o_pw, o_pb, o_mg, o_ms, o_uw, o_ub, o_dw, o_db, o_cq,
    B, F,
):
    me = NC * lax.axis_index("dp") + lax.axis_index("ctx")
    for s in range(2):
        o_bo[s] = bo[64 * s:64 * s + 64, :]
        o_gh[s] = gh[64 * s:64 * s + 64, :]
    o_pw[...] = gp[0, 0:32, :].astype(f32) + gp[1, 0:32, :].astype(f32)
    o_dw[...] = gp[0, 32:160, :].astype(f32) + gp[1, 32:160, :].astype(f32)
    low = lax.broadcasted_iota(jnp.int32, (32, 128), 1) < 64
    low1 = low[0:1]
    gains = jnp.zeros((32, 128), f32)
    for h in range(H):
        at = 2 * (h % 8) + h // 8
        one, two = sr[at], sr[NC + at]
        both = one + two
        peak = jnp.maximum(one, two)
        col = lax.broadcasted_iota(jnp.int32, (1, 512), 1)
        B[h:h + 1, :] = jnp.where(col == 192, peak, both)
        F[32 + 2 * h:33 + 2 * h, :] = both[:, 256:384]
        F[33 + 2 * h:34 + 2 * h, :] = both[:, 384:512]
        gains = gains + gra[h, :, 128:256].astype(f32)
        o_uw[:, 256 * h:256 * h + 256] = grb[h].astype(f32)
    top = B[:, 128:256]
    top = jnp.max(jnp.where(lax.broadcasted_iota(jnp.int32, (H, 128), 1) == 64, top, masked_score), axis=1, keepdims=True)
    ratio = jnp.broadcast_to(jnp.sqrt(clip_bound / jnp.maximum(top, clip_bound)), (H, 128))
    F[24:32, :] = jnp.zeros((8, 128), f32)
    for hp in range(H // 2):
        a, b = gra[2 * hp, :, 0:128].astype(f32), gra[2 * hp + 1, :, 0:128].astype(f32)
        va, vb = gra[2 * hp, :, 128:256].astype(f32), gra[2 * hp + 1, :, 128:256].astype(f32)
        o_qw[:, 128 * hp:128 * hp + 128] = jnp.where(low, a, pltpu.roll(b, 64, 1))
        o_qw[:, D + 128 * hp:D + 128 * hp + 128] = jnp.where(low, pltpu.roll(a, 64, 1), b)
        o_qw[:, 2 * D + 128 * hp:2 * D + 128 * hp + 128] = jnp.where(low, va, pltpu.roll(vb, 64, 1))
        ra, rb = B[2 * hp:2 * hp + 1, 0:128], B[2 * hp + 1:2 * hp + 2, 0:128]
        sa, sb = B[2 * hp:2 * hp + 1, 128:256], B[2 * hp + 1:2 * hp + 2, 128:256]
        F[hp:hp + 1, :] = jnp.where(low1, ra, pltpu.roll(rb, 64, 1))
        F[8 + hp:9 + hp, :] = jnp.where(low1, pltpu.roll(ra, 64, 1), rb)
        F[16 + hp:17 + hp, :] = jnp.where(low1, sa, pltpu.roll(sb, 64, 1))
        fac = jnp.where(low1, ratio[2 * hp:2 * hp + 1], ratio[2 * hp + 1:2 * hp + 2])
        for part in range(3):
            cols = slice(part * D + 128 * hp, part * D + 128 * hp + 128)
            w = qw[:, cols].astype(f32)
            o_cq[:, cols] = w * fac if part < 2 else w
    grows = jnp.concatenate([gains, jnp.zeros((96, 128), f32)], axis=0).T
    for i, o in enumerate((o_ag, o_as, o_mg, o_ms)):
        o[...] = grows[64 + i:65 + i, 0:32]
    row, shift = (96 * me) // 128, (96 * me) % 128
    turned = pltpu.roll(F[pl.ds(row, 1), :], (128 - shift) % 128, 1)
    after = pltpu.roll(F[pl.ds(row + 1, 1), :], (128 - shift) % 128, 1)
    col = lax.broadcasted_iota(jnp.int32, (1, 128), 1)
    o_qb[...] = jnp.where(col < 128 - shift, turned, after)[:, 0:96]
    o_ub[...] = F[pl.ds(32 + me, 1), :]
    dsum = ds[0:1, pl.ds(pl.multiple_of(128 * (me // 4), 128), 128)]
    dsum = pltpu.roll(dsum, (128 - 32 * (me % 4)) % 128, 1)[:, 0:32]
    o_pb[...] = dsum
    o_db[...] = dsum


def fast_shards(
    hidden_in, out_cotangent, attn_gain, attn_shift, qkv_weight, qkv_bias, proj_weight, proj_bias,
    mlp_gain, mlp_shift, up_weight, up_bias, down_weight, down_bias, picture_starts, group_order,
):
    vm = pl.BlockSpec(memory_space=pltpu.VMEM)
    sm = pl.BlockSpec(memory_space=pltpu.SMEM)
    hbm = pl.BlockSpec(memory_space=pl.ANY)
    V_ = pltpu.VMEM
    dma = pltpu.SemaphoreType.DMA

    def sds(shape, dtype=f32):
        return jax.ShapeDtypeStruct(shape, dtype)

    got = pl.pallas_call(
        block_kernel,
        out_shape=(
            sds((128, D), bf16), sds((128, D), bf16), sds((NC, 32, 256), bf16), sds((NC, 32, 256), bf16),
            sds((2, 160, D), bf16), sds((32, 1, 512)), sds((8, D)),
        ),
        in_specs=[sm, sm] + [hbm] * 14,
        out_specs=(vm,) * 7,
        scratch_shapes=[
            V_((32, 3 * D), bf16), V_((32, 4 * D), bf16), *(V_((1, n), bf16) for n in (32,) * 6 + (96, 128)), V_((NC, 32, 512), bf16),
            V_((TOK, D), bf16), V_((TOK, D), bf16), V_((TOK, D), bf16), V_((TOK, D), bf16),
            V_((D, 512), bf16), V_((384, D), bf16),
            V_((SL, 128), f32), V_((SL, 128), f32), V_((SL, 128), jnp.int32),
            V_((2, 8, SL), jnp.int32), V_((16, D), f32), V_((2, 8, 256), f32),
            V_((TOK, 128), bf16), V_((TOK, 128), bf16), V_((TOK, 128), bf16),
            V_((2, 64, SL), bf16), V_((2, 64, SL), bf16),
            V_((8, SL, 256), bf16), V_((8, 64, 256), f32),
            V_((TOK, 384), bf16), V_((TOK, 256), f32), V_((TOK, 128), bf16), V_((TOK, 512), bf16),
            V_((SL, 128), f32), V_((SL, 128), f32), V_((SL, 128), f32),
            V_((8, 256), f32), V_((8, D), f32),
            V_((384, TOK), bf16), V_((D, 256), bf16), V_((D, 256), bf16),
            V_((512, 256), bf16), V_((512, 256), bf16),
            V_((384, D), bf16), V_((1, 512), f32), V_((2, 8, D), f32),
            V_((128, D), f32), V_((2, 8, 64, D), f32), V_((2, 8, 64, D), bf16),
            V_((2, 8, 64, D), bf16), V_((4, 8, 64, D), bf16), V_((4, 8, 64, D), bf16),
            dma((16,)), dma((NC,)), dma((NC,)), dma((NC,)), dma((NC,)), dma((2, 2)), dma((2, 2)),
            dma((4, 16)), dma((4, 16)), dma((4, 16)), dma((4, 16)),
            dma((2,)), dma((2,)), dma((2, NC)), dma((2, NC)), dma((2, 2)), dma((2, 2)), dma((32,)), dma((32,)), dma, dma,
        ],
        compiler_params=pltpu.CompilerParams(
            collective_id=0, has_side_effects=True, vmem_limit_bytes=63 * 1024 * 1024
        ),
    )(
        group_order, picture_starts, hidden_in, out_cotangent, qkv_weight, up_weight, proj_weight, down_weight,
        *(v.reshape(1, -1) for v in (
            attn_gain, attn_shift, mlp_gain, mlp_shift, proj_bias, down_bias, qkv_bias, up_bias)),
    )
    r32 = sds((1, 32))
    outs = pl.pallas_call(
        finish_kernel,
        out_shape=(
            sds((2, 64, D), bf16), sds((2, 64, D), bf16), r32, r32, sds((32, 3 * D)), sds((1, 96)),
            sds((32, D)), r32, r32, r32, sds((32, 4 * D)), sds((1, 128)), sds((128, D)), r32, sds((32, 3 * D)),
        ),
        in_specs=[vm] * 8,
        out_specs=(vm,) * 15,
        scratch_shapes=[V_((H, 512), f32), V_((64, 128), f32)],
    )(*got, qkv_weight)
    return tuple(o.reshape(-1) if o.shape[0] == 1 else o for o in outs)


def solution(mesh):
    in_specs = (
        P("dp", "ctx", None),
        P("dp", "ctx", None),
        P(("dp", "ctx")),
        P(("dp", "ctx")),
        P(("dp", "ctx"), None),
        P(("dp", "ctx")),
        P(("dp", "ctx"), None),
        P(("dp", "ctx")),
        P(("dp", "ctx")),
        P(("dp", "ctx")),
        P(("dp", "ctx"), None),
        P(("dp", "ctx")),
        P(("dp", "ctx"), None),
        P(("dp", "ctx")),
        P("dp", None),
        P(),
    )
    out_specs = (
        P("dp", "ctx", None),
        P("dp", "ctx", None),
        P(("dp", "ctx")),
        P(("dp", "ctx")),
        P(("dp", "ctx"), None),
        P(("dp", "ctx")),
        P(("dp", "ctx"), None),
        P(("dp", "ctx")),
        P(("dp", "ctx")),
        P(("dp", "ctx")),
        P(("dp", "ctx"), None),
        P(("dp", "ctx")),
        P(("dp", "ctx"), None),
        P(("dp", "ctx")),
        P(("dp", "ctx"), None),
    )
    body = fast_shards if (mesh.shape["dp"], mesh.shape["ctx"]) == (2, H) else shards
    return jax.shard_map(body, mesh=mesh, in_specs=in_specs, out_specs=out_specs, check_vma=False)
```

```python
import math

import jax
import jax.numpy as jnp
from jax import lax
from jax.experimental import pallas as pl
from jax.experimental.pallas import tpu as pltpu
from jax.sharding import PartitionSpec as P

H = 16
HD = 64
ROT = 16
PIC = 256
PICS = 4


norm_eps = 1e-05
clip_bound = 8.0
rotary_base = 10000.0
masked_score = -1e30


def exact_gelu(values):
    return jax.nn.gelu(values, approximate=False)


def rotate(values, positions, turn_sign):
    half_rot = ROT // 2
    inv_freq = rotary_base ** (-2.0 * jnp.arange(half_rot, dtype=jnp.float32) / ROT)
    angles = positions.astype(jnp.float32)[:, None] * inv_freq[None, :]
    cosine = jnp.cos(angles)[None, :, None, :]
    sine_part = turn_sign * jnp.sin(angles)[None, :, None, :]
    lead_half = values[..., :half_rot]
    tail_half = values[..., half_rot:ROT]
    return jnp.concatenate(
        [
            lead_half * cosine - tail_half * sine_part,
            tail_half * cosine + lead_half * sine_part,
            values[..., ROT:],
        ],
        axis=-1,
    )


def positions_of(row_numbers, group_order, group_len):
    group_ids = row_numbers // group_len
    owners = jnp.arange(group_order.shape[0], dtype=jnp.int32)
    placed = jnp.sum(
        jnp.where(group_ids[:, None] == owners[None, :], group_order[None, :], 0), axis=1
    )
    return placed * group_len + row_numbers % group_len


def piece_ids(positions, picture_starts):
    inside = (positions[None, None, :] >= picture_starts[:, :, None]) & (
        positions[None, None, :] < picture_starts[:, :, None] + PIC
    )
    labels = jnp.arange(1, PICS + 1, dtype=jnp.int32)[None, :, None]
    return jnp.sum(jnp.where(inside, labels, 0), axis=1)


def allowed_for(query_pos, query_ids, key_pos, key_ids):
    causal = key_pos[None, None, :] <= query_pos[None, :, None]
    same_piece = (query_ids[:, :, None] == key_ids[:, None, :]) & (query_ids[:, :, None] > 0)
    return (causal | same_piece)[:, None]


def blocked(running, pieces, group_len, step_fn):
    piece_len = pieces[0].shape[1]
    step_len = math.gcd(piece_len, group_len)

    def one_block(current, block_index):
        row_begin = block_index * step_len
        parts = tuple(
            (lax.dynamic_slice_in_dim(member, row_begin, step_len, 1) for member in pieces)
        )
        return (step_fn(current, parts, row_begin), None)

    running, _ = lax.scan(one_block, running, jnp.arange(piece_len // step_len, dtype=jnp.int32))
    return running


def shards(
    hidden_in,
    out_cotangent,
    attn_gain,
    attn_shift,
    qkv_weight,
    qkv_bias,
    proj_weight,
    proj_bias,
    mlp_gain,
    mlp_shift,
    up_weight,
    up_bias,
    down_weight,
    down_bias,
    picture_starts,
    group_order,
):
    batch_size, group_len, model_dim = hidden_in.shape
    token_rows = batch_size * group_len
    shard_rows = attn_gain.shape[0]
    ff_dim = up_weight.shape[1]
    ff_ratio = ff_dim // model_dim
    score_scale = HD ** (-0.5)
    f32 = jnp.float32
    bf16 = jnp.bfloat16
    hidden = hidden_in.reshape(token_rows, model_dim).astype(f32)
    centered = hidden - jnp.mean(hidden, axis=1, keepdims=True)
    inv_std = lax.rsqrt(jnp.mean(centered * centered, axis=1, keepdims=True) + norm_eps)
    normed = centered * inv_std
    own_rows = lax.axis_index("ctx") * group_len + jnp.arange(group_len, dtype=jnp.int32)
    own_pos = positions_of(own_rows, group_order, group_len)
    own_ids = piece_ids(own_pos, picture_starts)
    small_local = jnp.concatenate(
        [
            jnp.stack([attn_gain, attn_shift, mlp_gain, mlp_shift, proj_bias, down_bias], axis=1),
            qkv_bias.reshape(shard_rows, 3),
            up_bias.reshape(shard_rows, ff_ratio),
        ],
        axis=1,
    )
    down_rows = down_weight.reshape(shard_rows, ff_ratio * model_dim)
    small_piece = lax.all_gather(small_local, ("dp", "ctx"), axis=0, tiled=True)
    qkv_piece = lax.all_gather(qkv_weight, ("dp", "ctx"), axis=0, tiled=True)
    up_piece = lax.all_gather(up_weight, ("dp", "ctx"), axis=0, tiled=True)
    piece_len = qkv_piece.shape[0]
    small_f = small_piece.astype(f32)
    attn_piece = (normed * small_f[:, 0] + small_f[:, 1]).astype(bf16)
    mlp_piece = (normed * small_f[:, 2] + small_f[:, 3]).astype(bf16)
    qkv_sum = jnp.dot(attn_piece, qkv_piece, preferred_element_type=f32)
    up_sum = jnp.dot(mlp_piece, up_piece, preferred_element_type=f32)
    bias_table = small_f
    qkv_sum, up_sum, norm_attn, norm_mlp, bias_table = (
        qkv_sum,
        up_sum,
        attn_piece,
        mlp_piece,
        bias_table,
    )
    qkv_full = qkv_sum + bias_table[:, 6:9].reshape(-1)
    up_pre = up_sum + bias_table[:, 9:].reshape(-1)
    split_heads = qkv_full.reshape(batch_size, group_len, 3, H, HD)
    queries = rotate(split_heads[:, :, 0], own_pos, 1.0).astype(bf16)
    key_rows = rotate(split_heads[:, :, 1], own_pos, 1.0).astype(bf16)
    value_rows = split_heads[:, :, 2].astype(bf16)
    query_flat = queries.reshape(batch_size, group_len, model_dim)
    key_flat = key_rows.reshape(batch_size, group_len, model_dim)
    value_flat = value_rows.reshape(batch_size, group_len, model_dim)

    def forward_step(running, parts, row_begin):
        key_part, value_part = parts
        piece_len = key_part.shape[1]
        key_pos = positions_of(
            row_begin + jnp.arange(piece_len, dtype=jnp.int32), group_order, group_len
        )
        allowed = allowed_for(own_pos, own_ids, key_pos, piece_ids(key_pos, picture_starts))
        row_peak, row_total, summed = running
        key_heads = key_part.reshape(batch_size, piece_len, H, HD)
        value_heads = value_part.reshape(batch_size, piece_len, H, HD)
        scores = (
            jnp.einsum("bqhd,bkhd->bhqk", queries, key_heads, preferred_element_type=f32)
            * score_scale
        )
        masked = jnp.where(allowed, scores, masked_score)
        new_peak = jnp.maximum(row_peak, jnp.max(masked, axis=-1))
        row_fade = jnp.exp(row_peak - new_peak)
        weights = jnp.where(allowed, jnp.exp(masked - new_peak[..., None]), 0.0)
        row_total = row_total * row_fade + jnp.sum(weights, axis=-1)
        summed = summed * row_fade[..., None] + jnp.einsum(
            "bhqk,bkhd->bhqd", weights.astype(bf16), value_heads, preferred_element_type=f32
        )
        return (new_peak, row_total, summed)

    start_attn = (
        jnp.full((batch_size, H, group_len), masked_score, f32),
        jnp.zeros((batch_size, H, group_len), f32),
        jnp.zeros((batch_size, H, group_len, HD), f32),
    )
    row_peak, row_total, summed = blocked(
        start_attn,
        (
            lax.all_gather(key_flat, "ctx", axis=1, tiled=True),
            lax.all_gather(value_flat, "ctx", axis=1, tiled=True),
        ),
        group_len,
        forward_step,
    )
    log_total = row_peak + jnp.log(row_total)
    attended = (summed / row_total[..., None]).transpose(0, 2, 1, 3)
    attended_low = attended.reshape(token_rows, model_dim).astype(bf16)
    head_max = lax.pmax(jnp.max(row_peak, axis=(0, 2)), ("dp", "ctx"))
    act_low = exact_gelu(up_pre).astype(bf16)
    proj_piece = lax.all_gather(proj_weight, ("dp", "ctx"), axis=0, tiled=True)
    down_piece = lax.all_gather(down_rows, ("dp", "ctx"), axis=0, tiled=True)
    piece_len = proj_piece.shape[0]
    mix_sum = jnp.dot(attended_low, proj_piece, preferred_element_type=f32)
    mix_sum = mix_sum + jnp.dot(
        act_low, down_piece.reshape(piece_len * ff_ratio, model_dim), preferred_element_type=f32
    )
    block_out = (
        (hidden + mix_sum + bias_table[:, 4] + bias_table[:, 5])
        .astype(bf16)
        .reshape(batch_size, group_len, model_dim)
    )
    grad_y = out_cotangent.reshape(token_rows, model_dim)
    grad_yf = grad_y.astype(f32)
    proj_piece = lax.all_gather(proj_weight, ("dp", "ctx"), axis=0, tiled=True)
    down_piece = lax.all_gather(down_rows, ("dp", "ctx"), axis=0, tiled=True)
    piece_len = proj_piece.shape[0]
    attn_part = jnp.einsum("rd,nd->rn", grad_y, proj_piece, preferred_element_type=f32)
    act_part = jnp.einsum(
        "rd,md->rm",
        grad_y,
        down_piece.reshape(piece_len * ff_ratio, model_dim),
        preferred_element_type=f32,
    )
    grad_attn = attn_part
    grad_act = act_part
    grad_attn, grad_act = (grad_attn, grad_act)
    _, gelu_back = jax.vjp(exact_gelu, up_pre)
    grad_up = gelu_back(grad_act)[0].astype(bf16)
    grad_attended = grad_attn.astype(bf16)
    out_sum = jnp.sum(grad_yf, axis=0)
    out_width = model_dim + ff_ratio * model_dim + 1
    grad_heads = grad_attended.reshape(batch_size, group_len, H, HD)
    row_dot = jnp.sum(grad_heads.astype(f32) * attended, axis=-1).transpose(0, 2, 1)

    def query_step(running, parts, row_begin):
        key_part, value_part = parts
        piece_len = key_part.shape[1]
        key_pos = positions_of(
            row_begin + jnp.arange(piece_len, dtype=jnp.int32), group_order, group_len
        )
        allowed = allowed_for(own_pos, own_ids, key_pos, piece_ids(key_pos, picture_starts))
        key_heads = key_part.reshape(batch_size, piece_len, H, HD)
        value_heads = value_part.reshape(batch_size, piece_len, H, HD)
        scores = (
            jnp.einsum("bqhd,bkhd->bhqk", queries, key_heads, preferred_element_type=f32)
            * score_scale
        )
        masked = jnp.where(allowed, scores, masked_score)
        prob_rows = jnp.where(allowed, jnp.exp(masked - log_total[..., None]), 0.0)
        grad_prob = jnp.einsum(
            "bqhd,bkhd->bhqk", grad_heads, value_heads, preferred_element_type=f32
        )
        grad_scores = (prob_rows * (grad_prob - row_dot[..., None])).astype(bf16)
        return running + jnp.einsum(
            "bhqk,bkhd->bhqd", grad_scores, key_heads, preferred_element_type=f32
        )

    grad_query = (
        blocked(
            jnp.zeros((batch_size, H, group_len, HD), f32),
            (
                lax.all_gather(key_flat, "ctx", axis=1, tiled=True),
                lax.all_gather(value_flat, "ctx", axis=1, tiled=True),
            ),
            group_len,
            query_step,
        )
        * score_scale
    )
    log_total_all, row_dot_all = (
        lax.all_gather(log_total, "ctx", axis=2, tiled=True),
        lax.all_gather(row_dot, "ctx", axis=2, tiled=True),
    )

    def key_step(running, parts, row_begin):
        query_part, grad_part = parts
        piece_len = query_part.shape[1]
        query_pos = positions_of(
            row_begin + jnp.arange(piece_len, dtype=jnp.int32), group_order, group_len
        )
        allowed = allowed_for(query_pos, piece_ids(query_pos, picture_starts), own_pos, own_ids)
        total_part = lax.dynamic_slice_in_dim(log_total_all, row_begin, piece_len, 2)
        dot_part = lax.dynamic_slice_in_dim(row_dot_all, row_begin, piece_len, 2)
        grad_key, grad_value = running
        query_heads = query_part.reshape(batch_size, piece_len, H, HD)
        grad_piece = grad_part.reshape(batch_size, piece_len, H, HD)
        scores = (
            jnp.einsum("bqhd,bkhd->bhqk", query_heads, key_rows, preferred_element_type=f32)
            * score_scale
        )
        masked = jnp.where(allowed, scores, masked_score)
        prob_rows = jnp.where(allowed, jnp.exp(masked - total_part[..., None]), 0.0)
        grad_value = grad_value + jnp.einsum(
            "bhqk,bqhd->bhkd", prob_rows.astype(bf16), grad_piece, preferred_element_type=f32
        )
        grad_prob = jnp.einsum(
            "bqhd,bkhd->bhqk", grad_piece, value_rows, preferred_element_type=f32
        )
        grad_scores = (prob_rows * (grad_prob - dot_part[..., None])).astype(bf16)
        grad_key = grad_key + jnp.einsum(
            "bhqk,bqhd->bhkd", grad_scores, query_heads, preferred_element_type=f32
        )
        return (grad_key, grad_value)

    start_keys = (
        jnp.zeros((batch_size, H, group_len, HD), f32),
        jnp.zeros((batch_size, H, group_len, HD), f32),
    )
    grad_key, grad_value = blocked(
        start_keys,
        (
            lax.all_gather(query_flat, "ctx", axis=1, tiled=True),
            lax.all_gather(
                grad_attended.reshape(batch_size, group_len, model_dim), "ctx", axis=1, tiled=True
            ),
        ),
        group_len,
        key_step,
    )
    grad_key = grad_key * score_scale
    grad_q_back = rotate(grad_query.transpose(0, 2, 1, 3), own_pos, -1.0)
    grad_k_back = rotate(grad_key.transpose(0, 2, 1, 3), own_pos, -1.0)
    grad_v_back = grad_value.transpose(0, 2, 1, 3)
    grad_qkv = (
        jnp.stack([grad_q_back, grad_k_back, grad_v_back], axis=2)
        .reshape(token_rows, 3 * model_dim)
        .astype(bf16)
    )
    qkv_piece = lax.all_gather(qkv_weight, ("dp", "ctx"), axis=0, tiled=True)
    up_piece = lax.all_gather(up_weight, ("dp", "ctx"), axis=0, tiled=True)
    attn_part = jnp.einsum("re,ne->rn", grad_qkv, qkv_piece, preferred_element_type=f32)
    mlp_part = jnp.einsum("rf,nf->rn", grad_up, up_piece, preferred_element_type=f32)
    grad_norm_attn = attn_part
    grad_norm_mlp = mlp_part
    grad_norm_attn, grad_norm_mlp = (grad_norm_attn, grad_norm_mlp)
    gain_table = bias_table[:, 0:4]
    grad_norm = grad_norm_attn * gain_table[:, 0] + grad_norm_mlp * gain_table[:, 2]
    grad_hidden_f = grad_yf + inv_std * (
        grad_norm
        - jnp.mean(grad_norm, axis=1, keepdims=True)
        - normed * jnp.mean(grad_norm * normed, axis=1, keepdims=True)
    )
    grad_hidden = grad_hidden_f.astype(bf16).reshape(batch_size, group_len, model_dim)
    gain_grads = jnp.stack(
        [
            jnp.sum(grad_norm_attn * normed, axis=0),
            jnp.sum(grad_norm_attn, axis=0),
            jnp.sum(grad_norm_mlp * normed, axis=0),
            jnp.sum(grad_norm_mlp, axis=0),
        ],
        axis=1,
    )
    in_small = jnp.concatenate(
        [
            jnp.sum(grad_qkv.astype(f32), axis=0).reshape(model_dim, 3),
            jnp.sum(grad_up.astype(f32), axis=0).reshape(model_dim, ff_ratio),
            gain_grads,
        ],
        axis=1,
    )
    proj_part = jnp.einsum("rn,rd->nd", attended_low, grad_y, preferred_element_type=f32)
    down_part = jnp.einsum("rm,rd->md", act_low, grad_y, preferred_element_type=f32).reshape(
        model_dim, ff_ratio * model_dim
    )
    qkv_part = jnp.einsum("rn,re->ne", norm_attn, grad_qkv, preferred_element_type=f32)
    up_part = jnp.einsum("rn,rf->nf", norm_mlp, grad_up, preferred_element_type=f32)
    every_rows = lax.psum_scatter(
        jnp.concatenate(
            [
                jnp.concatenate([proj_part, down_part, out_sum[:, None]], axis=1),
                jnp.concatenate([qkv_part, up_part, in_small], axis=1),
            ],
            axis=1,
        ),
        ("dp", "ctx"),
        scatter_dimension=0,
        tiled=True,
    )
    out_rows = every_rows[:, :out_width]
    in_rows = every_rows[:, out_width:]
    grad_proj_weight = out_rows[:, :model_dim]
    grad_down_weight = out_rows[:, model_dim : model_dim + ff_ratio * model_dim].reshape(
        shard_rows * ff_ratio, model_dim
    )
    grad_bias_out = out_rows[:, out_width - 1]
    qkv_width = 3 * model_dim
    grad_qkv_weight = in_rows[:, :qkv_width]
    grad_up_weight = in_rows[:, qkv_width : qkv_width + ff_dim]
    tail_cols = in_rows[:, qkv_width + ff_dim :]
    grad_qkv_bias = tail_cols[:, :3].reshape(-1)
    grad_up_bias = tail_cols[:, 3 : 3 + ff_ratio].reshape(-1)
    gain_rows = tail_cols[:, 3 + ff_ratio :]
    clip_ratio = jnp.sqrt(clip_bound / jnp.maximum(head_max, clip_bound))
    head_cols = jnp.repeat(clip_ratio, HD)
    factor = jnp.concatenate([head_cols, head_cols, jnp.ones((model_dim,), f32)])
    clipped_qkv = qkv_weight.astype(f32) * factor[None, :]
    return (
        block_out,
        grad_hidden,
        gain_rows[:, 0],
        gain_rows[:, 1],
        grad_qkv_weight,
        grad_qkv_bias,
        grad_proj_weight,
        grad_bias_out,
        gain_rows[:, 2],
        gain_rows[:, 3],
        grad_up_weight,
        grad_up_bias,
        grad_down_weight,
        grad_bias_out,
        clipped_qkv,
    )


MESH = pl.DeviceIdType.MESH
NT = (((1,), (1,)), ((), ()))
f32 = jnp.float32
bf16 = jnp.bfloat16
CH = 8
NC = 16
SL = 1024
TOK = 2048
D = 1024


def dot(a, b):
    return jnp.dot(a, b, preferred_element_type=f32)


def dot_nt(a, b):
    return lax.dot_general(a, b, NT, preferred_element_type=f32)


def block_kernel(
    go_ref, ps_ref, x_ref, dy_ref, qw_ref, uw_ref, pw_ref, dw_ref,
    ag_ref, as_ref, mg_ref, ms_ref, pb_ref, db_ref, qb_ref, ub_ref,
    bo_ref, gh_ref, gra_ref, grb_ref, gp_ref, sr_ref, ds_ref,
    QW, UW, V0, V1, V2, V3, V4, V5, V6, V7, WS,
    X, Y, NA, NM, WC, WPD, CT, ST, PK, LIM, SM, BV,
    Q, K, V, VT, KT, PT, ATT, AA, GP, DA, GG, DQ, DK, DV, HM, GN,
    TT, GA, GB, GYA, GYB, PDS, SROW, DSUM,
    TMP, LP, SB, RSB, SR, RR,
    in_s, w_s, w_r, wy_s, wy_r, pd_s, pd_r, ga_s, ga_r, rs_s, rs_r,
    gy_s, gy_r, gg_s, gg_r, gpd_s, gpd_r, sm_s, sm_r, dm_s, dm_r,
):
    d = lax.axis_index("dp")
    c = lax.axis_index("ctx")
    k = c // 2
    j = c % 2
    z = k // 2
    r = z + (k % 2) * (7 - 2 * z)
    head = 8 * j + k

    def ctx_of(pos, core):
        p = (pos + 16) % 8
        return 2 * (2 * p + (p // 4) * (15 - 4 * p)) + core

    right = (d, ctx_of(r + 1, j))
    left = (d, ctx_of(r - 1, j))
    sibling = (d, 2 * k + (1 - j))
    partner = (1 - d, c)

    def rcopy(src, dst, ss, rs, dev):
        return pltpu.make_async_remote_copy(
            src_ref=src, dst_ref=dst, send_sem=ss, recv_sem=rs,
            device_id=dev, device_id_type=MESH,
        )

    barrier = pltpu.get_barrier_semaphore()

    def hello(o, _):
        lin = (d * NC + c + o) % 32
        pl.semaphore_signal(barrier, inc=1, device_id=(lin // NC, lin % NC), device_id_type=MESH)
        return 0

    lax.fori_loop(1, 32, hello, 0)

    def own_rows(s):
        return pl.ds(pl.multiple_of(s * SL + 64 * c, 64), 64)

    vecs = (V0, V1, V2, V3, V4, V5, V6, V7)
    fetch = [pltpu.make_async_copy(qw_ref, QW, in_s.at[0]), pltpu.make_async_copy(uw_ref, UW, in_s.at[1])]
    for i, ref in enumerate((ag_ref, as_ref, mg_ref, ms_ref, pb_ref, db_ref)):
        fetch.append(pltpu.make_async_copy(ref, vecs[i], in_s.at[2 + i]))
    fetch.append(pltpu.make_async_copy(qb_ref, vecs[6], in_s.at[8]))
    fetch.append(pltpu.make_async_copy(ub_ref, vecs[7], in_s.at[9]))
    fetch_x = [pltpu.make_async_copy(x_ref.at[s], X.at[own_rows(s)], in_s.at[10 + s]) for s in range(2)]
    fetch_y = [pltpu.make_async_copy(dy_ref.at[s], Y.at[own_rows(s)], in_s.at[12 + s]) for s in range(2)]
    for cp in fetch + fetch_x + fetch_y:
        cp.start()
    pl.semaphore_wait(barrier, 31)

    class Gather:
        def __init__(self, buf, own, s, i):
            self.buf, self.own, self.s, self.i = buf, own, s, i

        def at(self, delta, core):
            row = self.s * SL + 64 * ctx_of(r + delta, core)
            return self.buf.at[pl.ds(pl.multiple_of(row, 64), 64)]

        def ring(self, t, way, back=0):
            region = self.at((t + back) * (2 * way - 1), j)
            slot = 4 * way + t
            return rcopy(region, region, ga_s.at[self.i, slot], ga_r.at[self.i, slot],
                         left if way else right)

        def steps(self, way):
            return 4 if way == self.s else 3

        def sib(self, slot, core):
            delta = (0, -1, -2, -3, 1, 2, 3, 4)[slot]
            region = self.at(delta, core)
            return rcopy(region, region, ga_s.at[self.i, 8 + slot], ga_r.at[self.i, 8 + slot], sibling)

        def start(self):
            self.own[self.s].wait()
            self.ring(0, 0).start()
            self.ring(0, 1).start()
            self.sib(0, j).start()

        def pump(self, t):
            for way in (0, 1):
                if t <= self.steps(way):
                    self.ring(t - 1, way, 1).wait_recv()
                    if t < self.steps(way):
                        self.ring(t, way).start()
                    self.sib(7 if t == 4 else t + 3 * way, j).start()

        def ready(self, t):
            for slot in ((0,) if t == 0 else (t, 3 + t) if t < 4 else (7,)):
                self.sib(slot, 1 - j).wait_recv()

        def drain(self):
            for way in (0, 1):
                for t in range(self.steps(way)):
                    self.ring(t, way).wait_send()
            for slot in range(8):
                self.sib(slot, j).wait_send()

    gx = [Gather(X, fetch_x, s, s) for s in range(2)]
    gd = [Gather(Y, fetch_y, s, 2 + s) for s in range(2)]
    gx[0].start()
    for cp in fetch:
        cp.wait()

    def lane(shape):
        return lax.broadcasted_iota(jnp.int32, shape, len(shape) - 1)

    TMP[:, 0:128] = jnp.zeros((128, 128), f32)
    for i in range(6):
        TMP[64 + i:65 + i, 0:32] = vecs[i][...].astype(f32)
    TMP[0:1, 0:96] = V6[...].astype(f32)
    vq, vu = TMP[0:1, 0:128], V7[...].astype(f32)
    for i in range(3):
        TMP[70 + i:71 + i, 0:128] = pltpu.roll(vq, (128 - 32 * i) % 128, 1)
    for i in range(4):
        TMP[73 + i:74 + i, 0:128] = pltpu.roll(vu, (128 - 32 * i) % 128, 1)
    vcols = TMP[:, 0:128].T[0:32, :]
    low32 = lane((32, 128)) < 64
    for hp in range(H // 2):
        q2 = QW[:, 128 * hp:128 * hp + 128].astype(f32)
        k2 = QW[:, D + 128 * hp:D + 128 * hp + 128].astype(f32)
        v2 = QW[:, 2 * D + 128 * hp:2 * D + 128 * hp + 128].astype(f32)
        WS[2 * hp, :, 0:128] = jnp.where(low32, q2, pltpu.roll(k2, 64, 1)).astype(bf16)
        WS[2 * hp + 1, :, 0:128] = jnp.where(low32, pltpu.roll(q2, 64, 1), k2).astype(bf16)
        WS[2 * hp, :, 128:256] = jnp.where(low32, v2, vcols).astype(bf16)
        WS[2 * hp + 1, :, 128:256] = jnp.where(low32, pltpu.roll(v2, 64, 1), vcols).astype(bf16)
    for h in range(H):
        WS[h, :, 256:512] = UW[:, 256 * h:256 * h + 256]

    def w_copy(o, dst_c, row):
        return rcopy(
            WS.at[8 * (dst_c % 2) + dst_c // 2],
            WC.at[pl.ds(pl.multiple_of(row, 32), 32)],
            w_s.at[o], w_r.at[o], (d, dst_c),
        )

    own_row = 32 * (NC * d + c)

    def w_send(o, _):
        w_copy(o, (c + o) % NC, own_row).start()
        return 0

    lax.fori_loop(1, NC, w_send, 0)
    WC[pl.ds(pl.multiple_of(own_row, 32), 32), :] = WS[head]

    def wy_copy(o, plane):
        row = 32 * (NC * plane + (c - o + NC) % NC)
        region = WC.at[pl.ds(pl.multiple_of(row, 32), 32)]
        return rcopy(region, region, wy_s.at[o], wy_r.at[o], partner)

    wy_copy(0, d).start()
    gx[1].start()

    def pd_copies(jj, dst_dp):
        dev = (dst_dp, 2 * k + d)
        return (
            rcopy(pw_ref, WPD.at[pl.ds(256 + 32 * jj, 32)], pd_s.at[dst_dp, 0], pd_r.at[jj, 0], dev),
            rcopy(dw_ref, WPD.at[pl.ds(128 * jj, 128)], pd_s.at[dst_dp, 1], pd_r.at[jj, 1], dev),
        )

    here = d == j

    def pd_start():
        for e in range(2):
            @pl.when(jnp.logical_not(here & (d == e)))
            def _():
                for cp in pd_copies(j, e):
                    cp.start()

    local_pd = (
        pltpu.make_async_copy(pw_ref, WPD.at[pl.ds(256 + 32 * j, 32)], in_s.at[14]),
        pltpu.make_async_copy(dw_ref, WPD.at[pl.ds(128 * j, 128)], in_s.at[15]),
    )

    @pl.when(here)
    def _():
        for cp in local_pd:
            cp.start()
    WPD[320:384, :] = jnp.zeros((64, D), bf16)

    rows_i = lax.broadcasted_iota(jnp.int32, (SL, 128), 0)
    place = jnp.zeros((SL, 128), jnp.int32)
    cols_i = lane((8, SL))
    place_row = jnp.zeros((8, SL), jnp.int32)
    for b in range(NC):
        gob = go_ref[b]
        place = jnp.where((rows_i >> 6) == b, gob, place)
        place_row = jnp.where((cols_i >> 6) == b, gob, place_row)
    place = place * 64 + (rows_i & 63)
    place_row = place_row * 64 + (cols_i & 63)
    PK[...] = place
    for s in range(2):
        lim = place_row
        for p in range(PICS):
            st = ps_ref[s, p]
            lim = jnp.where((place_row >= st) & (place_row < st + PIC), st + (PIC - 1), lim)
        LIM[s] = lim

    def make_table(i, _):
        rows = pl.ds(pl.multiple_of(i * 128, 128), 128)
        ln = lane((128, 128))
        l64 = ln & 63
        freq = jnp.zeros((128, 128), f32)
        for q in range(ROT // 2):
            freq = jnp.where((l64 & 7) == q, float(rotary_base ** (-2.0 * q / ROT)), freq)
        ang = PK[rows, :].astype(f32) * freq
        CT[rows, :] = jnp.where(l64 < ROT, jnp.cos(ang), 1.0)
        sn = jnp.sin(ang)
        ST[rows, :] = jnp.where(l64 < ROT // 2, -sn, jnp.where(l64 < ROT, sn, 0.0))
        return 0

    lax.fori_loop(0, SL // 128, make_table, 0)

    half = pl.ds(pl.multiple_of(512 * d, 512), 512)
    other = pl.ds(pl.multiple_of(512 * (1 - d), 512), 512)

    def w_wait(o, _):
        src_c = (c - o + NC) % NC
        w_copy(o, (c + o) % NC, 32 * (NC * d + src_c)).wait_recv()
        wy_copy(o, d).start()
        return 0

    lax.fori_loop(1, 6, w_wait, 0)
    gx[0].pump(1)
    lax.fori_loop(6, 11, w_wait, 0)
    gx[1].pump(1)
    lax.fori_loop(11, NC, w_wait, 0)
    pd_start()

    def wy_wait(o, _):
        wy_copy(o, 1 - d).wait_recv()
        return 0

    lax.fori_loop(0, NC, wy_wait, 0)

    SM[...] = WC[:, 128:256].astype(f32).T[64:80, :]
    en = lane((16, 256))
    vrow = lax.broadcasted_iota(jnp.int32, (16, 256), 0)
    feat = lax.broadcasted_iota(jnp.int32, (D, 256), 0)
    jl = lane((D, 256))
    smb = SM[...].astype(bf16)

    def pick(e_big, e_small, div, first):
        onehot = jnp.where(feat == div(e_big)[0], 1.0, 0.0).astype(bf16)
        got = dot(smb, onehot)
        return jnp.sum(jnp.where(vrow == first + div(e_small)[1], got, 0.0), axis=0, keepdims=True)

    def place_qkv(e):
        owner = ((e >> 5) * 171) >> 9
        return 32 * owner + (e & 31), (e >> 5) - 3 * owner

    def place_up(e):
        return 32 * (e >> 7) + (e & 31), (e >> 5) & 3

    def e_qkv(ln):
        return SL * (ln >> 6) + HD * head + (ln & 63)

    bq = pick(e_qkv(jl), e_qkv(en), place_qkv, 6)
    bq = jnp.where(lane((1, 256)) < 192, bq, 0.0)
    bu = pick(256 * head + jl, 256 * head + en, place_up, 9)
    BV[0] = jnp.broadcast_to(bq, (8, 256))
    BV[1] = jnp.broadcast_to(bu, (8, 256))

    def turn(v, cs, sn, sign):
        l64 = lane(v.shape) & 63
        mate = jnp.where(l64 < ROT // 2, pltpu.roll(v, 120, 1), pltpu.roll(v, 8, 1))
        return v * cs + sign * (mate * sn)

    def normed_of(rows_value):
        x = rows_value.astype(f32)
        cen = x - jnp.mean(x, axis=1, keepdims=True)
        inv = lax.rsqrt(jnp.mean(cen * cen, axis=1, keepdims=True) + norm_eps)
        return cen * inv, inv

    def chip_rows(s, deltas):
        return [pl.ds(pl.multiple_of(s * SL + 64 * ctx_of(r + e, 0), 128), 128) for e in deltas]

    def load(ref, rows, lo=0, hi=None):
        parts = [ref[x, lo:hi] for x in rows]
        return parts[0] if len(parts) == 1 else jnp.concatenate(parts, axis=0)

    def store(ref, rows, value, lo=0, hi=None):
        for i, x in enumerate(rows):
            ref[x, lo:hi] = value[128 * i:128 * i + 128]

    def n_stage(s, deltas):
        rows, trow = chip_rows(s, deltas), chip_rows(0, deltas)
        low = lane((128 * len(rows), 128)) < 64
        nrm, _ = normed_of(load(X, rows))
        na = (nrm * SM[0:1, :] + SM[1:2, :]).astype(bf16)
        nm = (nrm * SM[2:3, :] + SM[3:4, :]).astype(bf16)
        store(NA, rows, na)
        store(NM, rows, nm)
        qkv = dot(na, WC[:, 0:256]) + BV[0, 0:1, :]
        up = dot(nm, WC[:, 256:512]) + BV[1, 0:1, :]
        rot = turn(qkv[:, 0:128], load(CT, trow), load(ST, trow), 1.0)
        store(Q, rows, jnp.where(low, rot * 0.125, 0.0).astype(bf16))
        store(K, rows, jnp.where(low, pltpu.roll(rot, 64, 1), 0.0).astype(bf16))
        store(V, rows, jnp.where(low, qkv[:, 128:256], 0.0).astype(bf16))
        cdf = 0.5 * (1.0 + lax.erf(up * (2.0 ** -0.5)))
        store(AA, rows, (up * cdf).astype(bf16), 0, 256)
        store(GP, rows, cdf + up * (jnp.exp(-0.5 * up * up) * ((2.0 * math.pi) ** -0.5)))

    def n_blocks(s, t):
        gx[s].ready(t)
        n_stage(s, (t,) if t in (0, 4) else (t, -t))

    def dy_blocks(s, t):
        if t == 0:
            gd[s].ready(4)
        gd[s].ready(t)
        dy_stage(s, (0, 4) if t == 0 else (t, -t))

    def turn_kv(s):
        VT[s] = V[s * SL:s * SL + SL, :].astype(f32).T[0:64, :].astype(bf16)
        KT[s] = K[s * SL:s * SL + SL, :].astype(f32).T[0:64, :].astype(bf16)

    HM[...] = jnp.full((8, 256), masked_score, f32)

    def fwd(i, _):
        s = i // 4
        q0 = pl.multiple_of((i % 4) * 256, 256)
        rows = pl.ds(pl.multiple_of(i * 256, 256), 256)
        seq = pl.ds(pl.multiple_of(s * SL, SL), SL)
        st = dot_nt(K[seq, :], Q[rows, :])
        pk = PK[...]
        lim = LIM[s, 0:1, pl.ds(q0, 256)]
        masked = jnp.where(jnp.concatenate([pk, pk], axis=1) <= lim, st, masked_score)
        peak = jnp.max(masked, axis=0, keepdims=True)
        p = jnp.exp(masked - peak)
        tot = jnp.sum(p, axis=0, keepdims=True)
        pt = (p * (1.0 / tot)).astype(bf16)
        PT[i] = pt
        at = dot(VT[s], pt)
        ATT[i] = at
        AA[rows, 256:384] = jnp.concatenate([at, jnp.zeros((64, 256), f32)], axis=0).T.astype(bf16)
        HM[...] = jnp.maximum(HM[...], jnp.broadcast_to(peak, (8, 256)))
        return 0

    class Scatter:
        def __init__(self, i, s, group, partial):
            self.i, self.s, self.g, self.partial = i, s, group, partial

        def sib(self, slot):
            return rcopy(SB.at[self.g, slot], SR.at[self.i, slot],
                         rs_s.at[self.i, 8 + slot], rs_r.at[self.i, 8 + slot], sibling)

        def produce(self, p):
            value = self.partial(self.s, (4, 0) if p == 0 else (4 - p, p - 4))
            for i, slot in enumerate((0, 7) if p == 0 else (2 * p - 1, 2 * p)):
                TMP[...] = value[128 * i:128 * i + 128]
                LP[self.g, slot] = TMP[pl.ds(pl.multiple_of(64 * j, 64), 64), :]
                SB[self.g, slot] = TMP[pl.ds(pl.multiple_of(64 * (1 - j), 64), 64), :].astype(bf16)
                self.sib(slot).start()

        def lane_sum(self, slot):
            self.sib(slot).wait_recv()
            return LP[self.g, slot] + SR[self.i, slot].astype(f32)

        def ring(self, t, way):
            slot = 4 * way + t
            return rcopy(RSB.at[self.g, slot], RR.at[self.i, slot],
                         rs_s.at[self.i, slot], rs_r.at[self.i, slot], left if way else right)

        def pump(self, t):
            for way in (self.s,) if t == 0 else (0, 1):
                slot = 4 * way + t
                v = self.lane_sum(2 * t - 1 + way if t else 0)
                if t > 1 or (t == 1 and way == self.s):
                    self.ring(t - 1, way).wait_recv()
                    v = v + RR[self.i, slot - 1].astype(f32)
                RSB[self.g, slot] = v.astype(bf16)
                self.ring(t, way).start()

        def total(self):
            v = self.lane_sum(7)
            for way in (0, 1):
                self.ring(3, way).wait_recv()
                v = v + RR[self.i, 4 * way + 3].astype(f32)
            return v

        def drain(self):
            for slot in range(8):
                self.sib(slot).wait_send()
            for way in (0, 1):
                for t in range(0 if way == self.s else 1, 4):
                    self.ring(t, way).wait_send()

    def out_partial(s, deltas):
        return dot(load(AA, chip_rows(s, deltas)), WPD[...])

    out = [Scatter(s, s, s, out_partial) for s in range(2)]
    DSUM[d] = jnp.zeros((8, D), f32)

    def dy_stage(s, deltas):
        rows = chip_rows(s, deltas)
        dyb = load(Y, rows)
        back = dot_nt(dyb, WPD[...])
        store(GG, rows, (back[:, 0:256] * load(GP, rows)).astype(bf16), 256, 512)
        store(DA, rows, back[:, 256:384].astype(bf16))
        DSUM[d] += jnp.broadcast_to(jnp.sum(dyb.astype(f32), axis=0, keepdims=True), (8, D))

    def bwd(i, _):
        s = i // 4
        rows = pl.ds(pl.multiple_of(i * 256, 256), 256)
        seq = pl.ds(pl.multiple_of(s * SL, SL), SL)
        q0 = pl.ds(pl.multiple_of((i % 4) * 256, 256), 256)
        da = DA[rows, :]
        rd = jnp.sum(da.astype(f32).T[0:64, :] * ATT[i], axis=0, keepdims=True)
        dpt = dot_nt(V[seq, :], da)
        pt = PT[i]
        ds = (pt.astype(f32) * (dpt - rd)).astype(bf16)
        DV[...] += dot(pt, da)
        DK[...] += dot(ds, Q[rows, :])
        DQ[q0, :] = jnp.concatenate([dot(KT[s], ds), jnp.zeros((64, 256), f32)], axis=0).T * 0.125
        return 0

    def qkv_back(i, s):
        trow = pl.ds(pl.multiple_of(i * 128, 128), 128)
        rows = pl.ds(pl.multiple_of(s * SL + i * 128, 128), 128)
        both = DQ[trow, :] + pltpu.roll(DK[trow, :], 64, 1)
        GG[rows, 0:128] = turn(both, CT[trow, :], ST[trow, :], -1.0).astype(bf16)
        GG[rows, 128:256] = DV[trow, :].astype(bf16)
        return s

    GN[...] = jnp.zeros((8, D), f32)

    def g_partial(s, deltas):
        rows = chip_rows(s, deltas)
        nrm, _ = normed_of(load(X, rows))
        gna = dot_nt(load(GG, rows, 0, 256), WC[:, 0:256])
        gnm = dot_nt(load(GG, rows, 256, 512), WC[:, 256:512])
        GN[0:1, :] += jnp.sum(gna * nrm, axis=0, keepdims=True)
        GN[1:2, :] += jnp.sum(gna, axis=0, keepdims=True)
        GN[2:3, :] += jnp.sum(gnm * nrm, axis=0, keepdims=True)
        GN[3:4, :] += jnp.sum(gnm, axis=0, keepdims=True)
        return gna * SM[0:1, :] + gnm * SM[2:3, :]

    grad = [Scatter(2 + s, s, s, g_partial) for s in range(2)]

    def out_done(s):
        tot = out[s].total()
        bo_ref[s * 64:s * 64 + 64, :] = (
            X[own_rows(s), :].astype(f32) + tot + SM[4:5, :] + SM[5:6, :]
        ).astype(bf16)
        out[s].drain()

    def bwd_start():
        DV[...] = jnp.zeros((SL, 128), f32)
        DK[...] = jnp.zeros((SL, 128), f32)

    def transpose_gg(lo):
        def one(i, _):
            rows = pl.ds(pl.multiple_of(i * 256, 256), 256)
            TT[0:256, rows] = GG[rows, lo:lo + 256].T
            return 0
        lax.fori_loop(0, 8, one, 0)

    def qkv_grad(i, _):
        cols = pl.ds(pl.multiple_of(i * 256, 256), 256)
        a = dot(TT[0:256, :], NA[:, cols])
        a = jnp.concatenate([a[0:192], GN[:, cols], a[200:256]], axis=0)
        GA[cols, :] = a.T.astype(bf16)
        return 0

    def up_grad(i, _):
        cols = pl.ds(pl.multiple_of(i * 256, 256), 256)
        GB[cols, :] = dot(TT[0:256, :], NM[:, cols]).T.astype(bf16)
        return 0

    gya = rcopy(GA.at[other], GYA, gy_s.at[0], gy_r.at[0], partner)
    gyb = rcopy(GB.at[other], GYB, gy_s.at[1], gy_r.at[1], partner)

    def up_weights():
        transpose_gg(256)
        lax.fori_loop(0, 4, up_grad, 0)
        gyb.start()

    def qkv_weights():
        transpose_gg(0)
        lax.fori_loop(0, 4, qkv_grad, 0)
        gya.start()

    def transpose_aa(i, _):
        rows = pl.ds(pl.multiple_of(i * 256, 256), 256)
        TT[:, rows] = AA[rows, :].T
        return 0

    def pd_grad(i, _):
        cols = pl.ds(pl.multiple_of(i * 256, 256), 256)
        PDS[:, cols] = dot(TT[...], Y[:, cols]).astype(bf16)
        return 0

    def gpd_copies(jj, slot_dp):
        dev = (j, 2 * k + jj)
        return (
            rcopy(PDS.at[pl.ds(256 + 32 * jj, 32)], gp_ref.at[slot_dp, pl.ds(0, 32)],
                  gpd_s.at[jj, 0], gpd_r.at[slot_dp, 0], dev),
            rcopy(PDS.at[pl.ds(128 * jj, 128)], gp_ref.at[slot_dp, pl.ds(32, 128)],
                  gpd_s.at[jj, 1], gpd_r.at[slot_dp, 1], dev),
        )

    def pd_weights():
        lax.fori_loop(0, 8, transpose_aa, 0)
        lax.fori_loop(0, 4, pd_grad, 0)
        for jj in range(2):
            @pl.when(jnp.logical_not(here & (j == jj)))
            def _():
                for cp in gpd_copies(jj, d):
                    cp.start()

        @pl.when(here)
        def _():
            gp_ref[d, 0:32, :] = PDS[pl.ds(256 + 32 * j, 32), :]
            gp_ref[d, 32:160, :] = PDS[pl.ds(128 * j, 128), :]

    def g_copy(half_i, o, dst_c, slot):
        src, dst = ((GA, gra_ref), (GB, grb_ref))[half_i]
        return rcopy(src.at[pl.ds(pl.multiple_of(512 * d + 32 * dst_c, 32), 32)], dst.at[slot],
                     gg_s.at[half_i, o], gg_r.at[half_i, o], (d, dst_c))

    def weights_out(half_i):
        gy, G, GY, gr_ref = ((gya, GA, GYA, gra_ref), (gyb, GB, GYB, grb_ref))[half_i]
        gy.wait_recv()
        G[half, :] = (G[half, :].astype(f32) + GY[...].astype(f32)).astype(bf16)

        def g_send(o, _):
            g_copy(half_i, o, (c + o) % NC, head).start()
            return 0

        lax.fori_loop(1, NC, g_send, 0)
        gr_ref[head] = G[pl.ds(pl.multiple_of(512 * d + 32 * c, 32), 32), :]

    def pd_ready():
        for jj in range(2):
            @pl.when(jnp.logical_not(here & (j == jj)))
            def _():
                for cp in pd_copies(jj, 0):
                    cp.wait_recv()

        @pl.when(here)
        def _():
            for cp in local_pd:
                cp.wait()

    def fwd_tiles(lo, hi):
        lax.fori_loop(lo, hi, fwd, 0)

    def bwd_tiles(lo, hi):
        lax.fori_loop(lo, hi, bwd, 0)

    dm = rcopy(DSUM.at[d], DSUM.at[d], dm_s, dm_r, partner)

    me = NC * d + c

    def s_copy(o, slot):
        lin = (me + o) % 32
        return rcopy(SROW, sr_ref.at[slot], sm_s.at[o], sm_r.at[o], (lin // NC, lin % NC))

    def token_sums():
        srow = jnp.zeros((1, 512), f32)
        for i in range(TOK // 256):
            srow = srow + jnp.sum(GG[i * 256:i * 256 + 256, :].astype(f32), axis=0, keepdims=True)
        hmax = jnp.max(HM[...], axis=1, keepdims=True)[0:1, :]
        SROW[...] = jnp.where(lane((1, 512)) == 192, hmax, srow)
        sr_ref[me] = SROW[...]

        def s_send(o, _):
            s_copy(o, me).start()
            return 0

        lax.fori_loop(1, 32, s_send, 0)

    def grad_done(s):
        tot = grad[s].total()
        own = slice(s * 64, s * 64 + 64)
        nrm, inv = normed_of(X[own_rows(s), :])
        gh_ref[own, :] = (
            Y[own_rows(s), :].astype(f32)
            + inv * (tot - jnp.mean(tot, axis=1, keepdims=True)
                     - nrm * jnp.mean(tot * nrm, axis=1, keepdims=True))
        ).astype(bf16)

    gx[0].pump(2)
    n_blocks(1, 0)
    n_blocks(0, 1)
    gx[1].pump(2)
    n_blocks(0, 2)
    n_blocks(1, 1)
    gx[0].pump(3)
    gd[0].start()
    n_blocks(0, 0)
    pd_ready()
    n_blocks(0, 3)
    gx[1].pump(3)
    n_blocks(1, 3)
    gx[0].pump(4)
    n_blocks(1, 2)
    gd[1].start()
    n_blocks(0, 4)
    turn_kv(0)
    fwd_tiles(0, 2)
    gd[0].pump(1)
    gx[1].pump(4)
    fwd_tiles(2, 4)
    gd[1].pump(1)
    n_blocks(1, 4)
    turn_kv(1)
    fwd_tiles(4, 6)
    gd[0].pump(2)
    fwd_tiles(6, 8)
    out[0].produce(0)
    out[0].produce(1)
    dy_blocks(1, 1)
    gd[1].pump(2)
    out[0].produce(2)
    out[0].produce(3)
    out[1].produce(0)
    out[0].pump(0)
    dy_blocks(0, 1)
    out[1].produce(1)
    out[1].pump(0)
    gd[0].pump(3)
    out[1].produce(2)
    out[1].produce(3)
    gd[1].pump(3)
    dy_blocks(0, 2)
    out[0].pump(1)
    out[1].pump(1)
    dy_blocks(1, 2)
    gd[1].pump(4)
    gd[0].pump(4)
    dy_blocks(1, 0)
    dy_blocks(0, 0)
    dy_blocks(1, 3)
    dy_blocks(0, 3)
    bwd_start()
    out[0].pump(2)
    up_weights()
    out[1].pump(2)
    bwd_tiles(0, 2)
    bwd_tiles(2, 4)
    out[0].pump(3)
    lax.fori_loop(0, 8, qkv_back, 0)
    out[1].pump(3)
    bwd_start()
    bwd_tiles(4, 6)
    bwd_tiles(6, 8)
    weights_out(1)
    out_done(0)
    grad[0].produce(0)
    grad[0].produce(1)
    out_done(1)
    grad[0].pump(0)
    lax.fori_loop(0, 8, qkv_back, 1)
    grad[1].produce(0)
    grad[1].produce(1)
    grad[1].pump(0)
    grad[0].produce(2)
    grad[0].pump(1)
    grad[1].produce(2)
    grad[1].pump(1)
    grad[1].produce(3)
    grad[0].produce(3)
    qkv_weights()
    grad[0].pump(2)
    grad[1].pump(2)
    pd_weights()
    dm.start()
    grad[0].pump(3)
    token_sums()
    grad[1].pump(3)
    weights_out(0)
    grad_done(1)
    grad_done(0)

    for e in range(2):
        @pl.when(jnp.logical_not(here & (d == e)))
        def _():
            for cp in gpd_copies(0, e):
                cp.wait_recv()

    rcopy(DSUM.at[1 - d], DSUM.at[1 - d], dm_s, dm_r, partner).wait_recv()
    ds_ref[...] = DSUM[0] + DSUM[1]

    def g_wait(o, _):
        src_c = (c - o + NC) % NC
        for half_i in range(2):
            g_copy(half_i, o, (c + o) % NC, 8 * (src_c % 2) + src_c // 2).wait_recv()
        return 0

    lax.fori_loop(1, NC, g_wait, 0)

    def s_wait(o, _):
        s_copy(o, (me - o + 32) % 32).wait_recv()
        return 0

    lax.fori_loop(1, 32, s_wait, 0)

    def w_done(o, _):
        w_copy(o, (c + o) % NC, own_row).wait_send()
        for half_i in range(2):
            g_copy(half_i, o, (c + o) % NC, head).wait_send()
        wy_copy(o, d).wait_send()
        return 0

    lax.fori_loop(1, NC, w_done, 0)

    def s_done(o, _):
        s_copy(o, me).wait_send()
        return 0

    lax.fori_loop(1, 32, s_done, 0)
    wy_copy(0, d).wait_send()
    gya.wait_send()
    gyb.wait_send()
    dm.wait_send()
    for e in range(2):
        @pl.when(jnp.logical_not(here & (d == e)))
        def _():
            for cp in pd_copies(j, e):
                cp.wait_send()

        @pl.when(jnp.logical_not(here & (j == e)))
        def _():
            for cp in gpd_copies(e, d):
                cp.wait_send()
    for item in gx + gd + grad:
        item.drain()


def finish_kernel(
    bo, gh, gra, grb, gp, sr, ds, qw,
    o_bo, o_gh, o_ag, o_as, o_qw, o_qb, o_pw, o_pb, o_mg, o_ms, o_uw, o_ub, o_dw, o_db, o_cq,
    B, F,
):
    me = NC * lax.axis_index("dp") + lax.axis_index("ctx")
    for s in range(2):
        o_bo[s] = bo[64 * s:64 * s + 64, :]
        o_gh[s] = gh[64 * s:64 * s + 64, :]
    o_pw[...] = gp[0, 0:32, :].astype(f32) + gp[1, 0:32, :].astype(f32)
    o_dw[...] = gp[0, 32:160, :].astype(f32) + gp[1, 32:160, :].astype(f32)
    low = lax.broadcasted_iota(jnp.int32, (32, 128), 1) < 64
    low1 = low[0:1]
    gains = jnp.zeros((32, 128), f32)
    for h in range(H):
        at = 2 * (h % 8) + h // 8
        one, two = sr[at], sr[NC + at]
        both = one + two
        peak = jnp.maximum(one, two)
        col = lax.broadcasted_iota(jnp.int32, (1, 512), 1)
        B[h:h + 1, :] = jnp.where(col == 192, peak, both)
        F[32 + 2 * h:33 + 2 * h, :] = both[:, 256:384]
        F[33 + 2 * h:34 + 2 * h, :] = both[:, 384:512]
        gains = gains + gra[h, :, 128:256].astype(f32)
        o_uw[:, 256 * h:256 * h + 256] = grb[h].astype(f32)
    top = B[:, 128:256]
    top = jnp.max(jnp.where(lax.broadcasted_iota(jnp.int32, (H, 128), 1) == 64, top, masked_score), axis=1, keepdims=True)
    ratio = jnp.broadcast_to(jnp.sqrt(clip_bound / jnp.maximum(top, clip_bound)), (H, 128))
    F[24:32, :] = jnp.zeros((8, 128), f32)
    for hp in range(H // 2):
        a, b = gra[2 * hp, :, 0:128].astype(f32), gra[2 * hp + 1, :, 0:128].astype(f32)
        va, vb = gra[2 * hp, :, 128:256].astype(f32), gra[2 * hp + 1, :, 128:256].astype(f32)
        o_qw[:, 128 * hp:128 * hp + 128] = jnp.where(low, a, pltpu.roll(b, 64, 1))
        o_qw[:, D + 128 * hp:D + 128 * hp + 128] = jnp.where(low, pltpu.roll(a, 64, 1), b)
        o_qw[:, 2 * D + 128 * hp:2 * D + 128 * hp + 128] = jnp.where(low, va, pltpu.roll(vb, 64, 1))
        ra, rb = B[2 * hp:2 * hp + 1, 0:128], B[2 * hp + 1:2 * hp + 2, 0:128]
        sa, sb = B[2 * hp:2 * hp + 1, 128:256], B[2 * hp + 1:2 * hp + 2, 128:256]
        F[hp:hp + 1, :] = jnp.where(low1, ra, pltpu.roll(rb, 64, 1))
        F[8 + hp:9 + hp, :] = jnp.where(low1, pltpu.roll(ra, 64, 1), rb)
        F[16 + hp:17 + hp, :] = jnp.where(low1, sa, pltpu.roll(sb, 64, 1))
        fac = jnp.where(low1, ratio[2 * hp:2 * hp + 1], ratio[2 * hp + 1:2 * hp + 2])
        for part in range(3):
            cols = slice(part * D + 128 * hp, part * D + 128 * hp + 128)
            w = qw[:, cols].astype(f32)
            o_cq[:, cols] = w * fac if part < 2 else w
    grows = jnp.concatenate([gains, jnp.zeros((96, 128), f32)], axis=0).T
    for i, o in enumerate((o_ag, o_as, o_mg, o_ms)):
        o[...] = grows[64 + i:65 + i, 0:32]
    row, shift = (96 * me) // 128, (96 * me) % 128
    turned = pltpu.roll(F[pl.ds(row, 1), :], (128 - shift) % 128, 1)
    after = pltpu.roll(F[pl.ds(row + 1, 1), :], (128 - shift) % 128, 1)
    col = lax.broadcasted_iota(jnp.int32, (1, 128), 1)
    o_qb[...] = jnp.where(col < 128 - shift, turned, after)[:, 0:96]
    o_ub[...] = F[pl.ds(32 + me, 1), :]
    dsum = ds[0:1, pl.ds(pl.multiple_of(128 * (me // 4), 128), 128)]
    dsum = pltpu.roll(dsum, (128 - 32 * (me % 4)) % 128, 1)[:, 0:32]
    o_pb[...] = dsum
    o_db[...] = dsum


def fast_shards(
    hidden_in, out_cotangent, attn_gain, attn_shift, qkv_weight, qkv_bias, proj_weight, proj_bias,
    mlp_gain, mlp_shift, up_weight, up_bias, down_weight, down_bias, picture_starts, group_order,
):
    vm = pl.BlockSpec(memory_space=pltpu.VMEM)
    sm = pl.BlockSpec(memory_space=pltpu.SMEM)
    hbm = pl.BlockSpec(memory_space=pl.ANY)
    V_ = pltpu.VMEM
    dma = pltpu.SemaphoreType.DMA

    def sds(shape, dtype=f32):
        return jax.ShapeDtypeStruct(shape, dtype)

    got = pl.pallas_call(
        block_kernel,
        out_shape=(
            sds((128, D), bf16), sds((128, D), bf16), sds((NC, 32, 256), bf16), sds((NC, 32, 256), bf16),
            sds((2, 160, D), bf16), sds((32, 1, 512)), sds((8, D)),
        ),
        in_specs=[sm, sm] + [hbm] * 14,
        out_specs=(vm,) * 7,
        scratch_shapes=[
            V_((32, 3 * D), bf16), V_((32, 4 * D), bf16), *(V_((1, n), bf16) for n in (32,) * 6 + (96, 128)), V_((NC, 32, 512), bf16),
            V_((TOK, D), bf16), V_((TOK, D), bf16), V_((TOK, D), bf16), V_((TOK, D), bf16),
            V_((D, 512), bf16), V_((384, D), bf16),
            V_((SL, 128), f32), V_((SL, 128), f32), V_((SL, 128), jnp.int32),
            V_((2, 8, SL), jnp.int32), V_((16, D), f32), V_((2, 8, 256), f32),
            V_((TOK, 128), bf16), V_((TOK, 128), bf16), V_((TOK, 128), bf16),
            V_((2, 64, SL), bf16), V_((2, 64, SL), bf16),
            V_((8, SL, 256), bf16), V_((8, 64, 256), f32),
            V_((TOK, 384), bf16), V_((TOK, 256), f32), V_((TOK, 128), bf16), V_((TOK, 512), bf16),
            V_((SL, 128), f32), V_((SL, 128), f32), V_((SL, 128), f32),
            V_((8, 256), f32), V_((8, D), f32),
            V_((384, TOK), bf16), V_((D, 256), bf16), V_((D, 256), bf16),
            V_((512, 256), bf16), V_((512, 256), bf16),
            V_((384, D), bf16), V_((1, 512), f32), V_((2, 8, D), f32),
            V_((128, D), f32), V_((2, 8, 64, D), f32), V_((2, 8, 64, D), bf16),
            V_((2, 8, 64, D), bf16), V_((4, 8, 64, D), bf16), V_((4, 8, 64, D), bf16),
            dma((16,)), dma((NC,)), dma((NC,)), dma((NC,)), dma((NC,)), dma((2, 2)), dma((2, 2)),
            dma((4, 16)), dma((4, 16)), dma((4, 16)), dma((4, 16)),
            dma((2,)), dma((2,)), dma((2, NC)), dma((2, NC)), dma((2, 2)), dma((2, 2)), dma((32,)), dma((32,)), dma, dma,
        ],
        compiler_params=pltpu.CompilerParams(
            collective_id=0, has_side_effects=True, vmem_limit_bytes=63 * 1024 * 1024
        ),
    )(
        group_order, picture_starts, hidden_in, out_cotangent, qkv_weight, up_weight, proj_weight, down_weight,
        *(v.reshape(1, -1) for v in (
            attn_gain, attn_shift, mlp_gain, mlp_shift, proj_bias, down_bias, qkv_bias, up_bias)),
    )
    r32 = sds((1, 32))
    outs = pl.pallas_call(
        finish_kernel,
        out_shape=(
            sds((2, 64, D), bf16), sds((2, 64, D), bf16), r32, r32, sds((32, 3 * D)), sds((1, 96)),
            sds((32, D)), r32, r32, r32, sds((32, 4 * D)), sds((1, 128)), sds((128, D)), r32, sds((32, 3 * D)),
        ),
        in_specs=[vm] * 8,
        out_specs=(vm,) * 15,
        scratch_shapes=[V_((H, 512), f32), V_((64, 128), f32)],
    )(*got, qkv_weight)
    return tuple(o.reshape(-1) if o.shape[0] == 1 else o for o in outs)


def solution(mesh):
    in_specs = (
        P("dp", "ctx", None),
        P("dp", "ctx", None),
        P(("dp", "ctx")),
        P(("dp", "ctx")),
        P(("dp", "ctx"), None),
        P(("dp", "ctx")),
        P(("dp", "ctx"), None),
        P(("dp", "ctx")),
        P(("dp", "ctx")),
        P(("dp", "ctx")),
        P(("dp", "ctx"), None),
        P(("dp", "ctx")),
        P(("dp", "ctx"), None),
        P(("dp", "ctx")),
        P("dp", None),
        P(),
    )
    out_specs = (
        P("dp", "ctx", None),
        P("dp", "ctx", None),
        P(("dp", "ctx")),
        P(("dp", "ctx")),
        P(("dp", "ctx"), None),
        P(("dp", "ctx")),
        P(("dp", "ctx"), None),
        P(("dp", "ctx")),
        P(("dp", "ctx")),
        P(("dp", "ctx")),
        P(("dp", "ctx"), None),
        P(("dp", "ctx")),
        P(("dp", "ctx"), None),
        P(("dp", "ctx")),
        P(("dp", "ctx"), None),
    )
    body = fast_shards if (mesh.shape["dp"], mesh.shape["ctx"]) == (2, H) else shards
    return jax.shard_map(body, mesh=mesh, in_specs=in_specs, out_specs=out_specs, check_vma=False)
```
